32 devices in a mesh: dp: 4 (over z), fsdp: 8 (over y, x, core).
Axes of the slice: x: 2, y: 2, z: 4, core: 2. Of those that a mesh axis runs over, the one named last changes fastest.
Arguments:
- text_rows: bfloat16 [16384, 768], P(('dp', 'fsdp'))
- patches: bfloat16 [64, 32, 1024], P(('dp', 'fsdp')), may hold values from -6 to 6
- row_pair: int32 [16384], P(('dp', 'fsdp')), may hold values from -1 to 511, as said below
- row_region: int32 [16384], P(('dp', 'fsdp')), may hold values from 0 to 1, as said below
- self_qkv: bfloat16 [768, 2304], P(('dp', 'fsdp')), may hold values from -0.21875 to 0.21875
- self_out: bfloat16 [768, 768], P(('dp', 'fsdp')), may hold values from -0.4375 to 0.4375
- cross_query: bfloat16 [768, 768], P(('dp', 'fsdp')), may hold values from -0.21875 to 0.21875
- cross_key_value: bfloat16 [1024, 1536], P(('dp', 'fsdp')), may hold values from -0.1875 to 0.1875
- cross_out: bfloat16 [768, 768], P(('dp', 'fsdp')), may hold values from -0.625 to 0.625
- ffn_up: bfloat16 [768, 3072], P(('dp', 'fsdp')), may hold values from -0.21875 to 0.21875
- ffn_down: bfloat16 [3072, 768], P(('dp', 'fsdp')), may hold values from -0.109375 to 0.109375
- norm_gains: bfloat16 [3, 768], P(None, ('dp', 'fsdp')), may hold values from 0.5 to 1.5
- biases: bfloat16 [10, 768], P(None, ('dp', 'fsdp')), may hold values from -3 to 3
- ffn_bias: bfloat16 [3072], P(('dp', 'fsdp')), may hold values from -3 to 3
- cotangent: bfloat16 [16384, 768], P(('dp', 'fsdp')), may hold values from -6 to 6
Outputs:
- joined_text: bfloat16 [16384, 768], P(('dp', 'fsdp'))
- text_grad: float32 [16384, 768], P(('dp', 'fsdp'))
- patch_grad: float32 [64, 32, 1024], P(('dp', 'fsdp'))
- grad_self_qkv: float32 [768, 2304], P(('dp', 'fsdp'))
- grad_self_out: float32 [768, 768], P(('dp', 'fsdp'))
- grad_cross_query: float32 [768, 768], P(('dp', 'fsdp'))
- grad_cross_key_value: float32 [1024, 1536], P(('dp', 'fsdp'))
- grad_cross_out: float32 [768, 768], P(('dp', 'fsdp'))
- grad_ffn_up: float32 [768, 3072], P(('dp', 'fsdp'))
- grad_ffn_down: float32 [3072, 768], P(('dp', 'fsdp'))
- grad_norm_gains: float32 [3, 768], P(None, ('dp', 'fsdp'))
- grad_biases: float32 [10, 768], P(None, ('dp', 'fsdp'))
- grad_ffn_bias: float32 [3072], P(('dp', 'fsdp'))
The draws below stay inside these ranges and needn't reach their ends.
Inputs may be any that keep to these rules, and one draw needn't show every extreme that they name: `row_pair`: each aligned block of 128 rows holds whole pairs, each a run of consecutive rows with one value that no other pair among the same 512 rows has, followed by padding rows marked -1; a pair has max(2, 8) to 40 rows. `row_region`: all rows of one pair carry the same value.
All inputs are finite; a program needn't handle non-finite values.
Results may differ from the reference program's by a relative error of at most 0.018.
Values may be sent and summed in bfloat16 or wider, within the bound.
A program may use at most 256 MiB of HBM per device.

```python
import math
import jax
import jax.numpy as jnp
from jax import lax

D = 768
H = 12
HD = 64
FF = 3072
DV = 1024
CAP = 128
REG_DEV = 2
PR = 32
MAXLEN = 40
BLK = 512
TOK_DEV = 512
TOKENS = 16384
KEYS_DEV = 64
REGIONS = 64
N_DP = 4
N_FSDP = 8
DEVICES = 32


def pair_layout(key):
    key = jax.random.fold_in(key, 101)
    key_lengths, key_owner, key_jitter, key_region = jax.random.split(key, 4)
    blocks = TOKENS // CAP
    shortest = max(2, MAXLEN // 5)
    slot_count = CAP // shortest + 1
    lengths = jax.random.randint(key_lengths, (blocks, slot_count), shortest, MAXLEN + 1)
    pair_ends = jnp.cumsum(lengths, axis=1)
    lowest_base = max(CAP // 4, MAXLEN)
    owner_base = jax.random.randint(key_owner, (DEVICES,), lowest_base, CAP + 1)
    owner_base = owner_base.at[0].set(lowest_base)
    block_number = jnp.arange(blocks, dtype=jnp.int32)
    source_rank = block_number // N_DP
    target_rank = block_number % N_DP
    owner_rank = target_rank * N_FSDP + source_rank % N_FSDP
    jitter = jax.random.randint(key_jitter, (blocks,), 0, CAP // 4 + 1)
    row_limit = jnp.minimum(owner_base[owner_rank] + jitter, CAP)
    filled = jnp.max(jnp.where(pair_ends <= row_limit[:, None], pair_ends, 0), axis=1)
    position = jnp.arange(CAP, dtype=jnp.int32)
    pair_index = jnp.sum((pair_ends[:, None, :] <= position[None, :, None]).astype(jnp.int32), axis=2)
    live_rows = position[None, :] < filled[:, None]
    pair_ids = jnp.where(live_rows, target_rank[:, None] * CAP + CAP - 1 - pair_index, -1)
    regions = jax.random.randint(key_region, (blocks, slot_count), 0, REG_DEV)
    row_regions = jnp.take_along_axis(regions, jnp.minimum(pair_index, slot_count - 1), axis=1)
    return (pair_ids.reshape(TOKENS).astype(jnp.int32), row_regions.reshape(TOKENS).astype(jnp.int32))


def draw_row_pair(key, part):
    return pair_layout(key)[0]


def draw_row_region(key, part):
    return pair_layout(key)[1]


def draw_text_rows(key, part):
    key = jax.random.fold_in(key, 7)
    key_scale, key_entry = jax.random.split(key)
    column_scale = jnp.exp(jax.random.uniform(key_scale, (D,), jnp.float32, math.log(0.3), math.log(3.0)))
    entries = jnp.clip(jax.random.normal(key_entry, (TOKENS, D), jnp.float32), -6.0, 6.0)
    return (entries * column_scale[None, :]).astype(jnp.bfloat16)


def block_levels(own_key, shape, shards, low, largest):
    def one(axis_at, shards_of):
        steps = jax.random.uniform(jax.random.fold_in(jax.random.fold_in(own_key, 6), axis_at), (shards_of,), jnp.float32, low / len(shards), largest / len(shards))
        return jnp.repeat(jnp.exp(steps), shape[axis_at] // shards_of).reshape((-1,) + (1,) * (len(shape) - axis_at - 1))

    loudness = one(*shards[0])
    for cut in shards[1:]:
        loudness = loudness * one(*cut)
    return loudness


def gaussian(own_key, shape, spread, limit, shards=(), kind=jnp.bfloat16):
    values = spread * jax.random.normal(own_key, shape, jnp.float32)
    if shards:
        values = values * block_levels(own_key, shape, shards, -0.22, 0.18)
    return jnp.clip(values, -limit, limit).astype(kind)


def setup_inputs(seed: int = 0) -> dict:
    arg_keys = jax.random.split(jax.random.key(seed), 16)
    return {
        "text_rows": draw_text_rows(jax.random.fold_in(arg_keys[15], 71), 0),
        "patches": gaussian(arg_keys[1], (REGIONS, PR, DV), 1.0, 6.0, ((0, 32),)),
        "row_pair": draw_row_pair(jax.random.fold_in(arg_keys[15], 71), 0),
        "row_region": draw_row_region(jax.random.fold_in(arg_keys[15], 71), 0),
        "self_qkv": gaussian(arg_keys[4], (D, 3 * D), D ** -0.5, 0.21875, ((0, 32),)),
        "self_out": gaussian(arg_keys[5], (D, D), (D // 4) ** -0.5, 0.4375, ((0, 32),)),
        "cross_query": gaussian(arg_keys[6], (D, D), D ** -0.5, 0.21875, ((0, 32),)),
        "cross_key_value": gaussian(arg_keys[7], (DV, 2 * D), DV ** -0.5, 0.1875, ((0, 32),)),
        "cross_out": gaussian(arg_keys[8], (D, D), (D // 8) ** -0.5, 0.625, ((0, 32),)),
        "ffn_up": gaussian(arg_keys[9], (D, FF), D ** -0.5, 0.21875, ((0, 32),)),
        "ffn_down": gaussian(arg_keys[10], (FF, D), FF ** -0.5, 0.109375, ((0, 32),)),
        "norm_gains": jnp.clip(1.0 + 0.1 * jax.random.normal(arg_keys[11], (3, D), jnp.float32), 0.5, 1.5).astype(jnp.bfloat16),
        "biases": gaussian(arg_keys[12], (10, D), 0.5, 3.0, ((1, 32),)),
        "ffn_bias": gaussian(arg_keys[13], (FF,), 0.5, 3.0, ((0, 32),)),
        "cotangent": gaussian(arg_keys[14], (TOKENS, D), 1.0, 6.0, ((0, 32),)),
    }


EPSILON = 1e-06
NEGATIVE = -1e+30
PRECISE = lax.Precision.HIGHEST

@jax.custom_vjp
def low(v):
    return lax.optimization_barrier(v.astype(jnp.bfloat16)).astype(jnp.float32)

@jax.custom_vjp
def low_back(v):
    return v

def low_keep(v):
    return (low(v), None)

def low_pass(kept, grad):
    return (grad,)

def back_keep(v):
    return (v, None)

def back_low(kept, grad):
    return (low(grad),)
low.defvjp(low_keep, low_pass)
low_back.defvjp(back_keep, back_low)

def product(left, right):
    return jnp.dot(left, right, precision=PRECISE, preferred_element_type=jnp.float32)

def layer_norm(summed, gain_row, shift_row):
    center = summed - lax.optimization_barrier(jnp.mean(summed, axis=-1, keepdims=True))
    variance = lax.optimization_barrier(jnp.mean(center * center, axis=-1, keepdims=True))
    return center * lax.rsqrt(variance + EPSILON) * gain_row + shift_row

def attend_self(text_dev, pair_dev, weight_qkv, bias_query, bias_value):
    row_count = text_dev.shape[0]
    blocks = row_count // BLK
    projected = product(text_dev, weight_qkv)
    query_rows = low(low_back(projected[:, :D] + bias_query)).reshape(blocks, BLK, H, HD)
    key_rows = low(low_back(projected[:, D:2 * D])).reshape(blocks, BLK, H, HD)
    value_rows = low(low_back(projected[:, 2 * D:] + bias_value)).reshape(blocks, BLK, H, HD)
    scores = low_back(jnp.einsum('bqhd,bkhd->bhqk', query_rows, key_rows, precision=PRECISE) / math.sqrt(HD))
    segment = pair_dev.reshape(blocks, BLK)
    same_pair = (segment[:, :, None] == segment[:, None, :])[:, None]
    probability = jax.nn.softmax(jnp.where(same_pair, scores, NEGATIVE), axis=-1)
    context = jnp.einsum('bhqk,bkhd->bqhd', low(probability), value_rows, precision=PRECISE)
    return low(low_back(context.reshape(row_count, D)))

def attend_cross(queries, key_group, value_group, region_dev):
    owners = key_group.shape[0]
    query_rows = queries.reshape(owners, -1, H, HD)
    key_rows = key_group.reshape(owners, KEYS_DEV, H, HD)
    value_rows = value_group.reshape(owners, KEYS_DEV, H, HD)
    scores = low_back(jnp.einsum('bkhd,brhd->bhkr', key_rows, query_rows, precision=PRECISE) / math.sqrt(HD))
    key_region = jnp.arange(KEYS_DEV, dtype=jnp.int32) // PR
    same_region = (key_region[None, :, None] == region_dev.reshape(owners, 1, -1))[:, None]
    probability = jax.nn.softmax(jnp.where(same_region, scores, NEGATIVE), axis=2)
    context = jnp.einsum('bhkr,bkhd->brhd', low(probability), value_rows, precision=PRECISE)
    return low(low_back(context.reshape(-1, D)))

def device_layer(weights, key_all, value_all, text_dev, pair_dev, region_dev, device):
    weight_qkv, weight_sout, weight_cq, weight_cout, weight_up, weight_down, gains, bias_rows, bias_up = weights
    group_index = device % N_FSDP
    key_group = lax.dynamic_index_in_dim(key_all, group_index, axis=1, keepdims=False)
    value_group = lax.dynamic_index_in_dim(value_all, group_index, axis=1, keepdims=False)
    branch_self = low_back(product(attend_self(text_dev, pair_dev, weight_qkv, bias_rows[0], bias_rows[1]), weight_sout) + bias_rows[2])
    first = layer_norm(text_dev + branch_self, gains[0], bias_rows[7])
    queries = low(low_back(product(low(first), weight_cq) + bias_rows[3]))
    branch_cross = low_back(product(attend_cross(queries, key_group, value_group, region_dev), weight_cout) + bias_rows[5])
    second = layer_norm(first + branch_cross, gains[1], bias_rows[8])
    hidden_pre = low_back(product(low(second), weight_up) + bias_up)
    branch_ffn = low_back(product(low(jax.nn.gelu(hidden_pre, approximate=False)), weight_down) + bias_rows[6])
    result = layer_norm(second + branch_ffn, gains[2], bias_rows[9])
    return jnp.where((pair_dev >= 0)[:, None], result, 0.0)

def forward(text_rows, patches, self_qkv, self_out, cross_query, cross_key_value, cross_out, ffn_up, ffn_down, norm_gains, biases, ffn_bias, row_pair, row_region):
    patch_rows = patches.reshape(REGIONS * PR, DV)
    projected = product(patch_rows, cross_key_value)
    key_all = low(low_back(projected[:, :D])).reshape(N_DP, N_FSDP, KEYS_DEV, D)
    value_all = low(low_back(projected[:, D:] + biases[4])).reshape(N_DP, N_FSDP, KEYS_DEV, D)
    weights = (self_qkv, self_out, cross_query, cross_out, ffn_up, ffn_down, norm_gains, biases, ffn_bias)
    stepped = jax.checkpoint(device_layer)

    def one_device(device_item):
        return stepped(weights, key_all, value_all, device_item[0], device_item[1], device_item[2], device_item[3])
    result = lax.map(one_device, (text_rows.reshape(DEVICES, TOK_DEV, D), row_pair.reshape(DEVICES, TOK_DEV), row_region.reshape(DEVICES, TOK_DEV), jnp.arange(DEVICES, dtype=jnp.int32)))
    return result.reshape(TOKENS, D)

def reference(text_rows, patches, row_pair, row_region, self_qkv, self_out, cross_query, cross_key_value, cross_out, ffn_up, ffn_down, norm_gains, biases, ffn_bias, cotangent):
    floats = (text_rows.astype(jnp.float32), patches.astype(jnp.float32), self_qkv.astype(jnp.float32), self_out.astype(jnp.float32), cross_query.astype(jnp.float32), cross_key_value.astype(jnp.float32), cross_out.astype(jnp.float32), ffn_up.astype(jnp.float32), ffn_down.astype(jnp.float32), norm_gains.astype(jnp.float32), biases.astype(jnp.float32), ffn_bias.astype(jnp.float32))
    joined_rows, pullback = jax.vjp(lambda *values: forward(*values, row_pair, row_region), *floats)
    gradients = pullback(cotangent.astype(jnp.float32))
    return (joined_rows.astype(jnp.bfloat16), gradients[0], gradients[1], gradients[2], gradients[3], gradients[4], gradients[5], gradients[6], gradients[7], gradients[8], gradients[9], gradients[10], gradients[11])
```

```python
import functools
import math
import types

import jax
import jax.numpy as jnp
from jax import lax
from jax.experimental import pallas as pl
from jax.experimental.pallas import tpu as pltpu
from jax.sharding import PartitionSpec as P

H = 12
HD = 64
PR = 32
BLK = 512


EPSILON = 1e-06
NEGATIVE = -1e30


def times_transpose(left, right):
    return lax.dot_general(
        left, right, (((1,), (1,)), ((), ())), preferred_element_type=jnp.float32
    )


def transpose_times(left, right):
    return lax.dot_general(
        left, right, (((0,), (0,)), ((), ())), preferred_element_type=jnp.float32
    )


def gelu_exact(values):
    return jax.nn.gelu(values, approximate=False)


def norm_forward(summed, gain_row, shift_row):
    center = summed - jnp.mean(summed, axis=-1, keepdims=True)
    inverse = lax.rsqrt(jnp.mean(center * center, axis=-1, keepdims=True) + EPSILON)
    normed = center * inverse
    return (normed * gain_row + shift_row, normed, inverse)


def norm_backward(upstream, normed, inverse, gain_row):
    scaled = upstream * gain_row
    centered = (
        scaled
        - jnp.mean(scaled, axis=-1, keepdims=True)
        - normed * jnp.mean(scaled * normed, axis=-1, keepdims=True)
    )
    return (inverse * centered, jnp.sum(upstream * normed, axis=0), jnp.sum(upstream, axis=0))


def self_scores(query_rows, key_rows, segment):
    scores = jnp.einsum(
        "qhd,khd->hqk", query_rows, key_rows, preferred_element_type=jnp.float32
    ) * (1.0 / math.sqrt(HD))
    same_pair = segment[:, None] == segment[None, :]
    return jnp.where(same_pair[None], scores, NEGATIVE)


def self_window(window):
    query_rows, key_rows, value_rows, segment = window
    scores = self_scores(query_rows, key_rows, segment)
    highest = jnp.max(scores, axis=-1, keepdims=True)
    logsum = highest + jnp.log(jnp.sum(jnp.exp(scores - highest), axis=-1, keepdims=True))
    weights = jnp.exp(scores - logsum).astype(jnp.bfloat16)
    context = jnp.einsum("hqk,khd->qhd", weights, value_rows, preferred_element_type=jnp.float32)
    return (logsum, context.astype(jnp.bfloat16))


def self_window_back(window):
    query_rows, key_rows, value_rows, segment, logsum, grad_rows = window
    probability = jnp.exp(self_scores(query_rows, key_rows, segment) - logsum)
    grad_prob = jnp.einsum(
        "qhd,khd->hqk", grad_rows, value_rows, preferred_element_type=jnp.float32
    )
    grad_score = (
        probability * (grad_prob - jnp.sum(probability * grad_prob, axis=-1, keepdims=True))
    ).astype(jnp.bfloat16)
    scaling = 1.0 / math.sqrt(HD)
    grad_query = (
        jnp.einsum("hqk,khd->qhd", grad_score, key_rows, preferred_element_type=jnp.float32)
        * scaling
    )
    grad_key = (
        jnp.einsum("hqk,qhd->khd", grad_score, query_rows, preferred_element_type=jnp.float32)
        * scaling
    )
    grad_value = jnp.einsum(
        "hqk,qhd->khd",
        probability.astype(jnp.bfloat16),
        grad_rows,
        preferred_element_type=jnp.float32,
    )
    return jnp.concatenate(
        [grad_query.reshape(BLK, -1), grad_key.reshape(BLK, -1), grad_value.reshape(BLK, -1)],
        axis=1,
    ).astype(jnp.bfloat16)


def self_forward(text_rows, segment, weight_qkv, bias_query, bias_value):
    row_count, model_width = text_rows.shape
    blocks = row_count // BLK
    projected = jnp.dot(text_rows, weight_qkv, preferred_element_type=jnp.float32)
    query_rows = (
        (projected[:, :model_width] + bias_query).astype(jnp.bfloat16).reshape(blocks, BLK, H, HD)
    )
    key_rows = (
        projected[:, model_width : 2 * model_width].astype(jnp.bfloat16).reshape(blocks, BLK, H, HD)
    )
    value_rows = (
        (projected[:, 2 * model_width :] + bias_value)
        .astype(jnp.bfloat16)
        .reshape(blocks, BLK, H, HD)
    )
    segment = segment.reshape(blocks, BLK)
    logsum, context = lax.map(self_window, (query_rows, key_rows, value_rows, segment))
    return (
        (query_rows, key_rows, value_rows, segment, logsum),
        context.reshape(row_count, model_width),
    )


def self_backward(kept_self, grad_context):
    query_rows, key_rows, value_rows, segment, logsum = kept_self
    blocks = query_rows.shape[0]
    grad_rows = grad_context.reshape(blocks, BLK, H, HD)
    grad_projected = lax.map(
        self_window_back, (query_rows, key_rows, value_rows, segment, logsum, grad_rows)
    )
    return grad_projected.reshape(blocks * BLK, -1)


def cross_scores(query_rows, key_rows, region_rows):
    scores = jnp.einsum(
        "bkhd,brhd->bhkr", key_rows, query_rows, preferred_element_type=jnp.float32
    ) * (1.0 / math.sqrt(HD))
    key_region = lax.broadcasted_iota(jnp.int32, (key_rows.shape[1], 1), 0) // PR
    same_region = key_region[None] == region_rows[:, None, :]
    return jnp.where(same_region[:, None], scores, NEGATIVE)


def cross_forward(query_rows, key_rows, value_rows, region_rows):
    scores = cross_scores(query_rows, key_rows, region_rows)
    highest = jnp.max(scores, axis=2, keepdims=True)
    logsum = highest + jnp.log(jnp.sum(jnp.exp(scores - highest), axis=2, keepdims=True))
    weights = jnp.exp(scores - logsum).astype(jnp.bfloat16)
    context = jnp.einsum("bhkr,bkhd->brhd", weights, value_rows, preferred_element_type=jnp.float32)
    return (logsum, context.astype(jnp.bfloat16))


def cross_backward(query_rows, key_rows, value_rows, region_rows, logsum, grad_context):
    probability = jnp.exp(cross_scores(query_rows, key_rows, region_rows) - logsum)
    grad_prob = jnp.einsum(
        "bkhd,brhd->bhkr", value_rows, grad_context, preferred_element_type=jnp.float32
    )
    grad_score = (
        probability * (grad_prob - jnp.sum(probability * grad_prob, axis=2, keepdims=True))
    ).astype(jnp.bfloat16)
    scaling = 1.0 / math.sqrt(HD)
    grad_query = (
        jnp.einsum("bhkr,bkhd->brhd", grad_score, key_rows, preferred_element_type=jnp.float32)
        * scaling
    )
    grad_key = (
        jnp.einsum("bhkr,brhd->bkhd", grad_score, query_rows, preferred_element_type=jnp.float32)
        * scaling
    )
    grad_value = jnp.einsum(
        "bhkr,brhd->bkhd",
        probability.astype(jnp.bfloat16),
        grad_context,
        preferred_element_type=jnp.float32,
    )
    return (grad_query, grad_key, grad_value)


MESH = pl.DeviceIdType.MESH
WEIGHTS = ("qkv", "ckv", "sout", "cq", "cout", "up", "down")
LINK, CORE_LINK, HOP = 46e3, 400e3, 2.5


def named(names, refs):
    return types.SimpleNamespace(**dict(zip(names, refs)))


class Place:
    def __init__(self, line):
        self.line = line
        self.z = lax.axis_index("dp")
        self.f = lax.axis_index("fsdp")
        self.core = lax.rem(self.f, 2)
        self.x = lax.rem(self.f // 2, 2)
        self.y = self.f // 4
        self.other = {"c": 1 - self.core, "x": 1 - self.x, "y": 1 - self.y}
        steps = {"c": 1 - 2 * self.core, "x": 2 - 4 * self.x, "y": 4 - 8 * self.y}
        self.neighbours = {axis: self.f + step for axis, step in steps.items()}
        self.onward = [lax.rem(self.z + k, line) for k in range(line)]
        self.backward = [lax.rem(self.z + line - k, line) for k in range(line)]

    def across(self, axis):
        return (self.z, self.neighbours[axis])

    def along(self, offset):
        return (self.onward[offset], self.f)

    def ahead(self, offset):
        return self.onward[offset]

    def behind(self, offset):
        return self.backward[offset]

    def meet(self):
        barrier = pltpu.get_barrier_semaphore()
        partners = [self.across(axis) for axis in "cxy"] + [self.along(k) for k in range(1, self.line)]
        for device in partners:
            pl.semaphore_signal(barrier, inc=1, device_id=device, device_id_type=MESH)
        pl.semaphore_wait(barrier, len(partners))

    def block(self, whole):
        return tuple(slice(None) if axis in whole else getattr(self, axis) for axis in "zyx")


def spot(place):
    return place[0].at[place[1]] if isinstance(place, tuple) else place


class Copy:
    def __init__(self, make):
        self.make = make

    def wait_recv(self):
        self.make(True).wait_recv()

    def wait_send(self):
        self.make(False).wait_send()

    def wait(self):
        self.wait_send()
        self.wait_recv()


class LocalCopy(Copy):
    def wait(self):
        self.make(False).wait()


class Copies:
    def __init__(self, sent, received, local):
        self.sent, self.received, self.local = sent, received, local
        self.count = self.local_count = 0
        self.open = []
        self.writes = []

    def start(self, source, target, device, landing, remember=True):
        number = self.count
        self.count += 1
        copy = Copy(
            lambda arriving: pltpu.make_async_remote_copy(
                src_ref=spot(source),
                dst_ref=spot(landing if arriving else target),
                send_sem=self.sent.at[number],
                recv_sem=self.received.at[number],
                device_id=device,
                device_id_type=MESH,
            )
        )
        copy.make(False).start()
        if remember:
            self.open.append(copy)
        return copy

    def read(self, source, target):
        number = self.local_count
        self.local_count += 1
        copy = LocalCopy(
            lambda arriving: pltpu.make_async_copy(spot(source), spot(target), self.local.at[number])
        )
        copy.make(False).start()
        return copy

    def write(self, source, target):
        self.writes.append(self.read(source, target))

    def finish(self):
        for copy in self.writes:
            copy.wait()
        for copy in self.open:
            copy.wait_send()


class Clock:
    def __init__(self):
        self.now = 0.0
        self.free = dict.fromkeys("czyx", 0.0)

    def send(self, axis, size):
        rate = CORE_LINK if axis == "c" else LINK
        start = max(self.now, self.free[axis])
        self.free[axis] = start + size / rate
        return self.free[axis] + HOP


def volume(shape):
    return 2 * math.prod(shape)


class GatherUnit:
    def __init__(self, place, copies, clock, buffer, columns, order):
        self.place, self.copies, self.clock, self.buffer = place, copies, clock, buffer
        self.columns, self.order = columns, order + "c"
        self.held, self.stage, self.arrivals = "", 0, []
        self.size = volume((buffer.shape[4], columns.size))

    def view(self, index, half=None):
        half = self.place.core if half is None else half
        return self.buffer, (half,) + index + (slice(None), self.columns)

    def send(self):
        place = self.place
        axis = self.order[self.stage]
        mine = place.block(self.held)
        blocks = math.prod({"z": place.line, "y": 2, "x": 2}[held] for held in self.held)
        if axis == "z":
            moves = [(place.along(k), (place.behind(k),) + mine[1:], None) for k in range(1, place.line)]
            blocks *= place.line
        elif axis == "c":
            moves = [(place.across(axis), mine, place.other["c"])]
        else:
            level = "zyx".index(axis)
            moves = [(place.across(axis), mine[:level] + (place.other[axis],) + mine[level + 1 :], None)]
        self.arrivals = [
            self.copies.start(self.view(mine), self.view(mine), device, self.view(theirs, half))
            for device, theirs, half in moves
        ]
        self.due = self.clock.send(axis, blocks * self.size)
        self.held += axis
        self.stage += 1

    def step(self):
        for copy in self.arrivals:
            copy.wait_recv()
        self.clock.now = max(self.clock.now, self.due) + 0.1
        if self.stage == len(self.order):
            return True
        if self.stage == 1:
            self.begin()
        self.send()
        return False


class SumUnit:
    def __init__(self, place, copies, clock, total, landings, result, rows, columns, order):
        self.place, self.copies, self.clock, self.total = place, copies, clock, total
        self.landings, self.result, self.order = landings, result, order
        self.area = (rows, columns)
        self.left, self.stage, self.arrivals = "zyx", 0, []
        self.size = volume((rows.size, columns.size))

    def send(self):
        place, area, stage = self.place, self.area, self.stage
        axis = self.order[stage]
        mine = place.block(self.left)
        level = "zyx".index(axis)
        landing = self.landings[stage]
        self.left = self.left.replace(axis, "")
        each = math.prod({"z": place.line, "y": 2, "x": 2}[left] for left in self.left)
        blocks = each
        if axis == "z":
            moves = []
            for offset in range(1, place.line):
                span = pl.ds((offset - 1) * each, each) if each > 1 else offset - 1
                moves.append((place.along(offset), place.ahead(offset), span))
            blocks *= place.line
        else:
            span = pl.ds(0, each) if each > 1 else 0
            if stage == 0:
                span = (pl.ds(0, place.line), pl.ds(0, 2))
            moves = [(place.across(axis), place.other[axis], span)]
        self.arrivals = []
        for device, goal, span in moves:
            there = landing, (span if isinstance(span, tuple) else (span,)) + area
            source = self.total, mine[:level] + (goal,) + mine[level + 1 :] + area
            self.arrivals.append(self.copies.start(source, there, device, there))
        self.due = self.clock.send(axis, blocks * self.size)
        self.axis = axis
        self.stage += 1

    def step(self):
        for copy in self.arrivals:
            copy.wait_recv()
        self.clock.now = max(self.clock.now, self.due) + 0.2
        place, area, landing, line = self.place, self.area, self.landings[self.stage - 1], self.place.line

        def add(index, spots):
            value = self.total[index + area].astype(jnp.float32)
            for one in spots:
                value += landing[one + area].astype(jnp.float32)
            return value

        def store(index, spots):
            self.total[index + area] = add(index, spots).astype(jnp.bfloat16)

        if self.stage == 3:
            count = line - 1 if self.axis == "z" else 1
            value = add((place.z, place.y, place.x), [(k,) for k in range(count)])
            put_halves(self.result, area, value)
            return True
        if self.stage == 1:

            def one(z, carry):
                for other in range(2):
                    store((z, place.y, other) if self.axis == "y" else (z, other, place.x), [(z, other)])
                return carry

            lax.fori_loop(0, line, one, 0)
        elif self.axis == "z":
            for other in range(2):
                index = (place.z, place.y, other) if self.left == "x" else (place.z, other, place.x)
                store(index, [(k * 2 + other,) for k in range(line - 1)])
        else:

            def one(z, carry):
                store((z, place.y, place.x), [(z,)])
                return carry

            lax.fori_loop(0, line, one, 0)
        self.send()
        return False


def put_halves(final, area, value):
    rows, columns = area
    half = final.shape[1]
    done = 0
    while done < rows.size:
        core, at = (rows.start + done) // half, (rows.start + done) % half
        step = min(rows.size - done, half - at)
        final[core, pl.ds(at, step), columns] = value[done : done + step]
        done += step


class Schedule:
    def __init__(self, clock, done):
        self.clock, self.done = clock, done
        self.tasks, self.flying = [], []

    def task(self, cost, function, *arguments, ready=lambda: True):
        self.tasks.append((cost, functools.partial(function, *arguments), ready))

    def launch(self, unit):
        unit.send()
        self.flying.append(unit)

    def run(self, drain=True):
        while self.tasks or (drain and self.flying):
            soonest = min(self.flying, key=lambda unit: unit.due) if self.flying else None
            runnable = self.tasks and self.tasks[0][2]()
            if soonest is not None and (soonest.due <= self.clock.now or not runnable):
                if soonest.step():
                    self.flying.remove(soonest)
                    self.done(soonest)
            else:
                cost, function, _ = self.tasks.pop(0)
                function()
                self.clock.now += cost


def padded(rows):
    return -(-rows // 16) * 16


def matrix(value):
    return value.reshape(-1, value.shape[-1])


def dot(left, right, contract=(1, 0)):
    return lax.dot_general(
        left, right, (((contract[0],), (contract[1],)), ((), ())), preferred_element_type=jnp.float32
    )


def whole(buffer):
    return jnp.concatenate([matrix(buffer[0]), matrix(buffer[1])], axis=1)


def column_spans(rows, columns):
    wide = 384 if rows <= 64 else 128
    return [pl.ds(column, wide) for column in range(0, columns, wide)]


def merged_rows(place, mine, other):
    mine, other = mine.astype(jnp.float32), other.astype(jnp.float32)
    first = jnp.where(place.core == 0, mine, other)
    second = jnp.where(place.core == 0, other, mine)
    return jnp.concatenate([first, second], axis=0).astype(jnp.bfloat16)


def column_half(place, values, own):
    half = values.shape[1] // 2
    left, right = values[:, :half].astype(jnp.float32), values[:, half:].astype(jnp.float32)
    return jnp.where((place.core == 0) == own, left, right)

def gelu_pair(values):
    half_square = jnp.exp(values * values * -0.5)
    size = jnp.abs(values)
    t = 1.0 / (1.0 + (0.3275911 * math.sqrt(0.5)) * size)
    series = t * (
        0.5 * 0.254829592
        + t * (-0.5 * 0.284496736 + t * (0.5 * 1.421413741 + t * (-0.5 * 1.453152027 + t * (0.5 * 1.061405429))))
    )
    tail = series * half_square
    phi = jnp.where(values < 0, tail, 1.0 - tail)
    slope = phi + values * half_square * (1.0 / math.sqrt(2.0 * math.pi))
    return values * phi, slope


def spread_vectors(vectors_all, rows_out, hidden_out, narrow, wide, line):
    lanes = lax.broadcasted_iota(jnp.int32, (16, 128), 1)
    sums = {id(rows_out): {}, id(hidden_out): {}}

    def place(target, values, start, size):
        found = sums[id(target)]
        tile, shift = start // 128, start % 128
        rolled = pltpu.roll(values, shift, 1) if shift else values
        lane = lanes[: values.shape[0]]
        first = jnp.where((lane >= shift) & (lane < shift + size), rolled, 0.0)
        found[tile] = found[tile] + first if tile in found else first
        if shift + size > 128:
            second = jnp.where(lane < shift + size - 128, rolled, 0.0)
            tile += 1
            found[tile] = found[tile] + second if tile in found else second

    for z in range(line):
        for y in range(2):
            for x in range(2):
                for core in range(2):
                    device = ((z * 2 + y) * 2 + x) * 2 + core
                    values = vectors_all[core, z, y, x].astype(jnp.float32)
                    place(rows_out, values, device * narrow, narrow)
                    place(hidden_out, values[8:], device * wide, wide)
    for target in (rows_out, hidden_out):
        for tile, value in sums[id(target)].items():
            target[:, pl.ds(tile * 128, 128)] = value

KEPT = ("qkv", "attention", "query", "key_value", "cross_attention", "normed", "inverse", "slope", "joined", "rows")
PAIRS = ("text", "patches", "context", "low_one", "context_cross", "low_two", "hidden_low")
LOCAL = ("hidden", "context", "low_one", "context_cross", "low_two", "hidden_low")


def forward_kernel(line, *refs):
    refs = list(refs)
    take = lambda names: named(names, [refs.pop(0) for _ in names])
    shards = take(WEIGHTS)
    vectors, text, patches, pair_row, region_row = [refs.pop(0) for _ in range(5)]
    outs, kept_out, pairs = take(WEIGHTS), take(KEPT), take(PAIRS)
    buffers, outgoing, incoming = take(WEIGHTS), take(WEIGHTS), take(WEIGHTS)
    kept = named(KEPT + LOCAL, [refs.pop(0) for _ in KEPT + LOCAL])
    vectors_all, pair_column, work, keys_all, values_all, sent, received, local = refs
    place = Place(line)
    copies = Copies(sent, received, local)
    clock = Clock()
    tokens, width = text.shape
    rows_all, hidden_all = kept.rows, kept.hidden
    block = tokens // line
    narrow = shards.qkv.shape[0]
    keys = patches.shape[0]
    for name in WEIGHTS:
        shard, target = getattr(shards, name), getattr(outgoing, name)
        away = column_half(place, shard[...], False)
        padding = target.shape[0] - shard.shape[0]
        if padding:
            away = jnp.concatenate([away, jnp.zeros((padding, away.shape[1]), jnp.float32)], axis=0)
        target[...] = away.astype(jnp.bfloat16)
    vectors_all[place.core, place.z, place.y, place.x] = vectors[...]
    place.meet()
    swaps = {}
    for name in WEIGHTS:
        there = getattr(incoming, name)
        swaps[name] = copies.start(getattr(outgoing, name), there, place.across("c"), there)
    pair_column[...] = jnp.broadcast_to(pair_row[...].astype(jnp.float32), (128, tokens)).T
    arrivals = []

    def merge(name):
        swaps[name].wait_recv()
        shard = getattr(shards, name)
        mine = column_half(place, shard[...], True)
        other = getattr(incoming, name)[...][: shard.shape[0]]
        getattr(buffers, name)[place.core, place.z, place.y, place.x] = merged_rows(place, mine, other)

    def keep(source, target):
        copies.write(source, target)

    def pair(source, target, *columns):
        there = target.at[(place.core,) + columns]
        copies.write(source, there)
        arrivals.append(
            copies.start(source, there, place.across("c"), target.at[(1 - place.core,) + columns])
        )

    def row(number):
        return rows_all[pl.ds(number, 1), :]

    qkv, context, low_one, query, context_cross = (
        kept.qkv, kept.context, kept.low_one, kept.query, kept.context_cross
    )
    hidden, slope, low_two = kept.hidden_low, kept.slope, kept.low_two
    attention, cross_attention = kept.attention, kept.cross_attention
    key_value = kept.key_value

    def project_qkv(part):
        def one(half, carry):
            size = 384
            column = pl.multiple_of(half * (3 * size) + part * size, 128)
            value = dot(text[...], matrix(buffers.qkv[half, :, :, :, :, pl.ds(part * size, size)]))
            group = (half * 3 + part) // 2
            shift = pl.multiple_of(lax.rem(half * 3 + part, 2) * size, 128)
            biased = jnp.where(
                group == 0,
                rows_all[pl.ds(3, 1), pl.ds(shift, size)],
                jnp.where(group == 1, 0.0, rows_all[pl.ds(4, 1), pl.ds(shift, size)]),
            )
            qkv[:, pl.ds(column, size)] = (value + biased).astype(jnp.bfloat16)
            return carry

        lax.fori_loop(0, 2, one, 0)

    strip = 128

    def attend(pair):
        lane = lax.broadcasted_iota(jnp.int32, (strip, 128), 1)
        columns = pl.ds(pair * 128, 128)

        def one(number, carry):
            rows = pl.ds(pl.multiple_of(number * strip, strip), strip)
            two = qkv[rows, columns].astype(jnp.float32) * (1.0 / math.sqrt(HD))
            key_rows = qkv[:, pl.ds(width + pair * 128, 128)]
            value_rows = qkv[:, pl.ds(2 * width + pair * 128, 128)]
            same = jnp.concatenate([pair_column[rows, :]] * (tokens // 128), axis=1) == pair_row[...].astype(
                jnp.float32
            )
            result = None
            for head in range(2):
                own = (lane < HD) if head == 0 else (lane >= HD)
                scores = dot(jnp.where(own, two, 0.0).astype(jnp.bfloat16), key_rows, (1, 1))
                scores = jnp.where(same, scores, NEGATIVE)
                scores = jnp.exp(scores - jnp.max(scores, axis=1, keepdims=True))
                scores = scores * (1.0 / jnp.sum(scores, axis=1, keepdims=True))
                low = scores.astype(jnp.bfloat16)
                attention[pair * 2 + head, rows, :] = low
                value = dot(low, value_rows)
                result = value if head == 0 else jnp.where(own, value, result)
            context[rows, columns] = result.astype(jnp.bfloat16)
            return carry

        lax.fori_loop(0, tokens // strip, one, 0)
        keep(attention.at[pl.ds(2 * pair, 2)], kept_out.attention.at[pl.ds(2 * pair, 2)])

    def normalize(number, summed, low):
        normed, inverse = kept.normed, kept.inverse
        gain, shift = row(number), row(10 + number)
        step = 64

        def one(index, carry):
            rows = pl.ds(pl.multiple_of(index * step, step), step)
            value = work[rows, :] + summed(rows)
            center = value - jnp.mean(value, axis=1, keepdims=True)
            scale = lax.rsqrt(jnp.mean(center * center, axis=1, keepdims=True) + EPSILON)
            value = center * scale
            normed[number, rows, :] = value
            inverse[number, rows, :] = jnp.broadcast_to(scale, (step, 128))
            low(rows, value * gain + shift)
            return carry

        lax.fori_loop(0, tokens // step, one, 0)
        keep(normed.at[number], kept_out.normed.at[number])
        keep(inverse.at[number], kept_out.inverse.at[number])

    def self_out():
        work[...] = dot(context[...], whole(buffers.sout))

        def low(rows, value):
            low_one[rows, :] = value.astype(jnp.bfloat16)

        normalize(0, lambda rows: text[rows, :].astype(jnp.float32) + row(5), low)
        pair(context, pairs.context)
        pair(low_one, pairs.low_one)

    def project_patches(part):
        size = 384
        value = dot(patches[...], matrix(buffers.ckv[0, :, :, :, :, pl.ds(part * size, size)]))
        key_value[place.z, :, pl.ds(part * size, size)] = value.astype(jnp.bfloat16)
        value = dot(patches[...], matrix(buffers.ckv[1, :, :, :, :, pl.ds(part * size, size)]))
        value += rows_all[pl.ds(7, 1), pl.ds(part * size, size)]
        key_value[place.z, :, pl.ds(width + part * size, size)] = value.astype(jnp.bfloat16)

    shared = []

    def share_keys():
        for offset in range(1, line):
            origin = place.behind(offset)
            shared.append(
                copies.start(
                    key_value.at[place.z], key_value.at[place.z], place.along(offset), key_value.at[origin]
                )
            )

    def project_query():
        work[...] = dot(low_one[...], whole(buffers.cq))
        query[...] = (work[...] + row(6)).astype(jnp.bfloat16)
        keep(query, kept_out.query)

    def cross(owner):
        if owner == 0:
            for copy in shared:
                copy.wait_recv()
            keep(key_value, kept_out.key_value)
        lane = lax.broadcasted_iota(jnp.int32, (keys, width), 1) // HD
        for head in range(H):
            rows = pl.ds(head * keys, keys)
            keys_all[rows, :] = jnp.where(
                lane == head, key_value[owner, :, pl.ds(0, width)].astype(jnp.float32), 0.0
            ).astype(jnp.bfloat16)
            values_all[rows, :] = jnp.where(
                lane == head, key_value[owner, :, pl.ds(width, width)].astype(jnp.float32), 0.0
            ).astype(jnp.bfloat16)
        rows = pl.ds(owner * block, block)
        scores = dot(keys_all[...], query[rows, :], (1, 1)) * (1.0 / math.sqrt(HD))
        region = lax.broadcasted_iota(jnp.int32, (keys, block), 0) // PR
        same = region == region_row[:, rows]
        scores = jnp.where(same[None], scores.reshape(H, keys, block), NEGATIVE)
        scores = jnp.exp(scores - jnp.max(scores, axis=1, keepdims=True))
        scores = scores * (1.0 / jnp.sum(scores, axis=1, keepdims=True))
        scores = scores.reshape(H * keys, block).astype(jnp.bfloat16)
        cross_attention[owner] = scores
        context_cross[rows, :] = dot(scores, values_all[...], (0, 0)).astype(jnp.bfloat16)
        if owner == line - 1:
            keep(cross_attention, kept_out.cross_attention)
            pair(context_cross, pairs.context_cross)

    def cross_out():
        work[...] = dot(context_cross[...], whole(buffers.cout))
        first_gain, first_shift = row(0), row(10)

        def low(rows, value):
            low_two[rows, :] = value.astype(jnp.bfloat16)

        normalize(1, lambda rows: kept.normed[0, rows, :] * first_gain + first_shift + row(8), low)
        pair(low_two, pairs.low_two)

    def expand(part):
        size = 384
        half_width = buffers.up.shape[5]

        def one(half, carry):
            column = pl.multiple_of(half * half_width + part * size, 128)
            columns = pl.ds(column, size)
            value = dot(low_two[...], matrix(buffers.up[half, :, :, :, :, pl.ds(part * size, size)]))
            value, grad = gelu_pair(value + hidden_all[pl.ds(5, 1), columns])
            hidden[:, columns] = value.astype(jnp.bfloat16)
            slope[:, columns] = grad.astype(jnp.bfloat16)
            return carry

        lax.fori_loop(0, 2, one, 0)
        for half in range(2):
            columns = pl.ds(half * half_width + part * size, size)
            pair(hidden.at[:, columns], pairs.hidden_low, slice(None), columns)
            keep(slope.at[:, columns], kept_out.slope.at[:, columns])

    def contract(part):
        size = 128
        buffer = buffers.down
        columns = pl.ds(part * size, size)
        both = jnp.concatenate(
            [matrix(buffer[0, :, :, :, :, columns]), matrix(buffer[1, :, :, :, :, columns])], axis=1
        )
        value = dot(hidden[...], both)
        work[:, pl.ds(part * size, size)] = value[:, :size]
        work[:, pl.ds(width // 2 + part * size, size)] = value[:, size:]

    def finish():
        gain, shift = row(1), row(11)

        def low(rows, value):
            valid = jnp.concatenate([pair_column[rows, :]] * (width // 128), axis=1) >= 0
            kept.joined[rows, :] = jnp.where(valid, value, 0.0).astype(jnp.bfloat16)

        normalize(2, lambda rows: kept.normed[1, rows, :] * gain + shift + row(9), low)
        keep(kept.joined, kept_out.joined)

    present, counts = {}, {}
    waiting = []
    merged = set()

    def done(unit):
        present[unit.name] = present.get(unit.name, 0) + 1
        name = unit.name
        if present[name] == counts.get(name):
            keep(getattr(buffers, name), getattr(outs, name))

    schedule = Schedule(clock, done)

    def begin():
        if waiting:
            unit = waiting.pop(0)
            if unit.name and unit.name not in merged:
                merge(unit.name)
                merged.add(unit.name)
            schedule.launch(unit)

    def unit_of(buffer, name, columns):
        order = ("zyx", "zxy")[len(waiting) % 2]
        unit = GatherUnit(place, copies, clock, buffer, columns, order)
        unit.name, unit.begin = name, begin
        waiting.append(unit)

    unit_of(vectors_all, "", pl.ds(0, 128))
    for name in WEIGHTS:
        buffer = getattr(buffers, name)
        spans = column_spans(*buffer.shape[4:])
        counts[name] = len(spans)
        for columns in spans:
            unit_of(buffer, name, columns)

    def task(name, count, cost, function, *arguments):
        schedule.task(cost, function, *arguments, ready=lambda: present.get(name, 0) >= count)

    def spread():
        spread_vectors(vectors_all, rows_all, hidden_all, narrow, shards.down.shape[0], line)
        keep(rows_all, kept_out.rows)

    pair(text, pairs.text)
    pair(patches, pairs.patches)
    task("", 1, 1.0, spread)
    for part in range(3):
        task("qkv", part + 1, 1.5, project_qkv, part)
    task("", 1, 0.0, keep, qkv, kept_out.qkv)
    for number in range(H // 2):
        task("", 1, 1.8, attend, number)
        if number == 3:
            for part in range(2):
                task("ckv", part + 1, 0.5, project_patches, part)
            task("", 1, 0.1, share_keys)
    task("sout", 1, 2.0, self_out)
    task("cq", 1, 1.0, project_query)
    for owner in range(line):
        task("", 1, 1.5, cross, owner)
    task("cout", 1, 2.0, cross_out)
    for part in range(4):
        task("up", part + 1, 3.0, expand, part)
    for part in range(3):
        task("down", part + 1, 1.5, contract, part)
    task("", 1, 1.5, finish)
    for _ in range(3):
        begin()
    schedule.run()
    for copy in arrivals:
        copy.wait_recv()
    copies.finish()

SAVED = ("qkv", "attention", "query", "key_value", "cross_attention", "normed", "inverse", "slope", "rows")
ORDERS = ("yxz", "xyz")


class VectorUnit:
    def __init__(self, place, copies, clock, total, landings):
        self.place, self.copies, self.clock = place, copies, clock
        self.total, self.landings = total, landings
        self.stage = 0

    def send(self):
        place, stage = self.place, self.stage
        if stage < 3:
            devices = [place.across("cxy"[stage])]
        else:
            devices = [place.along(offset) for offset in range(1, place.line)]
        self.arrivals = []
        for number, device in enumerate(devices):
            there = self.landings, (stage + number,)
            self.arrivals.append(self.copies.start(self.total, there, device, there, False))
        self.due = self.clock.now + 3.0
        self.stage += 1

    def step(self):
        for copy in self.arrivals:
            copy.wait()
        value = self.total[...]
        for number in range(len(self.arrivals)):
            value += self.landings[self.stage - 1 + number]
        self.total[...] = value
        self.clock.now = max(self.clock.now, self.due) + 0.1
        if self.stage == 4:
            return True
        self.send()
        return False


def backward_kernel(line, *refs):
    refs = list(refs)
    take = lambda names: named(names, [refs.pop(0) for _ in names])
    pop = lambda count: [refs.pop(0) for _ in range(count)]
    weights, saved, pairs = take(WEIGHTS), take(SAVED), take(PAIRS)
    cotangent, pair_row = pop(2)
    outs = take(WEIGHTS)
    text_grad, patch_grad, gains_out, biases_out, hidden_out = pop(5)
    totals, first, second, third, finals, swapped, landed = (take(WEIGHTS) for _ in range(7))
    work, inverse, rows_all, small, small_landed, key_parts, key_landed, pair_column, hidden_sum = pop(9)
    grad_kv, sent, received, local = pop(4)
    place = Place(line)
    copies = Copies(sent, received, local)
    clock = Clock()
    core = place.core
    tokens, width = work.shape
    hidden_width = hidden_sum.shape[1]
    block = tokens // line
    keys = grad_kv.shape[0]
    scaling = 1.0 / math.sqrt(HD)
    remaining = {}
    swaps = {}

    def done(unit):
        if unit is vectors:
            return
        remaining[unit.name] -= 1
        if not remaining[unit.name]:
            final, there = getattr(finals, unit.name), getattr(swapped, unit.name)
            swaps[unit.name] = copies.start((final, (place.other["c"],)), there, place.across("c"), there)

    schedule = Schedule(clock, done)
    vectors = VectorUnit(place, copies, clock, small, small_landed)

    def launch(name, rows, columns, count):
        remaining.setdefault(name, count)
        landings = [getattr(group, name) for group in (first, second, third)]
        order = ORDERS[launch.number % len(ORDERS)]
        launch.number += 1
        unit = SumUnit(
            place, copies, clock, getattr(totals, name), landings, getattr(finals, name), rows, columns, order
        )
        unit.name = name
        schedule.launch(unit)

    launch.number = 0

    def task(cost, function, *arguments):
        schedule.task(cost, function, *arguments)

    def half(size, other=False, offset=0, part=None):
        which = 1 - core if other else core
        return pl.ds(pl.multiple_of(which * size + offset, 128), size if part is None else part)

    def hand_over(source, target, columns=None):
        size = target.shape[1]
        there = target if columns is None else (target, (slice(None), columns))
        away = half(size, True) if columns is None else half(size, True, columns.start, columns.size)
        return copies.start((source, (slice(None), away)), there, place.across("c"), there, False)

    def norm_back(number, bias_number, normed, upstream, low):
        gain = rows_all[pl.ds(number, 1), :]
        step = 64

        def one(index, carry):
            rows = pl.ds(pl.multiple_of(index * step, step), step)
            grad, normal = upstream(rows), normed[rows, :]
            scaled = grad * gain
            center = scaled - jnp.mean(scaled, axis=1, keepdims=True)
            center -= normal * jnp.mean(scaled * normal, axis=1, keepdims=True)
            value = inverse[number, rows, :][:, :1] * center
            work[rows, :] = value
            rounded = value.astype(jnp.bfloat16)
            low[rows, :] = rounded
            sums = (grad * normal, grad, rounded.astype(jnp.float32))
            return tuple(old + jnp.sum(new, axis=0, keepdims=True) for old, new in zip(carry, sums))

        zero = jnp.zeros((1, width), jnp.float32)
        gain_sum, shift_sum, bias_sum = lax.fori_loop(0, tokens // step, one, (zero, zero, zero))
        small[pl.ds(number, 1), :] = gain_sum
        small[pl.ds(10 + number, 1), :] = shift_sum
        small[pl.ds(bias_number, 1), :] = bias_sum

    def weight_grad(name, inputs, low, landing, columns, span=None):
        size = landing.shape[1]
        own = half(size, False, columns.start, columns.size)
        span = slice(None) if span is None else span
        value = dot(inputs[core, :, span], low[:, own], (0, 0))
        value += dot(inputs[1 - core, :, span], landing[:, columns], (0, 0))
        return value.astype(jnp.bfloat16)

    def spread_columns(name, inputs, low, columns, count):
        total = getattr(totals, name)
        value = weight_grad(name, inputs, low, getattr(landed, name), columns)
        total[:, :, :, :, columns] = value.reshape(total.shape[:4] + (columns.size,))
        launch(name, pl.ds(0, total.shape[3]), columns, count)

    def feed_forward(up, down, inputs_up, inputs_down, slope, normed, grad_low, cotangent_here):
        reads = [
            copies.read(source, target)
            for source, target in (
                (cotangent, cotangent_here),
                (saved.normed.at[2], normed),
                (saved.inverse, inverse),
                (saved.rows, rows_all),
                (weights.down, down),
                (saved.slope, slope),
                (pairs.hidden_low, inputs_down),
                (pairs.low_two, inputs_up),
                (weights.up, up),
            )
        ]
        sends = []

        def third_norm():
            for copy in reads[:4]:
                copy.wait()
            small[...] = jnp.zeros_like(small)

            def upstream(rows):
                valid = jnp.concatenate([pair_column[rows, :]] * (width // 128), axis=1) >= 0
                return jnp.where(valid, cotangent_here[rows, :].astype(jnp.float32), 0.0)

            norm_back(2, 9, normed, upstream, grad_low)
            sends.append(hand_over(grad_low, landed.down))

        size = 384
        half_width = hidden_width // 2

        def expand(other):
            if other:
                for copy in reads[4:6]:
                    copy.wait()

            def one(part, carry):
                column = (1 - core if other else core) * half_width + part * size
                number = column // size
                both = jnp.concatenate(
                    [matrix(down[side, number // 2, lax.rem(number, 2)]) for side in range(2)], axis=1
                )
                columns = pl.ds(pl.multiple_of(column, 128), size)
                value = dot(grad_low[...], both, (1, 1)) * slope[:, columns].astype(jnp.float32)
                value = value.astype(jnp.bfloat16)
                slope[:, columns] = value
                hidden_sum[pl.ds(0, 1), columns] = jnp.sum(value.astype(jnp.float32), axis=0, keepdims=True)
                return carry

            lax.fori_loop(0, half_width // size, one, 0)
            if other:
                sends.append(hand_over(slope, landed.up))

        def grad_down():
            reads[6].wait()
            sends[0].wait_recv()
            total = totals.down

            def one(z, carry):
                span = pl.ds(pl.multiple_of(z * (hidden_width // line), 128), hidden_width // line)
                value = weight_grad("down", inputs_down, grad_low, landed.down, pl.ds(0, width // 2), span)
                total[z] = value.reshape(total.shape[1:])
                return carry

            lax.fori_loop(0, line, one, 0)
            for row in range(0, total.shape[3], 48):
                launch("down", pl.ds(row, 48), pl.ds(0, width // 2), total.shape[3] // 48)

        def grad_up(part):
            if part == 0:
                reads[7].wait()
                sends[1].wait_recv()
                for k in range(4):
                    small[pl.ds(13 + k, 1), :] = hidden_sum[pl.ds(0, 1), pl.ds(k * width, width)]
            spread_columns("up", inputs_up, slope, pl.ds(part * size, size), half_width // size)

        def grad_second():
            reads[8].wait()
            for side in range(2):
                work[...] += dot(slope[:, pl.ds(side * half_width, half_width)], matrix(up[side]), (1, 1))

        task(2.0, third_norm)
        task(2.0, expand, True)
        task(4.0, grad_down)
        task(2.0, expand, False)
        for part in range(half_width // size):
            task(1.2, grad_up, part)
        task(3.0, grad_second)
        schedule.run(False)
        for copy in sends:
            copy.wait_send()

    def attentions(qkv_w, ckv_w, sout_w, cq_w, cout_w, left_one, left_two, patch_pair, normed, query, key_value,
                   cross_attention, keys_all, values_all, qkv, attention, scores_low, grad_two_low, grad_query,
                   grad_one_low, grad_context):
        order = (
            (saved.normed.at[1], normed.at[1]),
            (weights.cout, cout_w),
            (pairs.context_cross, left_one),
            (saved.key_value, key_value),
            (saved.cross_attention, cross_attention),
            (saved.query, query),
            (weights.cq, cq_w),
            (saved.normed.at[0], normed.at[0]),
            (pairs.low_one, left_two),
            (weights.sout, sout_w),
            (weights.ckv, ckv_w),
            (pairs.patches, patch_pair),
            (saved.qkv, qkv),
            (saved.attention.at[pl.ds(0, 2)], attention.at[0]),
            (weights.qkv, qkv_w),
        )
        reads = [copies.read(source, target) for source, target in order]
        waited = set()
        later = {}
        sends = {}
        size = 384
        third_part = pl.ds(0, width // 2)

        def need(*numbers):
            for number in numbers:
                if number not in waited:
                    reads[number].wait()
                    waited.add(number)

        def second_norm():
            need(0)
            norm_back(1, 8, normed.at[1], lambda rows: work[rows, :], grad_two_low)
            sends["t"] = hand_over(grad_two_low, landed.cout)

        def context_grad():
            need(1)
            grad_context[...] = dot(grad_two_low[...], whole(cout_w), (1, 1)).astype(jnp.bfloat16)

        def cross(offset):
            need(3, 4, 5)
            owner = place.ahead(offset)
            lane = lax.broadcasted_iota(jnp.int32, (keys, width), 1) // HD
            key_rows = key_value[owner, :, pl.ds(0, width)].astype(jnp.float32)
            value_rows = key_value[owner, :, pl.ds(width, width)].astype(jnp.float32)
            for head in range(H):
                rows = pl.ds(head * keys, keys)
                keys_all[rows, :] = jnp.where(lane == head, key_rows, 0.0).astype(jnp.bfloat16)
                values_all[rows, :] = jnp.where(lane == head, value_rows, 0.0).astype(jnp.bfloat16)
            rows = pl.ds(pl.multiple_of(owner * block, block), block)
            probability = cross_attention[owner].astype(jnp.float32).reshape(H, keys, block)
            grad = dot(values_all[...], grad_context[rows, :], (1, 1)).reshape(H, keys, block)
            grad = probability * (grad - jnp.sum(probability * grad, axis=1, keepdims=True))
            grad = grad.reshape(H * keys, block).astype(jnp.bfloat16)
            grad_query[rows, :] = (dot(grad, keys_all[...], (0, 0)) * scaling).astype(jnp.bfloat16)
            lane = lax.broadcasted_iota(jnp.int32, (keys, 128), 1)
            for pair in range(H // 2):
                columns = pl.ds(pair * 128, 128)
                heads = slice(pair * 2 * keys, (pair + 1) * 2 * keys)
                value = dot(grad[heads], query[rows, columns]) * scaling
                key_parts[offset, :, columns] = jnp.where(lane < HD, value[:keys], value[keys:]).astype(
                    jnp.bfloat16
                )
                value = dot(cross_attention[owner, pl.ds(heads.start, 2 * keys), :], grad_context[rows, columns])
                key_parts[offset, :, pl.ds(width + pair * 128, 128)] = jnp.where(
                    lane < HD, value[:keys], value[keys:]
                ).astype(jnp.bfloat16)
            if offset:
                there = key_landed, (offset - 1,)
                sends[offset] = copies.start((key_parts, (offset,)), there, place.along(offset), there)
            if offset == 0:
                sends["q"] = hand_over(grad_query, landed.cq)

        def grad_cout():
            need(2)
            sends["t"].wait_recv()
            spread_columns("cout", left_one, grad_two_low, third_part, 1)
            later["context"] = copies.read(pairs.context, left_one)

        def grad_first():
            need(6)
            work[...] += dot(grad_query[...], whole(cq_w), (1, 1))
            small[pl.ds(6, 1), :] = jnp.sum(grad_query[...].astype(jnp.float32), axis=0, keepdims=True)

        def first_norm():
            need(7)
            norm_back(0, 5, normed.at[0], lambda rows: work[rows, :], grad_one_low)
            sends["s"] = hand_over(grad_one_low, landed.sout)

        def grad_cq():
            need(8)
            sends["q"].wait_recv()
            spread_columns("cq", left_two, grad_query, third_part, 1)
            later["text"] = copies.read(pairs.text, left_two)

        def self_context():
            need(9)
            grad_context[...] = dot(grad_one_low[...], whole(sout_w), (1, 1)).astype(jnp.bfloat16)

        def grad_sout():
            later["context"].wait()
            sends["s"].wait_recv()
            spread_columns("sout", left_one, grad_one_low, third_part, 1)

        def key_grad():
            value = key_parts[0].astype(jnp.float32)
            for offset in range(1, line):
                sends[offset].wait_recv()
                value += key_landed[offset - 1].astype(jnp.float32)
            value = value.astype(jnp.bfloat16)
            grad_kv[...] = value
            sends["k"] = hand_over(grad_kv, landed.ckv)
            small[pl.ds(7, 1), :] = jnp.sum(value[:, width:].astype(jnp.float32), axis=0, keepdims=True)
            need(10)
            patch_grad[...] = dot(grad_kv[...], whole(ckv_w), (1, 1))

        def grad_ckv(part):
            if part == 0:
                need(11)
                sends["k"].wait_recv()
            spread_columns("ckv", patch_pair, grad_kv, pl.ds(part * size, size), 2)

        strip = 128

        def attend(pair):
            slot = pair % 2
            if pair == 0:
                need(12, 13)
            else:
                later[pair].wait()
            if pair + 1 < H // 2:
                later[pair + 1] = copies.read(
                    saved.attention.at[pl.ds(2 * pair + 2, 2)], attention.at[1 - slot]
                )
            columns, key_columns = pl.ds(pair * 128, 128), pl.ds(width + pair * 128, 128)
            value_columns = pl.ds(2 * width + pair * 128, 128)

            def own(value, head):
                lane = lax.broadcasted_iota(jnp.int32, value.shape, 1)
                return jnp.where((lane < HD) == (head == 0), value.astype(jnp.float32), 0.0).astype(jnp.bfloat16)

            def one(number, carry):
                rows = pl.ds(pl.multiple_of(number * strip, strip), strip)
                for head in range(2):
                    grad = dot(own(grad_context[rows, columns], head), qkv[:, value_columns], (1, 1))
                    probability = attention[slot, head, rows, :].astype(jnp.float32)
                    grad = probability * (grad - jnp.sum(probability * grad, axis=1, keepdims=True))
                    scores_low[head, rows, :] = grad.astype(jnp.bfloat16)
                return carry

            lax.fori_loop(0, tokens // strip, one, 0)
            query_grad = key_grad = value_grad = 0.0
            for head in range(2):
                query_grad += dot(scores_low[head], own(qkv[:, key_columns], head))
                key_grad += dot(scores_low[head], own(qkv[:, columns], head), (0, 0))
                value_grad += dot(attention[slot, head], own(grad_context[:, columns], head), (0, 0))
            query_grad = (query_grad * scaling).astype(jnp.bfloat16)
            value_grad = value_grad.astype(jnp.bfloat16)
            qkv[:, columns] = query_grad
            qkv[:, key_columns] = (key_grad * scaling).astype(jnp.bfloat16)
            qkv[:, value_columns] = value_grad
            small[pl.ds(3, 1), columns] = jnp.sum(query_grad.astype(jnp.float32), axis=0, keepdims=True)
            small[pl.ds(4, 1), columns] = jnp.sum(value_grad.astype(jnp.float32), axis=0, keepdims=True)
            if pair + 1 == H // 2:
                sends["p"] = hand_over(qkv, landed.qkv)
                schedule.launch(vectors)

        def grad_qkv(part):
            if part == 0:
                later["text"].wait()
                sends["p"].wait_recv()
            spread_columns("qkv", left_two, qkv, pl.ds(part * size, size), 3)

        def text_back(side):
            need(14)
            size = 3 * width // 2
            work[...] += dot(qkv[:, pl.ds(side * size, size)], matrix(qkv_w[side]), (1, 1))
            if side == 1:
                copies.write(work, text_grad)

        task(2.0, second_norm)
        task(1.0, context_grad)
        task(1.0, grad_cout)
        for offset in list(range(1, line)) + [0]:
            task(2.0, cross, offset)
        task(1.0, grad_first)
        task(2.0, first_norm)
        task(1.0, grad_cq)
        task(1.0, self_context)
        task(1.0, key_grad)
        task(1.0, grad_sout)
        for part in range(2):
            task(0.5, grad_ckv, part)
        for number in range(H // 2):
            task(2.5, attend, number)
        for part in range(3):
            task(1.2, grad_qkv, part)
        for side in range(2):
            task(1.5, text_back, side)
        schedule.run()
        for name in ("t", "q", "s", "k", "p"):
            sends[name].wait_send()

    pair_column[...] = jnp.broadcast_to(pair_row[...].astype(jnp.float32), (128, tokens)).T
    place.meet()
    low = jnp.bfloat16
    wide = (tokens, hidden_width)
    rows = (tokens, width)
    shape = lambda ref: pltpu.VMEM(ref.shape, ref.dtype)
    pl.run_scoped(
        feed_forward,
        shape(weights.up),
        shape(weights.down),
        shape(pairs.low_two),
        shape(pairs.hidden_low),
        pltpu.VMEM(wide, low),
        pltpu.VMEM(rows, jnp.float32),
        pltpu.VMEM(rows, low),
        pltpu.VMEM(rows, low),
    )
    pl.run_scoped(
        attentions,
        shape(weights.qkv),
        shape(weights.ckv),
        shape(weights.sout),
        shape(weights.cq),
        shape(weights.cout),
        shape(pairs.context),
        shape(pairs.context),
        shape(pairs.patches),
        pltpu.VMEM((2,) + rows, jnp.float32),
        shape(saved.query),
        shape(saved.key_value),
        shape(saved.cross_attention),
        pltpu.VMEM((H * keys, width), low),
        pltpu.VMEM((H * keys, width), low),
        shape(saved.qkv),
        pltpu.VMEM((2, 2, tokens, tokens), low),
        pltpu.VMEM((2, tokens, tokens), low),
        pltpu.VMEM(rows, low),
        pltpu.VMEM(rows, low),
        pltpu.VMEM(rows, low),
        pltpu.VMEM(rows, low),
    )
    device = place.z * 8 + place.f
    value = small[...]
    narrow, slim = gains_out.shape[1], hidden_out.shape[1]
    turned = pltpu.roll(value, lax.rem(width - device * narrow, width), 1)
    gains_out[...] = turned[:3, :narrow]
    biases_out[...] = turned[3:13, :narrow]
    number = lax.broadcasted_iota(jnp.int32, value.shape, 0)
    picked = jnp.sum(jnp.where(number == 13 + place.z, value, 0.0), axis=0, keepdims=True)
    picked = pltpu.roll(jnp.broadcast_to(picked, (8, width)), lax.rem(width - place.f * slim, width), 1)
    hidden_out[...] = picked[:1, :slim]
    for name in WEIGHTS:
        swaps[name].wait_recv()
        out = getattr(outs, name)
        mine, other = getattr(finals, name)[core], getattr(swapped, name)[...]
        middle = mine.shape[1]
        out[:, :middle] = jnp.where(core == 0, mine, other)
        out[:, middle:] = jnp.where(core == 0, other, mine)
    copies.finish()


def gathered(line, shards):
    return [(2, line, 2, 2, 2 * shard.shape[0], shard.shape[1] // 2) for shard in shards]


def forward_all(line, shards, vectors, text, patches, pair_row, region_row):
    tokens, width = text.shape
    keys, depth = patches.shape
    wide = shards[5].shape[1]
    low, full = jnp.bfloat16, jnp.float32
    rows = (tokens, width)
    kept = [
        ((tokens, 3 * width), low),
        ((H, tokens, tokens), low),
        (rows, low),
        ((line, keys, 2 * width), low),
        ((line, H * keys, tokens // line), low),
        ((3,) + rows, full),
        ((3, tokens, 128), full),
        ((tokens, wide), low),
        (rows, low),
        ((16, width), full),
    ]
    locals_ = [((8, wide), full), (rows, low), (rows, low), (rows, low), (rows, low), ((tokens, wide), low)]
    paired = [rows, (keys, depth), rows, rows, rows, rows, (tokens, wide)]
    shapes = gathered(line, shards)
    out_shape = [jax.ShapeDtypeStruct(shape, low) for shape in shapes]
    out_shape += [jax.ShapeDtypeStruct(*shape) for shape in kept]
    out_shape += [jax.ShapeDtypeStruct((2,) + shape, low) for shape in paired]
    scratch = [pltpu.VMEM(shape, low) for shape in shapes]
    for _ in range(2):
        scratch += [pltpu.VMEM((padded(shard.shape[0]), shard.shape[1] // 2), low) for shard in shards]
    scratch += [pltpu.VMEM(*shape) for shape in kept + locals_]
    scratch += [
        pltpu.VMEM((2, line, 2, 2, 16, 128), low),
        pltpu.VMEM((tokens, 128), full),
        pltpu.VMEM(rows, full),
        pltpu.VMEM((H * keys, width), low),
        pltpu.VMEM((H * keys, width), low),
        pltpu.SemaphoreType.DMA((160,)),
        pltpu.SemaphoreType.DMA((160,)),
        pltpu.SemaphoreType.DMA((96,)),
    ]
    outs = pl.pallas_call(
        functools.partial(forward_kernel, line),
        out_shape=out_shape,
        in_specs=[pl.BlockSpec(memory_space=pltpu.VMEM)] * (len(shards) + 5),
        out_specs=[pl.BlockSpec(memory_space=pl.ANY)] * len(out_shape),
        scratch_shapes=scratch,
        compiler_params=pltpu.CompilerParams(
            collective_id=0, has_side_effects=True, vmem_limit_bytes=62 * 2**20
        ),
    )(*shards, vectors, text, patches, pair_row, region_row)
    count = len(shards)
    return outs[:count], outs[count : count + len(kept)], outs[count + len(kept) :]


def backward_all(line, weights, saved, pairs, cotangent, pair_row, narrow, slim):
    low, full = jnp.bfloat16, jnp.float32
    tokens, width = cotangent.shape
    keys, depth = pairs[1].shape[1:]
    wide = pairs[-1].shape[2]
    sizes = [weight.shape[4:] for weight in weights]
    scratch = []
    for lead in ((line, 2, 2), (line, 2), (line,), (line - 1,)):
        scratch += [pltpu.VMEM(lead + size, low) for size in sizes]
    scratch += [pltpu.VMEM((2, size[0] // 2, size[1]), full) for size in sizes]
    scratch += [pltpu.VMEM((size[0] // 2, size[1]), full) for size in sizes]
    for name, size in zip(WEIGHTS, sizes):
        scratch.append(pltpu.VMEM((keys if name == "ckv" else tokens, size[1]), low))
    scratch += [
        pltpu.VMEM((tokens, width), full),
        pltpu.VMEM((3, tokens, 128), full),
        pltpu.VMEM((16, width), full),
        pltpu.VMEM((24, width), full),
        pltpu.VMEM((2 + line, 24, width), full),
        pltpu.VMEM((line, keys, 2 * width), low),
        pltpu.VMEM((line - 1, keys, 2 * width), low),
        pltpu.VMEM((tokens, 128), full),
        pltpu.VMEM((8, wide), full),
        pltpu.VMEM((keys, 2 * width), low),
        pltpu.SemaphoreType.DMA((160,)),
        pltpu.SemaphoreType.DMA((160,)),
        pltpu.SemaphoreType.DMA((64,)),
    ]
    out_shape = [jax.ShapeDtypeStruct((size[0] // 2, 2 * size[1]), full) for size in sizes]
    out_shape += [
        jax.ShapeDtypeStruct((tokens, width), full),
        jax.ShapeDtypeStruct((keys, depth), full),
        jax.ShapeDtypeStruct((3, narrow), full),
        jax.ShapeDtypeStruct((10, narrow), full),
        jax.ShapeDtypeStruct((1, slim), full),
    ]
    vmem, anywhere = pl.BlockSpec(memory_space=pltpu.VMEM), pl.BlockSpec(memory_space=pl.ANY)
    count = len(weights)
    outs = pl.pallas_call(
        functools.partial(backward_kernel, line),
        out_shape=out_shape,
        in_specs=[anywhere] * (count + len(saved) + len(pairs) + 1) + [vmem],
        out_specs=[vmem] * count + [anywhere] + [vmem] * 4,
        scratch_shapes=scratch,
        compiler_params=pltpu.CompilerParams(
            collective_id=1, has_side_effects=True, vmem_limit_bytes=63 * 2**20
        ),
    )(*weights, *saved, *pairs, cotangent, pair_row)
    return outs[:count], outs[count:]


def fast_body(
    text_rows,
    patches,
    row_pair,
    row_region,
    self_qkv,
    self_out,
    cross_query,
    cross_key_value,
    cross_out,
    ffn_up,
    ffn_down,
    norm_gains,
    biases,
    ffn_bias,
    cotangent,
):
    line = lax.axis_size("dp")
    narrow, slim = norm_gains.shape[1], ffn_bias.shape[0]
    vectors = jnp.concatenate(
        [
            jnp.pad(norm_gains, ((0, 0), (0, 128 - narrow))),
            jnp.pad(biases, ((0, 0), (0, 128 - narrow))),
            jnp.pad(ffn_bias[None], ((0, 2), (0, 128 - slim))),
        ],
        axis=0,
    )
    shards = (self_qkv, cross_key_value, self_out, cross_query, cross_out, ffn_up, ffn_down)
    pair_row = row_pair.reshape(1, -1)
    weights, kept, pairs = forward_all(
        line,
        shards,
        vectors,
        text_rows,
        patches.reshape(-1, patches.shape[2]),
        pair_row,
        row_region.reshape(1, -1),
    )
    joined = kept[8]
    saved = kept[:8] + kept[9:]
    grads, (text_grad, patch_grad, gains, shifts, hidden) = backward_all(
        line, weights, saved, pairs, cotangent, pair_row, narrow, slim
    )
    grad_qkv, grad_ckv, grad_sout, grad_cq, grad_cout, grad_up, grad_down = grads
    return (
        joined,
        text_grad,
        patch_grad.reshape(patches.shape),
        grad_qkv,
        grad_sout,
        grad_cq,
        grad_ckv,
        grad_cout,
        grad_up,
        grad_down,
        gains,
        shifts,
        hidden.reshape(-1),
    )


def body(
    text_rows,
    patches,
    row_pair,
    row_region,
    self_qkv,
    self_out,
    cross_query,
    cross_key_value,
    cross_out,
    ffn_up,
    ffn_down,
    norm_gains,
    biases,
    ffn_bias,
    cotangent,
):
    weight_qkv, weight_sout, weight_cq, weight_ckv, weight_cout, gains_all, bias_all = (
        lax.all_gather(self_qkv, ("dp", "fsdp"), axis=0, tiled=True),
        lax.all_gather(self_out, ("dp", "fsdp"), axis=0, tiled=True),
        lax.all_gather(cross_query, ("dp", "fsdp"), axis=0, tiled=True),
        lax.all_gather(cross_key_value, ("dp", "fsdp"), axis=0, tiled=True),
        lax.all_gather(cross_out, ("dp", "fsdp"), axis=0, tiled=True),
        lax.all_gather(norm_gains, ("dp", "fsdp"), axis=1, tiled=True),
        lax.all_gather(biases, ("dp", "fsdp"), axis=1, tiled=True),
    )
    weight_up, weight_down, bias_up_all = (
        lax.all_gather(ffn_up, ("dp", "fsdp"), axis=0, tiled=True),
        lax.all_gather(ffn_down, ("dp", "fsdp"), axis=0, tiled=True),
        lax.all_gather(ffn_bias, ("dp", "fsdp"), axis=0, tiled=True),
    )
    gains = gains_all.astype(jnp.float32)
    bias_rows = bias_all.astype(jnp.float32)
    bias_hidden = bias_up_all.astype(jnp.float32)
    row_count, model_width = text_rows.shape
    owners = lax.axis_size("dp")
    block_rows = row_count // owners
    valid = (row_pair >= 0)[:, None]
    patch_rows = patches.reshape(-1, patches.shape[2])
    kv_projected = jnp.dot(patch_rows, weight_ckv, preferred_element_type=jnp.float32)
    key_local = kv_projected[:, :model_width].astype(jnp.bfloat16)
    value_local = (kv_projected[:, model_width:] + bias_rows[4]).astype(jnp.bfloat16)
    keys_count = key_local.shape[0]
    kept_self, context_self = self_forward(
        text_rows, row_pair, weight_qkv, bias_rows[0], bias_rows[1]
    )
    branch_self = (
        jnp.dot(context_self, weight_sout, preferred_element_type=jnp.float32) + bias_rows[2]
    )
    first, normed_one, inverse_one = norm_forward(
        text_rows.astype(jnp.float32) + branch_self, gains[0], bias_rows[7]
    )
    first_low = first.astype(jnp.bfloat16)
    queries = (
        jnp.dot(first_low, weight_cq, preferred_element_type=jnp.float32) + bias_rows[3]
    ).astype(jnp.bfloat16)
    region_blocks = row_region.reshape(owners, block_rows)
    arrived, arrived_region = (
        lax.all_to_all(
            queries.reshape(owners, block_rows, model_width),
            "dp",
            split_axis=0,
            concat_axis=0,
            tiled=True,
        ),
        lax.all_to_all(region_blocks, "dp", split_axis=0, concat_axis=0, tiled=True),
    )
    arrived = arrived.reshape(1, owners * block_rows, H, HD)
    arrived_region = arrived_region.reshape(1, owners * block_rows)
    key_view = key_local.reshape(1, keys_count, H, HD)
    value_view = value_local.reshape(1, keys_count, H, HD)
    logsum_cross, context_owner = cross_forward(arrived, key_view, value_view, arrived_region)
    context_cross = lax.all_to_all(
        context_owner.reshape(owners, block_rows, model_width),
        "dp",
        split_axis=0,
        concat_axis=0,
        tiled=True,
    ).reshape(row_count, model_width)
    branch_cross = (
        jnp.dot(context_cross, weight_cout, preferred_element_type=jnp.float32) + bias_rows[5]
    )
    second, normed_two, inverse_two = norm_forward(first + branch_cross, gains[1], bias_rows[8])
    second_low = second.astype(jnp.bfloat16)
    hidden_pre = jnp.dot(second_low, weight_up, preferred_element_type=jnp.float32) + bias_hidden
    hidden_low = gelu_exact(hidden_pre).astype(jnp.bfloat16)
    branch_ffn = jnp.dot(hidden_low, weight_down, preferred_element_type=jnp.float32) + bias_rows[6]
    result, normed_three, inverse_three = norm_forward(second + branch_ffn, gains[2], bias_rows[9])
    joined_text = jnp.where(valid, result, 0.0).astype(jnp.bfloat16)
    upstream = jnp.where(valid, cotangent.astype(jnp.float32), 0.0)
    grad_three, grad_gain_three, grad_shift_three = norm_backward(
        upstream, normed_three, inverse_three, gains[2]
    )
    grad_ffn = grad_three.astype(jnp.bfloat16)
    grad_hidden = times_transpose(grad_ffn, weight_down)
    grad_pre = jax.vjp(gelu_exact, hidden_pre)[1](grad_hidden)[0].astype(jnp.bfloat16)
    ffn_terms = (
        transpose_times(second_low, grad_pre),
        transpose_times(hidden_low, grad_ffn),
        jnp.sum(grad_pre, axis=0, dtype=jnp.float32),
    )
    grad_up, grad_down, grad_up_bias = (
        lax.psum_scatter(ffn_terms[0], ("dp", "fsdp"), scatter_dimension=0, tiled=True),
        lax.psum_scatter(ffn_terms[1], ("dp", "fsdp"), scatter_dimension=0, tiled=True),
        lax.psum_scatter(ffn_terms[2], ("dp", "fsdp"), scatter_dimension=0, tiled=True),
    )
    grad_second = grad_three + times_transpose(grad_pre, weight_up)
    grad_two, grad_gain_two, grad_shift_two = norm_backward(
        grad_second, normed_two, inverse_two, gains[1]
    )
    grad_cross = grad_two.astype(jnp.bfloat16)
    grad_context = times_transpose(grad_cross, weight_cout).astype(jnp.bfloat16)
    grad_arrived = lax.all_to_all(
        grad_context.reshape(owners, block_rows, model_width),
        "dp",
        split_axis=0,
        concat_axis=0,
        tiled=True,
    ).reshape(1, owners * block_rows, H, HD)
    grad_query_owner, grad_key, grad_value = cross_backward(
        arrived, key_view, value_view, arrived_region, logsum_cross, grad_arrived
    )
    grad_queries = lax.all_to_all(
        grad_query_owner.astype(jnp.bfloat16).reshape(owners, block_rows, model_width),
        "dp",
        split_axis=0,
        concat_axis=0,
        tiled=True,
    ).reshape(row_count, model_width)
    grad_key_total = grad_key.reshape(keys_count, model_width)
    grad_value_total = grad_value.reshape(keys_count, model_width)
    grad_kv = jnp.concatenate(
        [grad_key_total.astype(jnp.bfloat16), grad_value_total.astype(jnp.bfloat16)], axis=1
    )
    patch_grad = times_transpose(grad_kv, weight_ckv).reshape(patches.shape)
    grad_ckv = transpose_times(patch_rows, grad_kv)
    grad_cross_value_bias = jnp.sum(grad_kv[:, model_width:], axis=0, dtype=jnp.float32)
    grad_first = grad_two + times_transpose(grad_queries, weight_cq)
    grad_cq = transpose_times(first_low, grad_queries)
    grad_cout = transpose_times(context_cross, grad_cross)
    grad_one, grad_gain_one, grad_shift_one = norm_backward(
        grad_first, normed_one, inverse_one, gains[0]
    )
    grad_self = grad_one.astype(jnp.bfloat16)
    grad_sout = transpose_times(context_self, grad_self)
    grad_context_self = times_transpose(grad_self, weight_sout).astype(jnp.bfloat16)
    grad_projected = self_backward(kept_self, grad_context_self)
    grad_qkv = transpose_times(text_rows, grad_projected)
    text_grad = grad_one + times_transpose(grad_projected, weight_qkv)
    gain_terms = jnp.stack([grad_gain_one, grad_gain_two, grad_gain_three])
    bias_terms = jnp.stack(
        [
            jnp.sum(grad_projected[:, :model_width], axis=0, dtype=jnp.float32),
            jnp.sum(grad_projected[:, 2 * model_width :], axis=0, dtype=jnp.float32),
            jnp.sum(grad_self, axis=0, dtype=jnp.float32),
            jnp.sum(grad_queries, axis=0, dtype=jnp.float32),
            grad_cross_value_bias,
            jnp.sum(grad_cross, axis=0, dtype=jnp.float32),
            jnp.sum(grad_ffn, axis=0, dtype=jnp.float32),
            grad_shift_one,
            grad_shift_two,
            grad_shift_three,
        ]
    )
    attn_terms = (grad_qkv, grad_sout, grad_cq, grad_ckv, grad_cout, gain_terms, bias_terms)
    shard_qkv, shard_sout, shard_cq, shard_ckv, shard_cout, shard_gains, shard_biases = (
        lax.psum_scatter(attn_terms[0], ("dp", "fsdp"), scatter_dimension=0, tiled=True),
        lax.psum_scatter(attn_terms[1], ("dp", "fsdp"), scatter_dimension=0, tiled=True),
        lax.psum_scatter(attn_terms[2], ("dp", "fsdp"), scatter_dimension=0, tiled=True),
        lax.psum_scatter(attn_terms[3], ("dp", "fsdp"), scatter_dimension=0, tiled=True),
        lax.psum_scatter(attn_terms[4], ("dp", "fsdp"), scatter_dimension=0, tiled=True),
        lax.psum_scatter(attn_terms[5], ("dp", "fsdp"), scatter_dimension=1, tiled=True),
        lax.psum_scatter(attn_terms[6], ("dp", "fsdp"), scatter_dimension=1, tiled=True),
    )
    return (
        joined_text,
        text_grad,
        patch_grad,
        shard_qkv,
        shard_sout,
        shard_cq,
        shard_ckv,
        shard_cout,
        grad_up,
        grad_down,
        shard_gains,
        shard_biases,
        grad_up_bias,
    )


def solution(mesh):
    in_specs = (
        P(("dp", "fsdp"), None),
        P(("dp", "fsdp"), None, None),
        P(("dp", "fsdp")),
        P(("dp", "fsdp")),
        P(("dp", "fsdp"), None),
        P(("dp", "fsdp"), None),
        P(("dp", "fsdp"), None),
        P(("dp", "fsdp"), None),
        P(("dp", "fsdp"), None),
        P(("dp", "fsdp"), None),
        P(("dp", "fsdp"), None),
        P(None, ("dp", "fsdp")),
        P(None, ("dp", "fsdp")),
        P(("dp", "fsdp")),
        P(("dp", "fsdp"), None),
    )
    out_specs = (
        P(("dp", "fsdp"), None),
        P(("dp", "fsdp"), None),
        P(("dp", "fsdp"), None, None),
        P(("dp", "fsdp"), None),
        P(("dp", "fsdp"), None),
        P(("dp", "fsdp"), None),
        P(("dp", "fsdp"), None),
        P(("dp", "fsdp"), None),
        P(("dp", "fsdp"), None),
        P(("dp", "fsdp"), None),
        P(None, ("dp", "fsdp")),
        P(None, ("dp", "fsdp")),
        P(("dp", "fsdp")),
    )
    fast = mesh.shape["fsdp"] == 8
    chosen = fast_body if fast else body
    return jax.shard_map(chosen, mesh=mesh, in_specs=in_specs, out_specs=out_specs, check_vma=False)
```

```python
import functools
import math
import types

import jax
import jax.numpy as jnp
from jax import lax
from jax.experimental import pallas as pl
from jax.experimental.pallas import tpu as pltpu
from jax.sharding import PartitionSpec as P

H = 12
HD = 64
PR = 32
BLK = 512


EPSILON = 1e-06
NEGATIVE = -1e30


def times_transpose(left, right):
    return lax.dot_general(
        left, right, (((1,), (1,)), ((), ())), preferred_element_type=jnp.float32
    )


def transpose_times(left, right):
    return lax.dot_general(
        left, right, (((0,), (0,)), ((), ())), preferred_element_type=jnp.float32
    )


def gelu_exact(values):
    return jax.nn.gelu(values, approximate=False)


def norm_forward(summed, gain_row, shift_row):
    center = summed - jnp.mean(summed, axis=-1, keepdims=True)
    inverse = lax.rsqrt(jnp.mean(center * center, axis=-1, keepdims=True) + EPSILON)
    normed = center * inverse
    return (normed * gain_row + shift_row, normed, inverse)


def norm_backward(upstream, normed, inverse, gain_row):
    scaled = upstream * gain_row
    centered = (
        scaled
        - jnp.mean(scaled, axis=-1, keepdims=True)
        - normed * jnp.mean(scaled * normed, axis=-1, keepdims=True)
    )
    return (inverse * centered, jnp.sum(upstream * normed, axis=0), jnp.sum(upstream, axis=0))


def self_scores(query_rows, key_rows, segment):
    scores = jnp.einsum(
        "qhd,khd->hqk", query_rows, key_rows, preferred_element_type=jnp.float32
    ) * (1.0 / math.sqrt(HD))
    same_pair = segment[:, None] == segment[None, :]
    return jnp.where(same_pair[None], scores, NEGATIVE)


def self_window(window):
    query_rows, key_rows, value_rows, segment = window
    scores = self_scores(query_rows, key_rows, segment)
    highest = jnp.max(scores, axis=-1, keepdims=True)
    logsum = highest + jnp.log(jnp.sum(jnp.exp(scores - highest), axis=-1, keepdims=True))
    weights = jnp.exp(scores - logsum).astype(jnp.bfloat16)
    context = jnp.einsum("hqk,khd->qhd", weights, value_rows, preferred_element_type=jnp.float32)
    return (logsum, context.astype(jnp.bfloat16))


def self_window_back(window):
    query_rows, key_rows, value_rows, segment, logsum, grad_rows = window
    probability = jnp.exp(self_scores(query_rows, key_rows, segment) - logsum)
    grad_prob = jnp.einsum(
        "qhd,khd->hqk", grad_rows, value_rows, preferred_element_type=jnp.float32
    )
    grad_score = (
        probability * (grad_prob - jnp.sum(probability * grad_prob, axis=-1, keepdims=True))
    ).astype(jnp.bfloat16)
    scaling = 1.0 / math.sqrt(HD)
    grad_query = (
        jnp.einsum("hqk,khd->qhd", grad_score, key_rows, preferred_element_type=jnp.float32)
        * scaling
    )
    grad_key = (
        jnp.einsum("hqk,qhd->khd", grad_score, query_rows, preferred_element_type=jnp.float32)
        * scaling
    )
    grad_value = jnp.einsum(
        "hqk,qhd->khd",
        probability.astype(jnp.bfloat16),
        grad_rows,
        preferred_element_type=jnp.float32,
    )
    return jnp.concatenate(
        [grad_query.reshape(BLK, -1), grad_key.reshape(BLK, -1), grad_value.reshape(BLK, -1)],
        axis=1,
    ).astype(jnp.bfloat16)


def self_forward(text_rows, segment, weight_qkv, bias_query, bias_value):
    row_count, model_width = text_rows.shape
    blocks = row_count // BLK
    projected = jnp.dot(text_rows, weight_qkv, preferred_element_type=jnp.float32)
    query_rows = (
        (projected[:, :model_width] + bias_query).astype(jnp.bfloat16).reshape(blocks, BLK, H, HD)
    )
    key_rows = (
        projected[:, model_width : 2 * model_width].astype(jnp.bfloat16).reshape(blocks, BLK, H, HD)
    )
    value_rows = (
        (projected[:, 2 * model_width :] + bias_value)
        .astype(jnp.bfloat16)
        .reshape(blocks, BLK, H, HD)
    )
    segment = segment.reshape(blocks, BLK)
    logsum, context = lax.map(self_window, (query_rows, key_rows, value_rows, segment))
    return (
        (query_rows, key_rows, value_rows, segment, logsum),
        context.reshape(row_count, model_width),
    )


def self_backward(kept_self, grad_context):
    query_rows, key_rows, value_rows, segment, logsum = kept_self
    blocks = query_rows.shape[0]
    grad_rows = grad_context.reshape(blocks, BLK, H, HD)
    grad_projected = lax.map(
        self_window_back, (query_rows, key_rows, value_rows, segment, logsum, grad_rows)
    )
    return grad_projected.reshape(blocks * BLK, -1)


def cross_scores(query_rows, key_rows, region_rows):
    scores = jnp.einsum(
        "bkhd,brhd->bhkr", key_rows, query_rows, preferred_element_type=jnp.float32
    ) * (1.0 / math.sqrt(HD))
    key_region = lax.broadcasted_iota(jnp.int32, (key_rows.shape[1], 1), 0) // PR
    same_region = key_region[None] == region_rows[:, None, :]
    return jnp.where(same_region[:, None], scores, NEGATIVE)


def cross_forward(query_rows, key_rows, value_rows, region_rows):
    scores = cross_scores(query_rows, key_rows, region_rows)
    highest = jnp.max(scores, axis=2, keepdims=True)
    logsum = highest + jnp.log(jnp.sum(jnp.exp(scores - highest), axis=2, keepdims=True))
    weights = jnp.exp(scores - logsum).astype(jnp.bfloat16)
    context = jnp.einsum("bhkr,bkhd->brhd", weights, value_rows, preferred_element_type=jnp.float32)
    return (logsum, context.astype(jnp.bfloat16))


def cross_backward(query_rows, key_rows, value_rows, region_rows, logsum, grad_context):
    probability = jnp.exp(cross_scores(query_rows, key_rows, region_rows) - logsum)
    grad_prob = jnp.einsum(
        "bkhd,brhd->bhkr", value_rows, grad_context, preferred_element_type=jnp.float32
    )
    grad_score = (
        probability * (grad_prob - jnp.sum(probability * grad_prob, axis=2, keepdims=True))
    ).astype(jnp.bfloat16)
    scaling = 1.0 / math.sqrt(HD)
    grad_query = (
        jnp.einsum("bhkr,bkhd->brhd", grad_score, key_rows, preferred_element_type=jnp.float32)
        * scaling
    )
    grad_key = (
        jnp.einsum("bhkr,brhd->bkhd", grad_score, query_rows, preferred_element_type=jnp.float32)
        * scaling
    )
    grad_value = jnp.einsum(
        "bhkr,brhd->bkhd",
        probability.astype(jnp.bfloat16),
        grad_context,
        preferred_element_type=jnp.float32,
    )
    return (grad_query, grad_key, grad_value)


MESH = pl.DeviceIdType.MESH
WEIGHTS = ("qkv", "ckv", "sout", "cq", "cout", "up", "down")
CORE_LINK = 400e3


def named(names, refs):
    return types.SimpleNamespace(**dict(zip(names, refs)))


class Place:
    def __init__(self, line):
        self.line = line
        self.z = lax.axis_index("dp")
        self.f = lax.axis_index("fsdp")
        self.core = lax.rem(self.f, 2)
        self.x = lax.rem(self.f // 2, 2)
        self.y = self.f // 4
        self.other = {"c": 1 - self.core, "x": 1 - self.x, "y": 1 - self.y}
        steps = {"c": 1 - 2 * self.core, "x": 2 - 4 * self.x, "y": 4 - 8 * self.y}
        self.neighbours = {axis: self.f + step for axis, step in steps.items()}
        self.onward = [lax.rem(self.z + k, line) for k in range(line)]
        self.backward = [lax.rem(self.z + line - k, line) for k in range(line)]

    def across(self, axis):
        return (self.z, self.neighbours[axis])

    def along(self, offset):
        return (self.onward[offset], self.f)

    def ahead(self, offset):
        return self.onward[offset]

    def behind(self, offset):
        return self.backward[offset]

    def meet(self):
        barrier = pltpu.get_barrier_semaphore()
        partners = [self.across(axis) for axis in "cxy"] + [self.along(k) for k in range(1, self.line)]
        for device in partners:
            pl.semaphore_signal(barrier, inc=1, device_id=device, device_id_type=MESH)
        pl.semaphore_wait(barrier, len(partners))

    def block(self, whole):
        return tuple(slice(None) if axis in whole else getattr(self, axis) for axis in "zyx")


def spot(place):
    return place[0].at[place[1]] if isinstance(place, tuple) else place


class Copy:
    def __init__(self, make):
        self.make = make

    def wait_recv(self):
        self.make(True).wait_recv()

    def wait_send(self):
        self.make(False).wait_send()

    def wait(self):
        self.wait_send()
        self.wait_recv()


class LocalCopy(Copy):
    def wait(self):
        self.make(False).wait()


class Copies:
    def __init__(self, sent, received, local):
        self.sent, self.received, self.local = sent, received, local
        self.count = self.local_count = 0
        self.open = []
        self.writes = []

    def start(self, source, target, device, landing, remember=True):
        number = self.count
        self.count += 1
        copy = Copy(
            lambda arriving: pltpu.make_async_remote_copy(
                src_ref=spot(source),
                dst_ref=spot(landing if arriving else target),
                send_sem=self.sent.at[number],
                recv_sem=self.received.at[number],
                device_id=device,
                device_id_type=MESH,
            )
        )
        copy.make(False).start()
        if remember:
            self.open.append(copy)
        return copy

    def read(self, source, target):
        number = self.local_count
        self.local_count += 1
        copy = LocalCopy(
            lambda arriving: pltpu.make_async_copy(spot(source), spot(target), self.local.at[number])
        )
        copy.make(False).start()
        return copy

    def write(self, source, target):
        self.writes.append(self.read(source, target))

    def finish(self):
        for copy in self.writes:
            copy.wait()
        for copy in self.open:
            copy.wait_send()


class Clock:
    def __init__(self, link, hop, far, slack):
        self.link, self.hop, self.far, self.slack = link, hop, far, slack
        self.now = 0.0
        self.free = dict.fromkeys("czyx", 0.0)

    def send(self, axis, size):
        rate = CORE_LINK if axis == "c" else self.link
        start = max(self.now, self.free[axis])
        self.free[axis] = start + size / rate
        return self.free[axis] + (1.5 if axis == "c" else self.far if axis == "z" else self.hop)


def volume(shape):
    return 2 * math.prod(shape)


class GatherUnit:
    def __init__(self, place, copies, clock, buffer, columns, order):
        self.place, self.copies, self.clock, self.buffer = place, copies, clock, buffer
        self.columns, self.order = columns, order + "c"
        self.held, self.stage, self.arrivals = "", 0, []
        self.size = volume((buffer.shape[4], columns.size))

    def view(self, index, half=None):
        half = self.place.core if half is None else half
        return self.buffer, (half,) + index + (slice(None), self.columns)

    def send(self):
        place = self.place
        axis = self.order[self.stage]
        mine = place.block(self.held)
        blocks = math.prod({"z": place.line, "y": 2, "x": 2}[held] for held in self.held)
        if axis == "z":
            moves = [(place.along(k), (place.behind(k),) + mine[1:], None) for k in range(1, place.line)]
            blocks *= place.line
        elif axis == "c":
            moves = [(place.across(axis), mine, place.other["c"])]
        else:
            level = "zyx".index(axis)
            moves = [(place.across(axis), mine[:level] + (place.other[axis],) + mine[level + 1 :], None)]
        self.arrivals = [
            self.copies.start(self.view(mine), self.view(mine), device, self.view(theirs, half))
            for device, theirs, half in moves
        ]
        self.due = self.clock.send(axis, blocks * self.size)
        self.held += axis
        self.stage += 1

    def step(self):
        for copy in self.arrivals:
            copy.wait_recv()
        self.clock.now = max(self.clock.now, self.due) + 0.1
        if self.stage == len(self.order):
            return True
        if self.stage == 1:
            self.begin()
        self.send()
        return False


class SumUnit:
    def __init__(self, place, copies, clock, total, landings, result, rows, columns, order):
        self.place, self.copies, self.clock, self.total = place, copies, clock, total
        self.landings, self.result, self.order = landings, result, order
        self.area = (rows, columns)
        self.left, self.stage, self.arrivals = "zyx", 0, []
        self.size = volume((rows.size, columns.size))

    def send(self):
        place, area, stage = self.place, self.area, self.stage
        axis = self.order[stage]
        mine = place.block(self.left)
        level = "zyx".index(axis)
        landing = self.landings[stage]
        self.left = self.left.replace(axis, "")
        each = math.prod({"z": place.line, "y": 2, "x": 2}[left] for left in self.left)
        blocks = each
        if axis == "z":
            moves = []
            for offset in range(1, place.line):
                span = pl.ds((offset - 1) * each, each) if each > 1 else offset - 1
                moves.append((place.along(offset), place.ahead(offset), span))
            blocks *= place.line
        else:
            span = pl.ds(0, each) if each > 1 else 0
            if stage == 0:
                span = (pl.ds(0, place.line), pl.ds(0, 2))
            moves = [(place.across(axis), place.other[axis], span)]
        self.arrivals = []
        for device, goal, span in moves:
            there = landing, (span if isinstance(span, tuple) else (span,)) + area
            source = self.total, mine[:level] + (goal,) + mine[level + 1 :] + area
            self.arrivals.append(self.copies.start(source, there, device, there))
        self.due = self.clock.send(axis, blocks * self.size)
        self.axis = axis
        self.stage += 1

    def step(self):
        for copy in self.arrivals:
            copy.wait_recv()
        self.clock.now = max(self.clock.now, self.due) + 0.2
        place, area, landing, line = self.place, self.area, self.landings[self.stage - 1], self.place.line

        def add(index, spots):
            value = self.total[index + area].astype(jnp.float32)
            for one in spots:
                value += landing[one + area].astype(jnp.float32)
            return value

        def store(index, spots):
            self.total[index + area] = add(index, spots).astype(jnp.bfloat16)

        if self.stage == 3:
            count = line - 1 if self.axis == "z" else 1
            value = add((place.z, place.y, place.x), [(k,) for k in range(count)])
            put_halves(self.result, area, value)
            return True
        if self.stage == 1:

            def one(z, carry):
                for other in range(2):
                    store((z, place.y, other) if self.axis == "y" else (z, other, place.x), [(z, other)])
                return carry

            lax.fori_loop(0, line, one, 0)
        elif self.axis == "z":
            for other in range(2):
                index = (place.z, place.y, other) if self.left == "x" else (place.z, other, place.x)
                store(index, [(k * 2 + other,) for k in range(line - 1)])
        else:

            def one(z, carry):
                store((z, place.y, place.x), [(z,)])
                return carry

            lax.fori_loop(0, line, one, 0)
        self.send()
        return False


def put_halves(final, area, value):
    rows, columns = area
    half = final.shape[1]
    done = 0
    while done < rows.size:
        core, at = (rows.start + done) // half, (rows.start + done) % half
        step = min(rows.size - done, half - at)
        final[core, pl.ds(at, step), columns] = value[done : done + step]
        done += step


class Schedule:
    def __init__(self, clock, done):
        self.clock, self.done = clock, done
        self.tasks, self.flying = [], []

    def task(self, cost, function, *arguments, ready=lambda: True):
        self.tasks.append((cost, functools.partial(function, *arguments), ready))

    def launch(self, unit):
        unit.send()
        self.flying.append(unit)

    def run(self, drain=True):
        while self.tasks or (drain and self.flying):
            soonest = min(self.flying, key=lambda unit: unit.due) if self.flying else None
            runnable = self.tasks and self.tasks[0][2]()
            if soonest is not None and (soonest.due + self.clock.slack <= self.clock.now or not runnable):
                if soonest.step():
                    self.flying.remove(soonest)
                    self.done(soonest)
            else:
                cost, function, _ = self.tasks.pop(0)
                function()
                self.clock.now += cost


def padded(rows):
    return -(-rows // 16) * 16


def matrix(value):
    return value.reshape(-1, value.shape[-1])


def dot(left, right, contract=(1, 0)):
    return lax.dot_general(
        left, right, (((contract[0],), (contract[1],)), ((), ())), preferred_element_type=jnp.float32
    )


def whole(buffer):
    return jnp.concatenate([matrix(buffer[0]), matrix(buffer[1])], axis=1)


def column_spans(rows, columns):
    wide = 384 if rows <= 64 else 128
    return [pl.ds(column, wide) for column in range(0, columns, wide)]


def merged_rows(place, mine, other):
    mine, other = mine.astype(jnp.float32), other.astype(jnp.float32)
    first = jnp.where(place.core == 0, mine, other)
    second = jnp.where(place.core == 0, other, mine)
    return jnp.concatenate([first, second], axis=0).astype(jnp.bfloat16)


def column_half(place, values, own):
    half = values.shape[1] // 2
    left, right = values[:, :half].astype(jnp.float32), values[:, half:].astype(jnp.float32)
    return jnp.where((place.core == 0) == own, left, right)

def gelu_pair(values):
    half_square = jnp.exp(values * values * -0.5)
    size = jnp.abs(values)
    t = 1.0 / (1.0 + (0.3275911 * math.sqrt(0.5)) * size)
    series = t * (
        0.5 * 0.254829592
        + t * (-0.5 * 0.284496736 + t * (0.5 * 1.421413741 + t * (-0.5 * 1.453152027 + t * (0.5 * 1.061405429))))
    )
    tail = series * half_square
    phi = jnp.where(values < 0, tail, 1.0 - tail)
    slope = phi + values * half_square * (1.0 / math.sqrt(2.0 * math.pi))
    return values * phi, slope


def spread_vectors(vectors_all, rows_out, hidden_out, narrow, wide, line):
    lanes = lax.broadcasted_iota(jnp.int32, (16, 128), 1)
    sums = {id(rows_out): {}, id(hidden_out): {}}

    def place(target, values, start, size):
        found = sums[id(target)]
        tile, shift = start // 128, start % 128
        rolled = pltpu.roll(values, shift, 1) if shift else values
        lane = lanes[: values.shape[0]]
        first = jnp.where((lane >= shift) & (lane < shift + size), rolled, 0.0)
        found[tile] = found[tile] + first if tile in found else first
        if shift + size > 128:
            second = jnp.where(lane < shift + size - 128, rolled, 0.0)
            tile += 1
            found[tile] = found[tile] + second if tile in found else second

    for z in range(line):
        for y in range(2):
            for x in range(2):
                for core in range(2):
                    device = ((z * 2 + y) * 2 + x) * 2 + core
                    values = vectors_all[core, z, y, x].astype(jnp.float32)
                    place(rows_out, values, device * narrow, narrow)
                    place(hidden_out, values[8:], device * wide, wide)
    for target in (rows_out, hidden_out):
        for tile, value in sums[id(target)].items():
            target[:, pl.ds(tile * 128, 128)] = value

KEPT = ("qkv", "attention", "query", "key_value", "cross_attention", "normed", "inverse", "slope", "joined", "rows")
PAIRS = ("text", "patches", "context", "low_one", "context_cross", "low_two", "hidden_low")
LOCAL = ("hidden", "context", "low_one", "context_cross", "low_two", "hidden_low")


def forward_kernel(line, *refs):
    refs = list(refs)
    take = lambda names: named(names, [refs.pop(0) for _ in names])
    shards = take(WEIGHTS)
    vectors, text, patches, pair_row, region_row = [refs.pop(0) for _ in range(5)]
    outs, kept_out, pairs = take(WEIGHTS), take(KEPT), take(PAIRS)
    buffers, outgoing, incoming = take(WEIGHTS), take(WEIGHTS), take(WEIGHTS)
    kept = named(KEPT + LOCAL, [refs.pop(0) for _ in KEPT + LOCAL])
    vectors_all, pair_column, work, keys_all, values_all, sent, received, local = refs
    place = Place(line)
    copies = Copies(sent, received, local)
    clock = Clock(55e3, 2.0, 4.5, 0.0)
    tokens, width = text.shape
    rows_all, hidden_all = kept.rows, kept.hidden
    block = tokens // line
    narrow = shards.qkv.shape[0]
    keys = patches.shape[0]
    for name in WEIGHTS:
        shard, target = getattr(shards, name), getattr(outgoing, name)
        away = column_half(place, shard[...], False)
        padding = target.shape[0] - shard.shape[0]
        if padding:
            away = jnp.concatenate([away, jnp.zeros((padding, away.shape[1]), jnp.float32)], axis=0)
        target[...] = away.astype(jnp.bfloat16)
    vectors_all[place.core, place.z, place.y, place.x] = vectors[...]
    place.meet()
    swaps = {}
    for name in WEIGHTS:
        there = getattr(incoming, name)
        swaps[name] = copies.start(getattr(outgoing, name), there, place.across("c"), there)
    pair_column[...] = jnp.broadcast_to(pair_row[...].astype(jnp.float32), (128, tokens)).T
    arrivals = []

    def merge(name):
        swaps[name].wait_recv()
        shard = getattr(shards, name)
        mine = column_half(place, shard[...], True)
        other = getattr(incoming, name)[...][: shard.shape[0]]
        getattr(buffers, name)[place.core, place.z, place.y, place.x] = merged_rows(place, mine, other)

    def keep(source, target):
        copies.write(source, target)

    def pair(source, target, *columns):
        there = target.at[(place.core,) + columns]
        copies.write(source, there)
        arrivals.append(
            copies.start(source, there, place.across("c"), target.at[(1 - place.core,) + columns])
        )

    def row(number):
        return rows_all[pl.ds(number, 1), :]

    qkv, context, low_one, query, context_cross = (
        kept.qkv, kept.context, kept.low_one, kept.query, kept.context_cross
    )
    hidden, slope, low_two = kept.hidden_low, kept.slope, kept.low_two
    attention, cross_attention = kept.attention, kept.cross_attention
    key_value = kept.key_value

    def project_qkv(part):
        def one(half, carry):
            size = 384
            column = pl.multiple_of(half * (3 * size) + part * size, 128)
            value = dot(text[...], matrix(buffers.qkv[half, :, :, :, :, pl.ds(part * size, size)]))
            group = (half * 3 + part) // 2
            shift = pl.multiple_of(lax.rem(half * 3 + part, 2) * size, 128)
            biased = jnp.where(
                group == 0,
                rows_all[pl.ds(3, 1), pl.ds(shift, size)],
                jnp.where(group == 1, 0.0, rows_all[pl.ds(4, 1), pl.ds(shift, size)]),
            )
            qkv[:, pl.ds(column, size)] = (value + biased).astype(jnp.bfloat16)
            return carry

        lax.fori_loop(0, 2, one, 0)

    strip = 128

    def attend(pair):
        lane = lax.broadcasted_iota(jnp.int32, (strip, 128), 1)
        columns = pl.ds(pair * 128, 128)

        def one(number, carry):
            rows = pl.ds(pl.multiple_of(number * strip, strip), strip)
            two = qkv[rows, columns].astype(jnp.float32) * (1.0 / math.sqrt(HD))
            key_rows = qkv[:, pl.ds(width + pair * 128, 128)]
            value_rows = qkv[:, pl.ds(2 * width + pair * 128, 128)]
            same = jnp.concatenate([pair_column[rows, :]] * (tokens // 128), axis=1) == pair_row[...].astype(
                jnp.float32
            )
            result = None
            for head in range(2):
                own = (lane < HD) if head == 0 else (lane >= HD)
                scores = dot(jnp.where(own, two, 0.0).astype(jnp.bfloat16), key_rows, (1, 1))
                scores = jnp.where(same, scores, NEGATIVE)
                scores = jnp.exp(scores - jnp.max(scores, axis=1, keepdims=True))
                scores = scores * (1.0 / jnp.sum(scores, axis=1, keepdims=True))
                low = scores.astype(jnp.bfloat16)
                attention[pair * 2 + head, rows, :] = low
                value = dot(low, value_rows)
                result = value if head == 0 else jnp.where(own, value, result)
            context[rows, columns] = result.astype(jnp.bfloat16)
            return carry

        lax.fori_loop(0, tokens // strip, one, 0)
        keep(attention.at[pl.ds(2 * pair, 2)], kept_out.attention.at[pl.ds(2 * pair, 2)])

    def normalize(number, summed, low):
        normed, inverse = kept.normed, kept.inverse
        gain, shift = row(number), row(10 + number)
        step = 64

        def one(index, carry):
            rows = pl.ds(pl.multiple_of(index * step, step), step)
            value = work[rows, :] + summed(rows)
            center = value - jnp.mean(value, axis=1, keepdims=True)
            scale = lax.rsqrt(jnp.mean(center * center, axis=1, keepdims=True) + EPSILON)
            value = center * scale
            normed[number, rows, :] = value
            inverse[number, rows, :] = jnp.broadcast_to(scale, (step, 128))
            low(rows, value * gain + shift)
            return carry

        lax.fori_loop(0, tokens // step, one, 0)
        keep(normed.at[number], kept_out.normed.at[number])
        keep(inverse.at[number], kept_out.inverse.at[number])

    def self_out():
        work[...] = dot(context[...], whole(buffers.sout))

        def low(rows, value):
            low_one[rows, :] = value.astype(jnp.bfloat16)

        normalize(0, lambda rows: text[rows, :].astype(jnp.float32) + row(5), low)
        pair(context, pairs.context)
        pair(low_one, pairs.low_one)

    def project_patches(part):
        size = 384
        value = dot(patches[...], matrix(buffers.ckv[0, :, :, :, :, pl.ds(part * size, size)]))
        key_value[place.z, :, pl.ds(part * size, size)] = value.astype(jnp.bfloat16)
        value = dot(patches[...], matrix(buffers.ckv[1, :, :, :, :, pl.ds(part * size, size)]))
        value += rows_all[pl.ds(7, 1), pl.ds(part * size, size)]
        key_value[place.z, :, pl.ds(width + part * size, size)] = value.astype(jnp.bfloat16)

    shared = []

    def share_keys():
        for offset in range(1, line):
            origin = place.behind(offset)
            shared.append(
                copies.start(
                    key_value.at[place.z], key_value.at[place.z], place.along(offset), key_value.at[origin]
                )
            )

    def project_query():
        work[...] = dot(low_one[...], whole(buffers.cq))
        query[...] = (work[...] + row(6)).astype(jnp.bfloat16)
        keep(query, kept_out.query)

    def cross(owner):
        if owner == 0:
            for copy in shared:
                copy.wait_recv()
            keep(key_value, kept_out.key_value)
        lane = lax.broadcasted_iota(jnp.int32, (keys, width), 1) // HD
        for head in range(H):
            rows = pl.ds(head * keys, keys)
            keys_all[rows, :] = jnp.where(
                lane == head, key_value[owner, :, pl.ds(0, width)].astype(jnp.float32), 0.0
            ).astype(jnp.bfloat16)
            values_all[rows, :] = jnp.where(
                lane == head, key_value[owner, :, pl.ds(width, width)].astype(jnp.float32), 0.0
            ).astype(jnp.bfloat16)
        rows = pl.ds(owner * block, block)
        scores = dot(keys_all[...], query[rows, :], (1, 1)) * (1.0 / math.sqrt(HD))
        region = lax.broadcasted_iota(jnp.int32, (keys, block), 0) // PR
        same = region == region_row[:, rows]
        scores = jnp.where(same[None], scores.reshape(H, keys, block), NEGATIVE)
        scores = jnp.exp(scores - jnp.max(scores, axis=1, keepdims=True))
        scores = scores * (1.0 / jnp.sum(scores, axis=1, keepdims=True))
        scores = scores.reshape(H * keys, block).astype(jnp.bfloat16)
        cross_attention[owner] = scores
        context_cross[rows, :] = dot(scores, values_all[...], (0, 0)).astype(jnp.bfloat16)
        if owner == line - 1:
            keep(cross_attention, kept_out.cross_attention)
            pair(context_cross, pairs.context_cross)

    def cross_out():
        work[...] = dot(context_cross[...], whole(buffers.cout))
        first_gain, first_shift = row(0), row(10)

        def low(rows, value):
            low_two[rows, :] = value.astype(jnp.bfloat16)

        normalize(1, lambda rows: kept.normed[0, rows, :] * first_gain + first_shift + row(8), low)
        pair(low_two, pairs.low_two)

    def expand(part):
        size = 384
        half_width = buffers.up.shape[5]

        def one(half, carry):
            column = pl.multiple_of(half * half_width + part * size, 128)
            columns = pl.ds(column, size)
            value = dot(low_two[...], matrix(buffers.up[half, :, :, :, :, pl.ds(part * size, size)]))
            value, grad = gelu_pair(value + hidden_all[pl.ds(5, 1), columns])
            hidden[:, columns] = value.astype(jnp.bfloat16)
            slope[:, columns] = grad.astype(jnp.bfloat16)
            return carry

        lax.fori_loop(0, 2, one, 0)
        for half in range(2):
            columns = pl.ds(half * half_width + part * size, size)
            pair(hidden.at[:, columns], pairs.hidden_low, slice(None), columns)
            keep(slope.at[:, columns], kept_out.slope.at[:, columns])

    def contract(part):
        size = 128
        buffer = buffers.down
        columns = pl.ds(part * size, size)
        both = jnp.concatenate(
            [matrix(buffer[0, :, :, :, :, columns]), matrix(buffer[1, :, :, :, :, columns])], axis=1
        )
        value = dot(hidden[...], both)
        work[:, pl.ds(part * size, size)] = value[:, :size]
        work[:, pl.ds(width // 2 + part * size, size)] = value[:, size:]

    def finish():
        gain, shift = row(1), row(11)

        def low(rows, value):
            valid = jnp.concatenate([pair_column[rows, :]] * (width // 128), axis=1) >= 0
            kept.joined[rows, :] = jnp.where(valid, value, 0.0).astype(jnp.bfloat16)

        normalize(2, lambda rows: kept.normed[1, rows, :] * gain + shift + row(9), low)
        keep(kept.joined, kept_out.joined)

    present, counts = {}, {}
    waiting = []
    merged = set()

    def done(unit):
        present[unit.name] = present.get(unit.name, 0) + 1
        name = unit.name
        if present[name] == counts.get(name):
            keep(getattr(buffers, name), getattr(outs, name))

    schedule = Schedule(clock, done)

    def begin():
        if waiting:
            unit = waiting.pop(0)
            if unit.name and unit.name not in merged:
                merge(unit.name)
                merged.add(unit.name)
            schedule.launch(unit)

    def unit_of(buffer, name, columns):
        order = ("zyx", "zxy")[len(waiting) % 2]
        unit = GatherUnit(place, copies, clock, buffer, columns, order)
        unit.name, unit.begin = name, begin
        waiting.append(unit)

    unit_of(vectors_all, "", pl.ds(0, 128))
    for name in WEIGHTS:
        buffer = getattr(buffers, name)
        spans = column_spans(*buffer.shape[4:])
        counts[name] = len(spans)
        for columns in spans:
            unit_of(buffer, name, columns)

    def task(name, count, cost, function, *arguments):
        schedule.task(cost, function, *arguments, ready=lambda: present.get(name, 0) >= count)

    def spread():
        spread_vectors(vectors_all, rows_all, hidden_all, narrow, shards.down.shape[0], line)
        keep(rows_all, kept_out.rows)

    pair(text, pairs.text)
    pair(patches, pairs.patches)
    task("", 1, 1.0, spread)
    for part in range(3):
        task("qkv", part + 1, 1.5, project_qkv, part)
    task("", 1, 0.0, keep, qkv, kept_out.qkv)
    for number in range(H // 2):
        task("", 1, 1.8, attend, number)
        if number == 3:
            for part in range(2):
                task("ckv", part + 1, 0.5, project_patches, part)
            task("", 1, 0.1, share_keys)
    task("sout", 1, 2.0, self_out)
    task("cq", 1, 1.0, project_query)
    for owner in range(line):
        task("", 1, 1.5, cross, owner)
    task("cout", 1, 2.0, cross_out)
    for part in range(4):
        task("up", part + 1, 3.0, expand, part)
    for part in range(3):
        task("down", part + 1, 1.5, contract, part)
    task("", 1, 1.5, finish)
    for _ in range(3):
        begin()
    schedule.run()
    for copy in arrivals:
        copy.wait_recv()
    copies.finish()

SAVED = ("qkv", "attention", "query", "key_value", "cross_attention", "normed", "inverse", "slope", "rows")
ORDERS = ("yxz", "xyz")


class VectorUnit:
    def __init__(self, place, copies, clock, total, landings):
        self.place, self.copies, self.clock = place, copies, clock
        self.total, self.landings = total, landings
        self.stage = 0

    def send(self):
        place, stage = self.place, self.stage
        if stage < 3:
            devices = [place.across("cxy"[stage])]
        else:
            devices = [place.along(offset) for offset in range(1, place.line)]
        self.arrivals = []
        for number, device in enumerate(devices):
            there = self.landings, (stage + number,)
            self.arrivals.append(self.copies.start(self.total, there, device, there, False))
        self.due = self.clock.now + 3.0
        self.stage += 1

    def step(self):
        for copy in self.arrivals:
            copy.wait()
        value = self.total[...]
        for number in range(len(self.arrivals)):
            value += self.landings[self.stage - 1 + number]
        self.total[...] = value
        self.clock.now = max(self.clock.now, self.due) + 0.1
        if self.stage == 4:
            return True
        self.send()
        return False


def backward_kernel(line, *refs):
    refs = list(refs)
    take = lambda names: named(names, [refs.pop(0) for _ in names])
    pop = lambda count: [refs.pop(0) for _ in range(count)]
    weights, saved, pairs = take(WEIGHTS), take(SAVED), take(PAIRS)
    cotangent, pair_row = pop(2)
    outs = take(WEIGHTS)
    text_grad, patch_grad, gains_out, biases_out, hidden_out = pop(5)
    totals, first, second, third, finals, swapped, landed = (take(WEIGHTS) for _ in range(7))
    work, inverse, rows_all, small, small_landed, key_parts, key_landed, pair_column, hidden_sum = pop(9)
    grad_kv, sent, received, local = pop(4)
    place = Place(line)
    copies = Copies(sent, received, local)
    clock = Clock(60e3, 2.5, 12.0, 3.0)
    core = place.core
    tokens, width = work.shape
    hidden_width = hidden_sum.shape[1]
    block = tokens // line
    keys = grad_kv.shape[0]
    scaling = 1.0 / math.sqrt(HD)
    remaining = {}
    swaps = {}

    def done(unit):
        if unit is vectors:
            return
        remaining[unit.name] -= 1
        if not remaining[unit.name]:
            final, there = getattr(finals, unit.name), getattr(swapped, unit.name)
            swaps[unit.name] = copies.start((final, (place.other["c"],)), there, place.across("c"), there)

    schedule = Schedule(clock, done)
    vectors = VectorUnit(place, copies, clock, small, small_landed)

    def launch(name, rows, columns, count):
        remaining.setdefault(name, count)
        landings = [getattr(group, name) for group in (first, second, third)]
        order = ORDERS[launch.number % len(ORDERS)]
        launch.number += 1
        unit = SumUnit(
            place, copies, clock, getattr(totals, name), landings, getattr(finals, name), rows, columns, order
        )
        unit.name = name
        schedule.launch(unit)

    launch.number = 0

    def task(cost, function, *arguments):
        schedule.task(cost, function, *arguments)

    def half(size, other=False, offset=0, part=None):
        which = 1 - core if other else core
        return pl.ds(pl.multiple_of(which * size + offset, 128), size if part is None else part)

    def hand_over(source, target, columns=None):
        size = target.shape[1]
        there = target if columns is None else (target, (slice(None), columns))
        away = half(size, True) if columns is None else half(size, True, columns.start, columns.size)
        return copies.start((source, (slice(None), away)), there, place.across("c"), there, False)

    def norm_back(number, bias_number, normed, upstream, low):
        gain = rows_all[pl.ds(number, 1), :]
        step = 64

        def one(index, carry):
            rows = pl.ds(pl.multiple_of(index * step, step), step)
            grad, normal = upstream(rows), normed[rows, :]
            scaled = grad * gain
            center = scaled - jnp.mean(scaled, axis=1, keepdims=True)
            center -= normal * jnp.mean(scaled * normal, axis=1, keepdims=True)
            value = inverse[number, rows, :][:, :1] * center
            work[rows, :] = value
            rounded = value.astype(jnp.bfloat16)
            low[rows, :] = rounded
            sums = (grad * normal, grad, rounded.astype(jnp.float32))
            return tuple(old + jnp.sum(new, axis=0, keepdims=True) for old, new in zip(carry, sums))

        zero = jnp.zeros((1, width), jnp.float32)
        gain_sum, shift_sum, bias_sum = lax.fori_loop(0, tokens // step, one, (zero, zero, zero))
        small[pl.ds(number, 1), :] = gain_sum
        small[pl.ds(10 + number, 1), :] = shift_sum
        small[pl.ds(bias_number, 1), :] = bias_sum

    def weight_grad(name, inputs, low, landing, columns, span=None):
        size = landing.shape[1]
        own = half(size, False, columns.start, columns.size)
        span = slice(None) if span is None else span
        value = dot(inputs[core, :, span], low[:, own], (0, 0))
        value += dot(inputs[1 - core, :, span], landing[:, columns], (0, 0))
        return value.astype(jnp.bfloat16)

    def spread_columns(name, inputs, low, columns, count):
        total = getattr(totals, name)
        value = weight_grad(name, inputs, low, getattr(landed, name), columns)
        total[:, :, :, :, columns] = value.reshape(total.shape[:4] + (columns.size,))
        launch(name, pl.ds(0, total.shape[3]), columns, count)

    def feed_forward(up, down, inputs_up, inputs_down, slope, normed, grad_low, cotangent_here):
        reads = [
            copies.read(source, target)
            for source, target in (
                (cotangent, cotangent_here),
                (saved.normed.at[2], normed),
                (saved.inverse, inverse),
                (saved.rows, rows_all),
                (weights.down, down),
                (saved.slope, slope),
                (pairs.hidden_low, inputs_down),
                (pairs.low_two, inputs_up),
                (weights.up, up),
            )
        ]
        sends = []

        def third_norm():
            for copy in reads[:4]:
                copy.wait()
            small[...] = jnp.zeros_like(small)

            def upstream(rows):
                valid = jnp.concatenate([pair_column[rows, :]] * (width // 128), axis=1) >= 0
                return jnp.where(valid, cotangent_here[rows, :].astype(jnp.float32), 0.0)

            norm_back(2, 9, normed, upstream, grad_low)
            sends.append(hand_over(grad_low, landed.down))

        size = 384
        half_width = hidden_width // 2

        def expand(other):
            if other:
                for copy in reads[4:6]:
                    copy.wait()

            def one(part, carry):
                column = (1 - core if other else core) * half_width + part * size
                number = column // size
                both = jnp.concatenate(
                    [matrix(down[side, number // 2, lax.rem(number, 2)]) for side in range(2)], axis=1
                )
                columns = pl.ds(pl.multiple_of(column, 128), size)
                value = dot(grad_low[...], both, (1, 1)) * slope[:, columns].astype(jnp.float32)
                value = value.astype(jnp.bfloat16)
                slope[:, columns] = value
                hidden_sum[pl.ds(0, 1), columns] = jnp.sum(value.astype(jnp.float32), axis=0, keepdims=True)
                return carry

            lax.fori_loop(0, half_width // size, one, 0)
            if other:
                sends.append(hand_over(slope, landed.up))

        def grad_down():
            reads[6].wait()
            sends[0].wait_recv()
            total = totals.down

            def one(z, carry):
                span = pl.ds(pl.multiple_of(z * (hidden_width // line), 128), hidden_width // line)
                value = weight_grad("down", inputs_down, grad_low, landed.down, pl.ds(0, width // 2), span)
                total[z] = value.reshape(total.shape[1:])
                return carry

            lax.fori_loop(0, line, one, 0)
            for row in range(0, total.shape[3], 48):
                launch("down", pl.ds(row, 48), pl.ds(0, width // 2), total.shape[3] // 48)

        def grad_up(part):
            if part == 0:
                reads[7].wait()
                sends[1].wait_recv()
                for k in range(4):
                    small[pl.ds(13 + k, 1), :] = hidden_sum[pl.ds(0, 1), pl.ds(k * width, width)]
            spread_columns("up", inputs_up, slope, pl.ds(part * size, size), half_width // size)

        def grad_second():
            reads[8].wait()
            for side in range(2):
                work[...] += dot(slope[:, pl.ds(side * half_width, half_width)], matrix(up[side]), (1, 1))

        task(2.0, third_norm)
        task(2.0, expand, True)
        task(4.0, grad_down)
        task(2.0, expand, False)
        for part in range(half_width // size):
            task(1.2, grad_up, part)
        task(3.0, grad_second)
        schedule.run(False)
        for copy in sends:
            copy.wait_send()

    def attentions(qkv_w, ckv_w, sout_w, cq_w, cout_w, left_one, left_two, patch_pair, normed, query, key_value,
                   cross_attention, keys_all, values_all, qkv, attention, scores_low, grad_two_low, grad_query,
                   grad_one_low, grad_context):
        order = (
            (saved.normed.at[1], normed.at[1]),
            (weights.cout, cout_w),
            (pairs.context_cross, left_one),
            (saved.key_value, key_value),
            (saved.cross_attention, cross_attention),
            (saved.query, query),
            (weights.cq, cq_w),
            (saved.normed.at[0], normed.at[0]),
            (pairs.low_one, left_two),
            (weights.sout, sout_w),
            (weights.ckv, ckv_w),
            (pairs.patches, patch_pair),
            (saved.qkv, qkv),
            (saved.attention.at[pl.ds(0, 2)], attention.at[0]),
            (weights.qkv, qkv_w),
        )
        reads = [copies.read(source, target) for source, target in order]
        waited = set()
        later = {}
        sends = {}
        size = 384
        third_part = pl.ds(0, width // 2)

        def need(*numbers):
            for number in numbers:
                if number not in waited:
                    reads[number].wait()
                    waited.add(number)

        def second_norm():
            need(0)
            norm_back(1, 8, normed.at[1], lambda rows: work[rows, :], grad_two_low)
            sends["t"] = hand_over(grad_two_low, landed.cout)

        def context_grad():
            need(1)
            grad_context[...] = dot(grad_two_low[...], whole(cout_w), (1, 1)).astype(jnp.bfloat16)

        def cross(offset):
            need(3, 4, 5)
            owner = place.ahead(offset)
            lane = lax.broadcasted_iota(jnp.int32, (keys, width), 1) // HD
            key_rows = key_value[owner, :, pl.ds(0, width)].astype(jnp.float32)
            value_rows = key_value[owner, :, pl.ds(width, width)].astype(jnp.float32)
            for head in range(H):
                rows = pl.ds(head * keys, keys)
                keys_all[rows, :] = jnp.where(lane == head, key_rows, 0.0).astype(jnp.bfloat16)
                values_all[rows, :] = jnp.where(lane == head, value_rows, 0.0).astype(jnp.bfloat16)
            rows = pl.ds(pl.multiple_of(owner * block, block), block)
            probability = cross_attention[owner].astype(jnp.float32).reshape(H, keys, block)
            grad = dot(values_all[...], grad_context[rows, :], (1, 1)).reshape(H, keys, block)
            grad = probability * (grad - jnp.sum(probability * grad, axis=1, keepdims=True))
            grad = grad.reshape(H * keys, block).astype(jnp.bfloat16)
            grad_query[rows, :] = (dot(grad, keys_all[...], (0, 0)) * scaling).astype(jnp.bfloat16)
            lane = lax.broadcasted_iota(jnp.int32, (keys, 128), 1)
            for pair in range(H // 2):
                columns = pl.ds(pair * 128, 128)
                heads = slice(pair * 2 * keys, (pair + 1) * 2 * keys)
                value = dot(grad[heads], query[rows, columns]) * scaling
                key_parts[offset, :, columns] = jnp.where(lane < HD, value[:keys], value[keys:]).astype(
                    jnp.bfloat16
                )
                value = dot(cross_attention[owner, pl.ds(heads.start, 2 * keys), :], grad_context[rows, columns])
                key_parts[offset, :, pl.ds(width + pair * 128, 128)] = jnp.where(
                    lane < HD, value[:keys], value[keys:]
                ).astype(jnp.bfloat16)
            if offset:
                there = key_landed, (offset - 1,)
                sends[offset] = copies.start((key_parts, (offset,)), there, place.along(offset), there)
            if offset == 0:
                sends["q"] = hand_over(grad_query, landed.cq)

        def grad_cout():
            need(2)
            sends["t"].wait_recv()
            spread_columns("cout", left_one, grad_two_low, third_part, 1)
            later["context"] = copies.read(pairs.context, left_one)

        def grad_first():
            need(6)
            work[...] += dot(grad_query[...], whole(cq_w), (1, 1))
            small[pl.ds(6, 1), :] = jnp.sum(grad_query[...].astype(jnp.float32), axis=0, keepdims=True)

        def first_norm():
            need(7)
            norm_back(0, 5, normed.at[0], lambda rows: work[rows, :], grad_one_low)
            sends["s"] = hand_over(grad_one_low, landed.sout)

        def grad_cq():
            need(8)
            sends["q"].wait_recv()
            spread_columns("cq", left_two, grad_query, third_part, 1)
            later["text"] = copies.read(pairs.text, left_two)

        def self_context():
            need(9)
            grad_context[...] = dot(grad_one_low[...], whole(sout_w), (1, 1)).astype(jnp.bfloat16)

        def grad_sout():
            later["context"].wait()
            sends["s"].wait_recv()
            spread_columns("sout", left_one, grad_one_low, third_part, 1)

        def key_grad():
            value = key_parts[0].astype(jnp.float32)
            for offset in range(1, line):
                sends[offset].wait_recv()
                value += key_landed[offset - 1].astype(jnp.float32)
            value = value.astype(jnp.bfloat16)
            grad_kv[...] = value
            sends["k"] = hand_over(grad_kv, landed.ckv)
            small[pl.ds(7, 1), :] = jnp.sum(value[:, width:].astype(jnp.float32), axis=0, keepdims=True)
            need(10)
            patch_grad[...] = dot(grad_kv[...], whole(ckv_w), (1, 1))

        def grad_ckv(part):
            if part == 0:
                need(11)
                sends["k"].wait_recv()
            spread_columns("ckv", patch_pair, grad_kv, pl.ds(part * size, size), 2)

        strip = 128

        def attend(pair):
            slot = pair % 2
            if pair == 0:
                need(12, 13)
            else:
                later[pair].wait()
            if pair + 1 < H // 2:
                later[pair + 1] = copies.read(
                    saved.attention.at[pl.ds(2 * pair + 2, 2)], attention.at[1 - slot]
                )
            columns, key_columns = pl.ds(pair * 128, 128), pl.ds(width + pair * 128, 128)
            value_columns = pl.ds(2 * width + pair * 128, 128)

            def own(value, head):
                lane = lax.broadcasted_iota(jnp.int32, value.shape, 1)
                return jnp.where((lane < HD) == (head == 0), value.astype(jnp.float32), 0.0).astype(jnp.bfloat16)

            def one(number, carry):
                rows = pl.ds(pl.multiple_of(number * strip, strip), strip)
                for head in range(2):
                    grad = dot(own(grad_context[rows, columns], head), qkv[:, value_columns], (1, 1))
                    probability = attention[slot, head, rows, :].astype(jnp.float32)
                    grad = probability * (grad - jnp.sum(probability * grad, axis=1, keepdims=True))
                    scores_low[head, rows, :] = grad.astype(jnp.bfloat16)
                return carry

            lax.fori_loop(0, tokens // strip, one, 0)
            query_grad = key_grad = value_grad = 0.0
            for head in range(2):
                query_grad += dot(scores_low[head], own(qkv[:, key_columns], head))
                key_grad += dot(scores_low[head], own(qkv[:, columns], head), (0, 0))
                value_grad += dot(attention[slot, head], own(grad_context[:, columns], head), (0, 0))
            query_grad = (query_grad * scaling).astype(jnp.bfloat16)
            value_grad = value_grad.astype(jnp.bfloat16)
            qkv[:, columns] = query_grad
            qkv[:, key_columns] = (key_grad * scaling).astype(jnp.bfloat16)
            qkv[:, value_columns] = value_grad
            small[pl.ds(3, 1), columns] = jnp.sum(query_grad.astype(jnp.float32), axis=0, keepdims=True)
            small[pl.ds(4, 1), columns] = jnp.sum(value_grad.astype(jnp.float32), axis=0, keepdims=True)
            if pair + 1 == H // 2:
                sends["p"] = hand_over(qkv, landed.qkv)
                schedule.launch(vectors)

        def grad_qkv(part):
            if part == 0:
                later["text"].wait()
                sends["p"].wait_recv()
            spread_columns("qkv", left_two, qkv, pl.ds(part * size, size), 3)

        def text_back(side):
            need(14)
            size = 3 * width // 2
            work[...] += dot(qkv[:, pl.ds(side * size, size)], matrix(qkv_w[side]), (1, 1))
            if side == 1:
                copies.write(work, text_grad)

        task(2.0, second_norm)
        task(1.0, context_grad)
        task(1.0, grad_cout)
        for offset in list(range(1, line)) + [0]:
            task(2.0, cross, offset)
        task(1.0, grad_first)
        task(2.0, first_norm)
        task(1.0, grad_cq)
        task(1.0, self_context)
        task(1.0, key_grad)
        task(1.0, grad_sout)
        for part in range(2):
            task(0.5, grad_ckv, part)
        for number in range(H // 2):
            task(2.5, attend, number)
        for part in range(3):
            task(1.2, grad_qkv, part)
        for side in range(2):
            task(1.5, text_back, side)
        schedule.run()
        for name in ("t", "q", "s", "k", "p"):
            sends[name].wait_send()

    pair_column[...] = jnp.broadcast_to(pair_row[...].astype(jnp.float32), (128, tokens)).T
    place.meet()
    low = jnp.bfloat16
    wide = (tokens, hidden_width)
    rows = (tokens, width)
    shape = lambda ref: pltpu.VMEM(ref.shape, ref.dtype)
    pl.run_scoped(
        feed_forward,
        shape(weights.up),
        shape(weights.down),
        shape(pairs.low_two),
        shape(pairs.hidden_low),
        pltpu.VMEM(wide, low),
        pltpu.VMEM(rows, jnp.float32),
        pltpu.VMEM(rows, low),
        pltpu.VMEM(rows, low),
    )
    pl.run_scoped(
        attentions,
        shape(weights.qkv),
        shape(weights.ckv),
        shape(weights.sout),
        shape(weights.cq),
        shape(weights.cout),
        shape(pairs.context),
        shape(pairs.context),
        shape(pairs.patches),
        pltpu.VMEM((2,) + rows, jnp.float32),
        shape(saved.query),
        shape(saved.key_value),
        shape(saved.cross_attention),
        pltpu.VMEM((H * keys, width), low),
        pltpu.VMEM((H * keys, width), low),
        shape(saved.qkv),
        pltpu.VMEM((2, 2, tokens, tokens), low),
        pltpu.VMEM((2, tokens, tokens), low),
        pltpu.VMEM(rows, low),
        pltpu.VMEM(rows, low),
        pltpu.VMEM(rows, low),
        pltpu.VMEM(rows, low),
    )
    device = place.z * 8 + place.f
    value = small[...]
    narrow, slim = gains_out.shape[1], hidden_out.shape[1]
    turned = pltpu.roll(value, lax.rem(width - device * narrow, width), 1)
    gains_out[...] = turned[:3, :narrow]
    biases_out[...] = turned[3:13, :narrow]
    number = lax.broadcasted_iota(jnp.int32, value.shape, 0)
    picked = jnp.sum(jnp.where(number == 13 + place.z, value, 0.0), axis=0, keepdims=True)
    picked = pltpu.roll(jnp.broadcast_to(picked, (8, width)), lax.rem(width - place.f * slim, width), 1)
    hidden_out[...] = picked[:1, :slim]
    for name in WEIGHTS:
        swaps[name].wait_recv()
        out = getattr(outs, name)
        mine, other = getattr(finals, name)[core], getattr(swapped, name)[...]
        middle = mine.shape[1]
        out[:, :middle] = jnp.where(core == 0, mine, other)
        out[:, middle:] = jnp.where(core == 0, other, mine)
    copies.finish()


def gathered(line, shards):
    return [(2, line, 2, 2, 2 * shard.shape[0], shard.shape[1] // 2) for shard in shards]


def forward_all(line, shards, vectors, text, patches, pair_row, region_row):
    tokens, width = text.shape
    keys, depth = patches.shape
    wide = shards[5].shape[1]
    low, full = jnp.bfloat16, jnp.float32
    rows = (tokens, width)
    kept = [
        ((tokens, 3 * width), low),
        ((H, tokens, tokens), low),
        (rows, low),
        ((line, keys, 2 * width), low),
        ((line, H * keys, tokens // line), low),
        ((3,) + rows, full),
        ((3, tokens, 128), full),
        ((tokens, wide), low),
        (rows, low),
        ((16, width), full),
    ]
    locals_ = [((8, wide), full), (rows, low), (rows, low), (rows, low), (rows, low), ((tokens, wide), low)]
    paired = [rows, (keys, depth), rows, rows, rows, rows, (tokens, wide)]
    shapes = gathered(line, shards)
    out_shape = [jax.ShapeDtypeStruct(shape, low) for shape in shapes]
    out_shape += [jax.ShapeDtypeStruct(*shape) for shape in kept]
    out_shape += [jax.ShapeDtypeStruct((2,) + shape, low) for shape in paired]
    scratch = [pltpu.VMEM(shape, low) for shape in shapes]
    for _ in range(2):
        scratch += [pltpu.VMEM((padded(shard.shape[0]), shard.shape[1] // 2), low) for shard in shards]
    scratch += [pltpu.VMEM(*shape) for shape in kept + locals_]
    scratch += [
        pltpu.VMEM((2, line, 2, 2, 16, 128), low),
        pltpu.VMEM((tokens, 128), full),
        pltpu.VMEM(rows, full),
        pltpu.VMEM((H * keys, width), low),
        pltpu.VMEM((H * keys, width), low),
        pltpu.SemaphoreType.DMA((160,)),
        pltpu.SemaphoreType.DMA((160,)),
        pltpu.SemaphoreType.DMA((96,)),
    ]
    outs = pl.pallas_call(
        functools.partial(forward_kernel, line),
        out_shape=out_shape,
        in_specs=[pl.BlockSpec(memory_space=pltpu.VMEM)] * (len(shards) + 5),
        out_specs=[pl.BlockSpec(memory_space=pl.ANY)] * len(out_shape),
        scratch_shapes=scratch,
        compiler_params=pltpu.CompilerParams(
            collective_id=0, has_side_effects=True, vmem_limit_bytes=62 * 2**20
        ),
    )(*shards, vectors, text, patches, pair_row, region_row)
    count = len(shards)
    return outs[:count], outs[count : count + len(kept)], outs[count + len(kept) :]


def backward_all(line, weights, saved, pairs, cotangent, pair_row, narrow, slim):
    low, full = jnp.bfloat16, jnp.float32
    tokens, width = cotangent.shape
    keys, depth = pairs[1].shape[1:]
    wide = pairs[-1].shape[2]
    sizes = [weight.shape[4:] for weight in weights]
    scratch = []
    for lead in ((line, 2, 2), (line, 2), (line,), (line - 1,)):
        scratch += [pltpu.VMEM(lead + size, low) for size in sizes]
    scratch += [pltpu.VMEM((2, size[0] // 2, size[1]), full) for size in sizes]
    scratch += [pltpu.VMEM((size[0] // 2, size[1]), full) for size in sizes]
    for name, size in zip(WEIGHTS, sizes):
        scratch.append(pltpu.VMEM((keys if name == "ckv" else tokens, size[1]), low))
    scratch += [
        pltpu.VMEM((tokens, width), full),
        pltpu.VMEM((3, tokens, 128), full),
        pltpu.VMEM((16, width), full),
        pltpu.VMEM((24, width), full),
        pltpu.VMEM((2 + line, 24, width), full),
        pltpu.VMEM((line, keys, 2 * width), low),
        pltpu.VMEM((line - 1, keys, 2 * width), low),
        pltpu.VMEM((tokens, 128), full),
        pltpu.VMEM((8, wide), full),
        pltpu.VMEM((keys, 2 * width), low),
        pltpu.SemaphoreType.DMA((160,)),
        pltpu.SemaphoreType.DMA((160,)),
        pltpu.SemaphoreType.DMA((64,)),
    ]
    out_shape = [jax.ShapeDtypeStruct((size[0] // 2, 2 * size[1]), full) for size in sizes]
    out_shape += [
        jax.ShapeDtypeStruct((tokens, width), full),
        jax.ShapeDtypeStruct((keys, depth), full),
        jax.ShapeDtypeStruct((3, narrow), full),
        jax.ShapeDtypeStruct((10, narrow), full),
        jax.ShapeDtypeStruct((1, slim), full),
    ]
    vmem, anywhere = pl.BlockSpec(memory_space=pltpu.VMEM), pl.BlockSpec(memory_space=pl.ANY)
    count = len(weights)
    outs = pl.pallas_call(
        functools.partial(backward_kernel, line),
        out_shape=out_shape,
        in_specs=[anywhere] * (count + len(saved) + len(pairs) + 1) + [vmem],
        out_specs=[vmem] * count + [anywhere] + [vmem] * 4,
        scratch_shapes=scratch,
        compiler_params=pltpu.CompilerParams(
            collective_id=1, has_side_effects=True, vmem_limit_bytes=63 * 2**20
        ),
    )(*weights, *saved, *pairs, cotangent, pair_row)
    return outs[:count], outs[count:]


def hand_out_kernel(count, *refs):
    semaphores = refs[-1]
    moves = [
        pltpu.make_async_copy(source, target, semaphores.at[number])
        for number, (source, target) in enumerate(zip(refs[:count], refs[count : 2 * count]))
    ]
    for move in moves:
        move.start()
    for move in moves:
        move.wait()


def hand_out(values):
    count = len(values)
    anywhere = pl.BlockSpec(memory_space=pl.ANY)
    return pl.pallas_call(
        functools.partial(hand_out_kernel, count),
        out_shape=[jax.ShapeDtypeStruct(value.shape, value.dtype) for value in values],
        in_specs=[anywhere] * count,
        out_specs=[pl.BlockSpec(memory_space=pltpu.VMEM)] * count,
        scratch_shapes=[pltpu.SemaphoreType.DMA((count,))],
        compiler_params=pltpu.CompilerParams(vmem_limit_bytes=63 * 2**20),
    )(*values)


def fast_body(
    text_rows,
    patches,
    row_pair,
    row_region,
    self_qkv,
    self_out,
    cross_query,
    cross_key_value,
    cross_out,
    ffn_up,
    ffn_down,
    norm_gains,
    biases,
    ffn_bias,
    cotangent,
):
    line = lax.axis_size("dp")
    narrow, slim = norm_gains.shape[1], ffn_bias.shape[0]
    vectors = jnp.concatenate(
        [
            jnp.pad(norm_gains, ((0, 0), (0, 128 - narrow))),
            jnp.pad(biases, ((0, 0), (0, 128 - narrow))),
            jnp.pad(ffn_bias[None], ((0, 2), (0, 128 - slim))),
        ],
        axis=0,
    )
    shards = (self_qkv, cross_key_value, self_out, cross_query, cross_out, ffn_up, ffn_down)
    pair_row = row_pair.reshape(1, -1)
    weights, kept, pairs = forward_all(
        line,
        shards,
        vectors,
        text_rows,
        patches.reshape(-1, patches.shape[2]),
        pair_row,
        row_region.reshape(1, -1),
    )
    joined = kept[8]
    saved = kept[:8] + kept[9:]
    grads, (text_grad, patch_grad, gains, shifts, hidden) = backward_all(
        line, weights, saved, pairs, cotangent, pair_row, narrow, slim
    )
    results = hand_out((joined, text_grad, patch_grad, gains, shifts, hidden, *grads))
    joined, text_grad, patch_grad, gains, shifts, hidden, *grads = results
    grad_qkv, grad_ckv, grad_sout, grad_cq, grad_cout, grad_up, grad_down = grads
    return (
        joined,
        text_grad,
        patch_grad.reshape(patches.shape),
        grad_qkv,
        grad_sout,
        grad_cq,
        grad_ckv,
        grad_cout,
        grad_up,
        grad_down,
        gains,
        shifts,
        hidden.reshape(-1),
    )


def body(
    text_rows,
    patches,
    row_pair,
    row_region,
    self_qkv,
    self_out,
    cross_query,
    cross_key_value,
    cross_out,
    ffn_up,
    ffn_down,
    norm_gains,
    biases,
    ffn_bias,
    cotangent,
):
    weight_qkv, weight_sout, weight_cq, weight_ckv, weight_cout, gains_all, bias_all = (
        lax.all_gather(self_qkv, ("dp", "fsdp"), axis=0, tiled=True),
        lax.all_gather(self_out, ("dp", "fsdp"), axis=0, tiled=True),
        lax.all_gather(cross_query, ("dp", "fsdp"), axis=0, tiled=True),
        lax.all_gather(cross_key_value, ("dp", "fsdp"), axis=0, tiled=True),
        lax.all_gather(cross_out, ("dp", "fsdp"), axis=0, tiled=True),
        lax.all_gather(norm_gains, ("dp", "fsdp"), axis=1, tiled=True),
        lax.all_gather(biases, ("dp", "fsdp"), axis=1, tiled=True),
    )
    weight_up, weight_down, bias_up_all = (
        lax.all_gather(ffn_up, ("dp", "fsdp"), axis=0, tiled=True),
        lax.all_gather(ffn_down, ("dp", "fsdp"), axis=0, tiled=True),
        lax.all_gather(ffn_bias, ("dp", "fsdp"), axis=0, tiled=True),
    )
    gains = gains_all.astype(jnp.float32)
    bias_rows = bias_all.astype(jnp.float32)
    bias_hidden = bias_up_all.astype(jnp.float32)
    row_count, model_width = text_rows.shape
    owners = lax.axis_size("dp")
    block_rows = row_count // owners
    valid = (row_pair >= 0)[:, None]
    patch_rows = patches.reshape(-1, patches.shape[2])
    kv_projected = jnp.dot(patch_rows, weight_ckv, preferred_element_type=jnp.float32)
    key_local = kv_projected[:, :model_width].astype(jnp.bfloat16)
    value_local = (kv_projected[:, model_width:] + bias_rows[4]).astype(jnp.bfloat16)
    keys_count = key_local.shape[0]
    kept_self, context_self = self_forward(
        text_rows, row_pair, weight_qkv, bias_rows[0], bias_rows[1]
    )
    branch_self = (
        jnp.dot(context_self, weight_sout, preferred_element_type=jnp.float32) + bias_rows[2]
    )
    first, normed_one, inverse_one = norm_forward(
        text_rows.astype(jnp.float32) + branch_self, gains[0], bias_rows[7]
    )
    first_low = first.astype(jnp.bfloat16)
    queries = (
        jnp.dot(first_low, weight_cq, preferred_element_type=jnp.float32) + bias_rows[3]
    ).astype(jnp.bfloat16)
    region_blocks = row_region.reshape(owners, block_rows)
    arrived, arrived_region = (
        lax.all_to_all(
            queries.reshape(owners, block_rows, model_width),
            "dp",
            split_axis=0,
            concat_axis=0,
            tiled=True,
        ),
        lax.all_to_all(region_blocks, "dp", split_axis=0, concat_axis=0, tiled=True),
    )
    arrived = arrived.reshape(1, owners * block_rows, H, HD)
    arrived_region = arrived_region.reshape(1, owners * block_rows)
    key_view = key_local.reshape(1, keys_count, H, HD)
    value_view = value_local.reshape(1, keys_count, H, HD)
    logsum_cross, context_owner = cross_forward(arrived, key_view, value_view, arrived_region)
    context_cross = lax.all_to_all(
        context_owner.reshape(owners, block_rows, model_width),
        "dp",
        split_axis=0,
        concat_axis=0,
        tiled=True,
    ).reshape(row_count, model_width)
    branch_cross = (
        jnp.dot(context_cross, weight_cout, preferred_element_type=jnp.float32) + bias_rows[5]
    )
    second, normed_two, inverse_two = norm_forward(first + branch_cross, gains[1], bias_rows[8])
    second_low = second.astype(jnp.bfloat16)
    hidden_pre = jnp.dot(second_low, weight_up, preferred_element_type=jnp.float32) + bias_hidden
    hidden_low = gelu_exact(hidden_pre).astype(jnp.bfloat16)
    branch_ffn = jnp.dot(hidden_low, weight_down, preferred_element_type=jnp.float32) + bias_rows[6]
    result, normed_three, inverse_three = norm_forward(second + branch_ffn, gains[2], bias_rows[9])
    joined_text = jnp.where(valid, result, 0.0).astype(jnp.bfloat16)
    upstream = jnp.where(valid, cotangent.astype(jnp.float32), 0.0)
    grad_three, grad_gain_three, grad_shift_three = norm_backward(
        upstream, normed_three, inverse_three, gains[2]
    )
    grad_ffn = grad_three.astype(jnp.bfloat16)
    grad_hidden = times_transpose(grad_ffn, weight_down)
    grad_pre = jax.vjp(gelu_exact, hidden_pre)[1](grad_hidden)[0].astype(jnp.bfloat16)
    ffn_terms = (
        transpose_times(second_low, grad_pre),
        transpose_times(hidden_low, grad_ffn),
        jnp.sum(grad_pre, axis=0, dtype=jnp.float32),
    )
    grad_up, grad_down, grad_up_bias = (
        lax.psum_scatter(ffn_terms[0], ("dp", "fsdp"), scatter_dimension=0, tiled=True),
        lax.psum_scatter(ffn_terms[1], ("dp", "fsdp"), scatter_dimension=0, tiled=True),
        lax.psum_scatter(ffn_terms[2], ("dp", "fsdp"), scatter_dimension=0, tiled=True),
    )
    grad_second = grad_three + times_transpose(grad_pre, weight_up)
    grad_two, grad_gain_two, grad_shift_two = norm_backward(
        grad_second, normed_two, inverse_two, gains[1]
    )
    grad_cross = grad_two.astype(jnp.bfloat16)
    grad_context = times_transpose(grad_cross, weight_cout).astype(jnp.bfloat16)
    grad_arrived = lax.all_to_all(
        grad_context.reshape(owners, block_rows, model_width),
        "dp",
        split_axis=0,
        concat_axis=0,
        tiled=True,
    ).reshape(1, owners * block_rows, H, HD)
    grad_query_owner, grad_key, grad_value = cross_backward(
        arrived, key_view, value_view, arrived_region, logsum_cross, grad_arrived
    )
    grad_queries = lax.all_to_all(
        grad_query_owner.astype(jnp.bfloat16).reshape(owners, block_rows, model_width),
        "dp",
        split_axis=0,
        concat_axis=0,
        tiled=True,
    ).reshape(row_count, model_width)
    grad_key_total = grad_key.reshape(keys_count, model_width)
    grad_value_total = grad_value.reshape(keys_count, model_width)
    grad_kv = jnp.concatenate(
        [grad_key_total.astype(jnp.bfloat16), grad_value_total.astype(jnp.bfloat16)], axis=1
    )
    patch_grad = times_transpose(grad_kv, weight_ckv).reshape(patches.shape)
    grad_ckv = transpose_times(patch_rows, grad_kv)
    grad_cross_value_bias = jnp.sum(grad_kv[:, model_width:], axis=0, dtype=jnp.float32)
    grad_first = grad_two + times_transpose(grad_queries, weight_cq)
    grad_cq = transpose_times(first_low, grad_queries)
    grad_cout = transpose_times(context_cross, grad_cross)
    grad_one, grad_gain_one, grad_shift_one = norm_backward(
        grad_first, normed_one, inverse_one, gains[0]
    )
    grad_self = grad_one.astype(jnp.bfloat16)
    grad_sout = transpose_times(context_self, grad_self)
    grad_context_self = times_transpose(grad_self, weight_sout).astype(jnp.bfloat16)
    grad_projected = self_backward(kept_self, grad_context_self)
    grad_qkv = transpose_times(text_rows, grad_projected)
    text_grad = grad_one + times_transpose(grad_projected, weight_qkv)
    gain_terms = jnp.stack([grad_gain_one, grad_gain_two, grad_gain_three])
    bias_terms = jnp.stack(
        [
            jnp.sum(grad_projected[:, :model_width], axis=0, dtype=jnp.float32),
            jnp.sum(grad_projected[:, 2 * model_width :], axis=0, dtype=jnp.float32),
            jnp.sum(grad_self, axis=0, dtype=jnp.float32),
            jnp.sum(grad_queries, axis=0, dtype=jnp.float32),
            grad_cross_value_bias,
            jnp.sum(grad_cross, axis=0, dtype=jnp.float32),
            jnp.sum(grad_ffn, axis=0, dtype=jnp.float32),
            grad_shift_one,
            grad_shift_two,
            grad_shift_three,
        ]
    )
    attn_terms = (grad_qkv, grad_sout, grad_cq, grad_ckv, grad_cout, gain_terms, bias_terms)
    shard_qkv, shard_sout, shard_cq, shard_ckv, shard_cout, shard_gains, shard_biases = (
        lax.psum_scatter(attn_terms[0], ("dp", "fsdp"), scatter_dimension=0, tiled=True),
        lax.psum_scatter(attn_terms[1], ("dp", "fsdp"), scatter_dimension=0, tiled=True),
        lax.psum_scatter(attn_terms[2], ("dp", "fsdp"), scatter_dimension=0, tiled=True),
        lax.psum_scatter(attn_terms[3], ("dp", "fsdp"), scatter_dimension=0, tiled=True),
        lax.psum_scatter(attn_terms[4], ("dp", "fsdp"), scatter_dimension=0, tiled=True),
        lax.psum_scatter(attn_terms[5], ("dp", "fsdp"), scatter_dimension=1, tiled=True),
        lax.psum_scatter(attn_terms[6], ("dp", "fsdp"), scatter_dimension=1, tiled=True),
    )
    return (
        joined_text,
        text_grad,
        patch_grad,
        shard_qkv,
        shard_sout,
        shard_cq,
        shard_ckv,
        shard_cout,
        grad_up,
        grad_down,
        shard_gains,
        shard_biases,
        grad_up_bias,
    )


def solution(mesh):
    in_specs = (
        P(("dp", "fsdp"), None),
        P(("dp", "fsdp"), None, None),
        P(("dp", "fsdp")),
        P(("dp", "fsdp")),
        P(("dp", "fsdp"), None),
        P(("dp", "fsdp"), None),
        P(("dp", "fsdp"), None),
        P(("dp", "fsdp"), None),
        P(("dp", "fsdp"), None),
        P(("dp", "fsdp"), None),
        P(("dp", "fsdp"), None),
        P(None, ("dp", "fsdp")),
        P(None, ("dp", "fsdp")),
        P(("dp", "fsdp")),
        P(("dp", "fsdp"), None),
    )
    out_specs = (
        P(("dp", "fsdp"), None),
        P(("dp", "fsdp"), None),
        P(("dp", "fsdp"), None, None),
        P(("dp", "fsdp"), None),
        P(("dp", "fsdp"), None),
        P(("dp", "fsdp"), None),
        P(("dp", "fsdp"), None),
        P(("dp", "fsdp"), None),
        P(("dp", "fsdp"), None),
        P(("dp", "fsdp"), None),
        P(None, ("dp", "fsdp")),
        P(None, ("dp", "fsdp")),
        P(("dp", "fsdp")),
    )
    fast = mesh.shape["fsdp"] == 8
    chosen = fast_body if fast else body
    return jax.shard_map(chosen, mesh=mesh, in_specs=in_specs, out_specs=out_specs, check_vma=False)
```

```python
import functools
import math
import types

import jax
import jax.numpy as jnp
from jax import lax
from jax.experimental import pallas as pl
from jax.experimental.pallas import tpu as pltpu
from jax.sharding import PartitionSpec as P

H = 12
HD = 64
PR = 32
BLK = 512


EPSILON = 1e-06
NEGATIVE = -1e30


def times_transpose(left, right):
    return lax.dot_general(
        left, right, (((1,), (1,)), ((), ())), preferred_element_type=jnp.float32
    )


def transpose_times(left, right):
    return lax.dot_general(
        left, right, (((0,), (0,)), ((), ())), preferred_element_type=jnp.float32
    )


def gelu_exact(values):
    return jax.nn.gelu(values, approximate=False)


def norm_forward(summed, gain_row, shift_row):
    center = summed - jnp.mean(summed, axis=-1, keepdims=True)
    inverse = lax.rsqrt(jnp.mean(center * center, axis=-1, keepdims=True) + EPSILON)
    normed = center * inverse
    return (normed * gain_row + shift_row, normed, inverse)


def norm_backward(upstream, normed, inverse, gain_row):
    scaled = upstream * gain_row
    centered = (
        scaled
        - jnp.mean(scaled, axis=-1, keepdims=True)
        - normed * jnp.mean(scaled * normed, axis=-1, keepdims=True)
    )
    return (inverse * centered, jnp.sum(upstream * normed, axis=0), jnp.sum(upstream, axis=0))


def self_scores(query_rows, key_rows, segment):
    scores = jnp.einsum(
        "qhd,khd->hqk", query_rows, key_rows, preferred_element_type=jnp.float32
    ) * (1.0 / math.sqrt(HD))
    same_pair = segment[:, None] == segment[None, :]
    return jnp.where(same_pair[None], scores, NEGATIVE)


def self_window(window):
    query_rows, key_rows, value_rows, segment = window
    scores = self_scores(query_rows, key_rows, segment)
    highest = jnp.max(scores, axis=-1, keepdims=True)
    logsum = highest + jnp.log(jnp.sum(jnp.exp(scores - highest), axis=-1, keepdims=True))
    weights = jnp.exp(scores - logsum).astype(jnp.bfloat16)
    context = jnp.einsum("hqk,khd->qhd", weights, value_rows, preferred_element_type=jnp.float32)
    return (logsum, context.astype(jnp.bfloat16))


def self_window_back(window):
    query_rows, key_rows, value_rows, segment, logsum, grad_rows = window
    probability = jnp.exp(self_scores(query_rows, key_rows, segment) - logsum)
    grad_prob = jnp.einsum(
        "qhd,khd->hqk", grad_rows, value_rows, preferred_element_type=jnp.float32
    )
    grad_score = (
        probability * (grad_prob - jnp.sum(probability * grad_prob, axis=-1, keepdims=True))
    ).astype(jnp.bfloat16)
    scaling = 1.0 / math.sqrt(HD)
    grad_query = (
        jnp.einsum("hqk,khd->qhd", grad_score, key_rows, preferred_element_type=jnp.float32)
        * scaling
    )
    grad_key = (
        jnp.einsum("hqk,qhd->khd", grad_score, query_rows, preferred_element_type=jnp.float32)
        * scaling
    )
    grad_value = jnp.einsum(
        "hqk,qhd->khd",
        probability.astype(jnp.bfloat16),
        grad_rows,
        preferred_element_type=jnp.float32,
    )
    return jnp.concatenate(
        [grad_query.reshape(BLK, -1), grad_key.reshape(BLK, -1), grad_value.reshape(BLK, -1)],
        axis=1,
    ).astype(jnp.bfloat16)


def self_forward(text_rows, segment, weight_qkv, bias_query, bias_value):
    row_count, model_width = text_rows.shape
    blocks = row_count // BLK
    projected = jnp.dot(text_rows, weight_qkv, preferred_element_type=jnp.float32)
    query_rows = (
        (projected[:, :model_width] + bias_query).astype(jnp.bfloat16).reshape(blocks, BLK, H, HD)
    )
    key_rows = (
        projected[:, model_width : 2 * model_width].astype(jnp.bfloat16).reshape(blocks, BLK, H, HD)
    )
    value_rows = (
        (projected[:, 2 * model_width :] + bias_value)
        .astype(jnp.bfloat16)
        .reshape(blocks, BLK, H, HD)
    )
    segment = segment.reshape(blocks, BLK)
    logsum, context = lax.map(self_window, (query_rows, key_rows, value_rows, segment))
    return (
        (query_rows, key_rows, value_rows, segment, logsum),
        context.reshape(row_count, model_width),
    )


def self_backward(kept_self, grad_context):
    query_rows, key_rows, value_rows, segment, logsum = kept_self
    blocks = query_rows.shape[0]
    grad_rows = grad_context.reshape(blocks, BLK, H, HD)
    grad_projected = lax.map(
        self_window_back, (query_rows, key_rows, value_rows, segment, logsum, grad_rows)
    )
    return grad_projected.reshape(blocks * BLK, -1)


def cross_scores(query_rows, key_rows, region_rows):
    scores = jnp.einsum(
        "bkhd,brhd->bhkr", key_rows, query_rows, preferred_element_type=jnp.float32
    ) * (1.0 / math.sqrt(HD))
    key_region = lax.broadcasted_iota(jnp.int32, (key_rows.shape[1], 1), 0) // PR
    same_region = key_region[None] == region_rows[:, None, :]
    return jnp.where(same_region[:, None], scores, NEGATIVE)


def cross_forward(query_rows, key_rows, value_rows, region_rows):
    scores = cross_scores(query_rows, key_rows, region_rows)
    highest = jnp.max(scores, axis=2, keepdims=True)
    logsum = highest + jnp.log(jnp.sum(jnp.exp(scores - highest), axis=2, keepdims=True))
    weights = jnp.exp(scores - logsum).astype(jnp.bfloat16)
    context = jnp.einsum("bhkr,bkhd->brhd", weights, value_rows, preferred_element_type=jnp.float32)
    return (logsum, context.astype(jnp.bfloat16))


def cross_backward(query_rows, key_rows, value_rows, region_rows, logsum, grad_context):
    probability = jnp.exp(cross_scores(query_rows, key_rows, region_rows) - logsum)
    grad_prob = jnp.einsum(
        "bkhd,brhd->bhkr", value_rows, grad_context, preferred_element_type=jnp.float32
    )
    grad_score = (
        probability * (grad_prob - jnp.sum(probability * grad_prob, axis=2, keepdims=True))
    ).astype(jnp.bfloat16)
    scaling = 1.0 / math.sqrt(HD)
    grad_query = (
        jnp.einsum("bhkr,bkhd->brhd", grad_score, key_rows, preferred_element_type=jnp.float32)
        * scaling
    )
    grad_key = (
        jnp.einsum("bhkr,brhd->bkhd", grad_score, query_rows, preferred_element_type=jnp.float32)
        * scaling
    )
    grad_value = jnp.einsum(
        "bhkr,brhd->bkhd",
        probability.astype(jnp.bfloat16),
        grad_context,
        preferred_element_type=jnp.float32,
    )
    return (grad_query, grad_key, grad_value)


MESH = pl.DeviceIdType.MESH
WEIGHTS = ("qkv", "ckv", "sout", "cq", "cout", "up", "down")
CORE_LINK = 400e3


def named(names, refs):
    return types.SimpleNamespace(**dict(zip(names, refs)))


class Place:
    def __init__(self, line):
        self.line = line
        self.z = lax.axis_index("dp")
        self.f = lax.axis_index("fsdp")
        self.core = lax.rem(self.f, 2)
        self.x = lax.rem(self.f // 2, 2)
        self.y = self.f // 4
        self.other = {"c": 1 - self.core, "x": 1 - self.x, "y": 1 - self.y}
        steps = {"c": 1 - 2 * self.core, "x": 2 - 4 * self.x, "y": 4 - 8 * self.y}
        self.neighbours = {axis: self.f + step for axis, step in steps.items()}
        self.onward = [lax.rem(self.z + k, line) for k in range(line)]
        self.backward = [lax.rem(self.z + line - k, line) for k in range(line)]

    def across(self, axis):
        return (self.z, self.neighbours[axis])

    def along(self, offset):
        return (self.onward[offset], self.f)

    def ahead(self, offset):
        return self.onward[offset]

    def behind(self, offset):
        return self.backward[offset]

    def greet(self):
        barrier = pltpu.get_barrier_semaphore()
        partners = [self.across(axis) for axis in "cxy"] + [self.along(k) for k in range(1, self.line)]
        for device in partners:
            pl.semaphore_signal(barrier, inc=1, device_id=device, device_id_type=MESH)

    def meet(self):
        pl.semaphore_wait(pltpu.get_barrier_semaphore(), 2 + self.line)

    def block(self, whole):
        return tuple(slice(None) if axis in whole else getattr(self, axis) for axis in "zyx")


def spot(place):
    return place[0].at[place[1]] if isinstance(place, tuple) else place


class Copy:
    def __init__(self, make):
        self.make = make

    def wait_recv(self):
        self.make(True).wait_recv()

    def wait_send(self):
        self.make(False).wait_send()

    def wait(self):
        self.wait_send()
        self.wait_recv()


class LocalCopy(Copy):
    def wait(self):
        self.make(False).wait()


class Copies:
    def __init__(self, sent, received, local):
        self.sent, self.received, self.local = sent, received, local
        self.count = self.local_count = 0
        self.open = []
        self.writes = []

    def start(self, source, target, device, landing, remember=True):
        number = self.count
        self.count += 1
        copy = Copy(
            lambda arriving: pltpu.make_async_remote_copy(
                src_ref=spot(source),
                dst_ref=spot(landing if arriving else target),
                send_sem=self.sent.at[number],
                recv_sem=self.received.at[number],
                device_id=device,
                device_id_type=MESH,
            )
        )
        copy.make(False).start()
        if remember:
            self.open.append(copy)
        return copy

    def read(self, source, target):
        number = self.local_count
        self.local_count += 1
        copy = LocalCopy(
            lambda arriving: pltpu.make_async_copy(spot(source), spot(target), self.local.at[number])
        )
        copy.make(False).start()
        return copy

    def write(self, source, target):
        self.writes.append(self.read(source, target))

    def finish(self):
        for copy in self.writes:
            copy.wait()
        for copy in self.open:
            copy.wait_send()


class Clock:
    def __init__(self, link, hop, far, slack, scale):
        self.scale = scale
        self.link, self.hop, self.far, self.slack = link, hop, far, slack
        self.now = 0.0
        self.free = dict.fromkeys("czyx", 0.0)

    def send(self, axis, size):
        rate = CORE_LINK if axis == "c" else self.link
        start = max(self.now, self.free[axis])
        self.free[axis] = start + size / rate
        return self.free[axis] + (1.5 if axis == "c" else self.far if axis == "z" else self.hop)


def volume(shape):
    return 2 * math.prod(shape)


class GatherUnit:
    def __init__(self, place, copies, clock, buffer, columns, order):
        self.place, self.copies, self.clock, self.buffer = place, copies, clock, buffer
        self.columns, self.order = columns, order + "c"
        self.held, self.stage, self.arrivals = "", 0, []
        self.size = volume((buffer.shape[4], columns.size))

    def view(self, index, half=None):
        half = self.place.core if half is None else half
        return self.buffer, (half,) + index + (slice(None), self.columns)

    def send(self):
        place = self.place
        axis = self.order[self.stage]
        mine = place.block(self.held)
        blocks = math.prod({"z": place.line, "y": 2, "x": 2}[held] for held in self.held)
        if axis == "z":
            moves = [(place.along(k), (place.behind(k),) + mine[1:], None) for k in range(1, place.line)]
            blocks *= place.line
        elif axis == "c":
            moves = [(place.across(axis), mine, place.other["c"])]
        else:
            level = "zyx".index(axis)
            moves = [(place.across(axis), mine[:level] + (place.other[axis],) + mine[level + 1 :], None)]
        self.arrivals = [
            self.copies.start(self.view(mine), self.view(mine), device, self.view(theirs, half))
            for device, theirs, half in moves
        ]
        self.due = self.clock.send(axis, blocks * self.size)
        self.held += axis
        self.stage += 1

    def step(self):
        for copy in self.arrivals:
            copy.wait_recv()
        self.clock.now = max(self.clock.now, self.due) + 0.1
        if self.stage == len(self.order):
            return True
        if self.stage == 1:
            self.begin()
        self.send()
        return False


class SumUnit:
    def __init__(self, place, copies, clock, total, landings, result, rows, columns, order):
        self.place, self.copies, self.clock, self.total = place, copies, clock, total
        self.landings, self.result, self.order = landings, result, order
        self.area = (rows, columns)
        self.left, self.stage, self.arrivals = "zyx", 0, []
        self.size = volume((rows.size, columns.size))

    def send(self):
        place, area, stage = self.place, self.area, self.stage
        axis = self.order[stage]
        mine = place.block(self.left)
        level = "zyx".index(axis)
        landing = self.landings[stage]
        self.left = self.left.replace(axis, "")
        each = math.prod({"z": place.line, "y": 2, "x": 2}[left] for left in self.left)
        blocks = each
        if axis == "z":
            moves = []
            for offset in range(1, place.line):
                span = pl.ds((offset - 1) * each, each) if each > 1 else offset - 1
                moves.append((place.along(offset), place.ahead(offset), span))
            blocks *= place.line
        else:
            span = pl.ds(0, each) if each > 1 else 0
            if stage == 0:
                span = (pl.ds(0, place.line), pl.ds(0, 2))
            moves = [(place.across(axis), place.other[axis], span)]
        self.arrivals = []
        for device, goal, span in moves:
            there = landing, (span if isinstance(span, tuple) else (span,)) + area
            source = self.total, mine[:level] + (goal,) + mine[level + 1 :] + area
            self.arrivals.append(self.copies.start(source, there, device, there))
        self.due = self.clock.send(axis, blocks * self.size)
        self.axis = axis
        self.stage += 1

    def send_slab(self, z):
        place, axis = self.place, self.order[0]
        index = (z, place.other[axis], slice(None)) if axis == "y" else (z, slice(None), place.other[axis])
        there = self.landings[0], (z, slice(None)) + self.area
        self.arrivals.append(
            self.copies.start((self.total, index + self.area), there, place.across(axis), there)
        )
        self.due = self.clock.send(axis, 2 * self.size)
        if z == place.line - 1:
            self.left = self.left.replace(axis, "")
            self.axis, self.stage = axis, 1

    def step(self):
        for copy in self.arrivals:
            copy.wait_recv()
        self.clock.now = max(self.clock.now, self.due) + 0.2
        place, area, landing, line = self.place, self.area, self.landings[self.stage - 1], self.place.line

        def add(index, spots):
            value = self.total[index + area].astype(jnp.float32)
            for one in spots:
                value += landing[one + area].astype(jnp.float32)
            return value

        def store(index, spots):
            self.total[index + area] = add(index, spots).astype(jnp.bfloat16)

        if self.stage == 3:
            count = line - 1 if self.axis == "z" else 1
            value = add((place.z, place.y, place.x), [(k,) for k in range(count)])
            put_halves(self.result, area, value)
            return True
        if self.stage == 1:

            def one(z, carry):
                for other in range(2):
                    store((z, place.y, other) if self.axis == "y" else (z, other, place.x), [(z, other)])
                return carry

            lax.fori_loop(0, line, one, 0)
        elif self.axis == "z":
            for other in range(2):
                index = (place.z, place.y, other) if self.left == "x" else (place.z, other, place.x)
                store(index, [(k * 2 + other,) for k in range(line - 1)])
        else:

            def one(z, carry):
                store((z, place.y, place.x), [(z,)])
                return carry

            lax.fori_loop(0, line, one, 0)
        self.send()
        return False


def put_halves(final, area, value):
    rows, columns = area
    half = final.shape[1]
    done = 0
    while done < rows.size:
        core, at = (rows.start + done) // half, (rows.start + done) % half
        step = min(rows.size - done, half - at)
        final[core, pl.ds(at, step), columns] = value[done : done + step]
        done += step


class Schedule:
    def __init__(self, clock, done):
        self.clock, self.done = clock, done
        self.tasks, self.flying = [], []

    def task(self, cost, function, *arguments, ready=lambda: True):
        self.tasks.append((cost, functools.partial(function, *arguments), ready))

    def launch(self, unit):
        unit.send()
        self.flying.append(unit)

    def run(self, drain=True):
        while self.tasks or (drain and self.flying):
            soonest = min(self.flying, key=lambda unit: unit.due) if self.flying else None
            runnable = self.tasks and self.tasks[0][2]()
            if soonest is not None and (soonest.due + self.clock.slack <= self.clock.now or not runnable):
                if soonest.step():
                    self.flying.remove(soonest)
                    self.done(soonest)
            else:
                cost, function, _ = self.tasks.pop(0)
                function()
                self.clock.now += cost * self.clock.scale


def padded(rows):
    return -(-rows // 16) * 16


def matrix(value):
    return value.reshape(-1, value.shape[-1])


def dot(left, right, contract=(1, 0)):
    return lax.dot_general(
        left, right, (((contract[0],), (contract[1],)), ((), ())), preferred_element_type=jnp.float32
    )


def whole(buffer):
    return jnp.concatenate([matrix(buffer[0]), matrix(buffer[1])], axis=1)


def column_spans(rows, columns):
    wide = 384 if rows <= 64 else 128
    return [pl.ds(column, wide) for column in range(0, columns, wide)]


def merged_rows(place, mine, other):
    mine, other = mine.astype(jnp.float32), other.astype(jnp.float32)
    first = jnp.where(place.core == 0, mine, other)
    second = jnp.where(place.core == 0, other, mine)
    return jnp.concatenate([first, second], axis=0).astype(jnp.bfloat16)


def column_half(place, values, own):
    half = values.shape[1] // 2
    left, right = values[:, :half].astype(jnp.float32), values[:, half:].astype(jnp.float32)
    return jnp.where((place.core == 0) == own, left, right)

def gelu_pair(values):
    half_square = jnp.exp(values * values * -0.5)
    size = jnp.abs(values)
    t = 1.0 / (1.0 + (0.3275911 * math.sqrt(0.5)) * size)
    series = t * (
        0.5 * 0.254829592
        + t * (-0.5 * 0.284496736 + t * (0.5 * 1.421413741 + t * (-0.5 * 1.453152027 + t * (0.5 * 1.061405429))))
    )
    tail = series * half_square
    phi = jnp.where(values < 0, tail, 1.0 - tail)
    slope = phi + values * half_square * (1.0 / math.sqrt(2.0 * math.pi))
    return values * phi, slope


def spread_vectors(vectors_all, rows_out, hidden_out, narrow, wide, line):
    lanes = lax.broadcasted_iota(jnp.int32, (16, 128), 1)
    sums = {id(rows_out): {}, id(hidden_out): {}}

    def place(target, values, start, size):
        found = sums[id(target)]
        tile, shift = start // 128, start % 128
        rolled = pltpu.roll(values, shift, 1) if shift else values
        lane = lanes[: values.shape[0]]
        first = jnp.where((lane >= shift) & (lane < shift + size), rolled, 0.0)
        found[tile] = found[tile] + first if tile in found else first
        if shift + size > 128:
            second = jnp.where(lane < shift + size - 128, rolled, 0.0)
            tile += 1
            found[tile] = found[tile] + second if tile in found else second

    for z in range(line):
        for y in range(2):
            for x in range(2):
                for core in range(2):
                    device = ((z * 2 + y) * 2 + x) * 2 + core
                    values = vectors_all[core, z, y, x].astype(jnp.float32)
                    place(rows_out, values, device * narrow, narrow)
                    place(hidden_out, values[8:], device * wide, wide)
    for target in (rows_out, hidden_out):
        for tile, value in sums[id(target)].items():
            target[:, pl.ds(tile * 128, 128)] = value

KEPT = ("qkv", "attention", "query", "key_value", "cross_attention", "normed", "inverse", "slope", "joined", "rows")
PAIRS = ("text", "patches", "context", "low_one", "context_cross", "low_two", "hidden_low")
LOCAL = ("hidden", "context", "low_one", "context_cross", "low_two", "hidden_low")


def forward_kernel(line, *refs):
    refs = list(refs)
    take = lambda names: named(names, [refs.pop(0) for _ in names])
    shards = take(WEIGHTS)
    vectors, text, patches, pair_row, region_row = [refs.pop(0) for _ in range(5)]
    outs, kept_out, pairs = take(WEIGHTS), take(KEPT), take(PAIRS)
    buffers, outgoing, incoming = take(WEIGHTS), take(WEIGHTS), take(WEIGHTS)
    kept = named(KEPT + LOCAL, [refs.pop(0) for _ in KEPT + LOCAL])
    vectors_all, pair_column, work, keys_all, values_all, sent, received, local = refs
    place = Place(line)
    copies = Copies(sent, received, local)
    clock = Clock(55e3, 1.5, 4.5, -0.5, 1.0)
    tokens, width = text.shape
    rows_all, hidden_all = kept.rows, kept.hidden
    block = tokens // line
    narrow = shards.qkv.shape[0]
    keys = patches.shape[0]
    place.greet()
    for name in WEIGHTS:
        shard, target = getattr(shards, name), getattr(outgoing, name)
        away = column_half(place, shard[...], False)
        padding = target.shape[0] - shard.shape[0]
        if padding:
            away = jnp.concatenate([away, jnp.zeros((padding, away.shape[1]), jnp.float32)], axis=0)
        target[...] = away.astype(jnp.bfloat16)
    vectors_all[place.core, place.z, place.y, place.x] = vectors[...]
    place.meet()
    swaps = {}
    for name in WEIGHTS:
        there = getattr(incoming, name)
        swaps[name] = copies.start(getattr(outgoing, name), there, place.across("c"), there)
    pair_column[...] = jnp.broadcast_to(pair_row[...].astype(jnp.float32), (128, tokens)).T
    arrivals = []

    def merge(name):
        swaps[name].wait_recv()
        shard = getattr(shards, name)
        mine = column_half(place, shard[...], True)
        other = getattr(incoming, name)[...][: shard.shape[0]]
        getattr(buffers, name)[place.core, place.z, place.y, place.x] = merged_rows(place, mine, other)

    def keep(source, target):
        copies.write(source, target)

    def pair(source, target, *columns):
        there = target.at[(place.core,) + columns]
        copies.write(source, there)
        arrivals.append(
            copies.start(source, there, place.across("c"), target.at[(1 - place.core,) + columns])
        )

    def row(number):
        return rows_all[pl.ds(number, 1), :]

    qkv, context, low_one, query, context_cross = (
        kept.qkv, kept.context, kept.low_one, kept.query, kept.context_cross
    )
    hidden, slope, low_two = kept.hidden_low, kept.slope, kept.low_two
    attention, cross_attention = kept.attention, kept.cross_attention
    key_value = kept.key_value

    def project_qkv(part):
        def one(half, carry):
            size = 384
            column = pl.multiple_of(half * (3 * size) + part * size, 128)
            value = dot(text[...], matrix(buffers.qkv[half, :, :, :, :, pl.ds(part * size, size)]))
            group = (half * 3 + part) // 2
            shift = pl.multiple_of(lax.rem(half * 3 + part, 2) * size, 128)
            biased = jnp.where(
                group == 0,
                rows_all[pl.ds(3, 1), pl.ds(shift, size)],
                jnp.where(group == 1, 0.0, rows_all[pl.ds(4, 1), pl.ds(shift, size)]),
            )
            qkv[:, pl.ds(column, size)] = (value + biased).astype(jnp.bfloat16)
            return carry

        lax.fori_loop(0, 2, one, 0)

    strip = 128

    def attend(pair):
        lane = lax.broadcasted_iota(jnp.int32, (strip, 128), 1)
        columns = pl.ds(pair * 128, 128)

        def one(number, carry):
            rows = pl.ds(pl.multiple_of(number * strip, strip), strip)
            two = qkv[rows, columns].astype(jnp.float32) * (1.0 / math.sqrt(HD))
            key_rows = qkv[:, pl.ds(width + pair * 128, 128)]
            value_rows = qkv[:, pl.ds(2 * width + pair * 128, 128)]
            same = jnp.concatenate([pair_column[rows, :]] * (tokens // 128), axis=1) == pair_row[...].astype(
                jnp.float32
            )
            result = None
            for head in range(2):
                own = (lane < HD) if head == 0 else (lane >= HD)
                scores = dot(jnp.where(own, two, 0.0).astype(jnp.bfloat16), key_rows, (1, 1))
                scores = jnp.where(same, scores, NEGATIVE)
                scores = jnp.exp(scores - jnp.max(scores, axis=1, keepdims=True))
                scores = scores * (1.0 / jnp.sum(scores, axis=1, keepdims=True))
                low = scores.astype(jnp.bfloat16)
                attention[pair * 2 + head, rows, :] = low
                value = dot(low, value_rows)
                result = value if head == 0 else jnp.where(own, value, result)
            context[rows, columns] = result.astype(jnp.bfloat16)
            return carry

        lax.fori_loop(0, tokens // strip, one, 0)
        keep(attention.at[pl.ds(2 * pair, 2)], kept_out.attention.at[pl.ds(2 * pair, 2)])

    def normalize(number, summed, low):
        normed, inverse = kept.normed, kept.inverse
        gain, shift = row(number), row(10 + number)
        step = 64

        def one(index, carry):
            rows = pl.ds(pl.multiple_of(index * step, step), step)
            value = work[rows, :] + summed(rows)
            center = value - jnp.mean(value, axis=1, keepdims=True)
            scale = lax.rsqrt(jnp.mean(center * center, axis=1, keepdims=True) + EPSILON)
            value = center * scale
            normed[number, rows, :] = value
            inverse[number, rows, :] = jnp.broadcast_to(scale, (step, 128))
            low(rows, value * gain + shift)
            return carry

        lax.fori_loop(0, tokens // step, one, 0)
        keep(normed.at[number], kept_out.normed.at[number])
        keep(inverse.at[number], kept_out.inverse.at[number])

    def self_out():
        work[...] = dot(context[...], whole(buffers.sout))

        def low(rows, value):
            low_one[rows, :] = value.astype(jnp.bfloat16)

        normalize(0, lambda rows: text[rows, :].astype(jnp.float32) + row(5), low)
        pair(context, pairs.context)
        pair(low_one, pairs.low_one)

    def project_patches(part):
        size = 384
        value = dot(patches[...], matrix(buffers.ckv[0, :, :, :, :, pl.ds(part * size, size)]))
        key_value[place.z, :, pl.ds(part * size, size)] = value.astype(jnp.bfloat16)
        value = dot(patches[...], matrix(buffers.ckv[1, :, :, :, :, pl.ds(part * size, size)]))
        value += rows_all[pl.ds(7, 1), pl.ds(part * size, size)]
        key_value[place.z, :, pl.ds(width + part * size, size)] = value.astype(jnp.bfloat16)

    shared = []

    def share_keys():
        for offset in range(1, line):
            origin = place.behind(offset)
            shared.append(
                copies.start(
                    key_value.at[place.z], key_value.at[place.z], place.along(offset), key_value.at[origin]
                )
            )

    def project_query():
        work[...] = dot(low_one[...], whole(buffers.cq))
        query[...] = (work[...] + row(6)).astype(jnp.bfloat16)
        keep(query, kept_out.query)

    def cross(owner):
        if owner == 0:
            for copy in shared:
                copy.wait_recv()
            keep(key_value, kept_out.key_value)
        lane = lax.broadcasted_iota(jnp.int32, (keys, width), 1) // HD
        for head in range(H):
            rows = pl.ds(head * keys, keys)
            keys_all[rows, :] = jnp.where(
                lane == head, key_value[owner, :, pl.ds(0, width)].astype(jnp.float32), 0.0
            ).astype(jnp.bfloat16)
            values_all[rows, :] = jnp.where(
                lane == head, key_value[owner, :, pl.ds(width, width)].astype(jnp.float32), 0.0
            ).astype(jnp.bfloat16)
        rows = pl.ds(owner * block, block)
        scores = dot(keys_all[...], query[rows, :], (1, 1)) * (1.0 / math.sqrt(HD))
        region = lax.broadcasted_iota(jnp.int32, (keys, block), 0) // PR
        same = region == region_row[:, rows]
        scores = jnp.where(same[None], scores.reshape(H, keys, block), NEGATIVE)
        scores = jnp.exp(scores - jnp.max(scores, axis=1, keepdims=True))
        scores = scores * (1.0 / jnp.sum(scores, axis=1, keepdims=True))
        scores = scores.reshape(H * keys, block).astype(jnp.bfloat16)
        cross_attention[owner] = scores
        context_cross[rows, :] = dot(scores, values_all[...], (0, 0)).astype(jnp.bfloat16)
        if owner == line - 1:
            keep(cross_attention, kept_out.cross_attention)
            pair(context_cross, pairs.context_cross)

    def cross_out():
        work[...] = dot(context_cross[...], whole(buffers.cout))
        first_gain, first_shift = row(0), row(10)

        def low(rows, value):
            low_two[rows, :] = value.astype(jnp.bfloat16)

        normalize(1, lambda rows: kept.normed[0, rows, :] * first_gain + first_shift + row(8), low)
        pair(low_two, pairs.low_two)

    def expand(part):
        size = 384
        half_width = buffers.up.shape[5]

        def one(half, carry):
            column = pl.multiple_of(half * half_width + part * size, 128)
            columns = pl.ds(column, size)
            value = dot(low_two[...], matrix(buffers.up[half, :, :, :, :, pl.ds(part * size, size)]))
            value, grad = gelu_pair(value + hidden_all[pl.ds(5, 1), columns])
            hidden[:, columns] = value.astype(jnp.bfloat16)
            slope[:, columns] = grad.astype(jnp.bfloat16)
            return carry

        lax.fori_loop(0, 2, one, 0)
        for half in range(2):
            columns = pl.ds(half * half_width + part * size, size)
            pair(hidden.at[:, columns], pairs.hidden_low, slice(None), columns)
            keep(slope.at[:, columns], kept_out.slope.at[:, columns])

    def contract(part):
        size = 128
        buffer = buffers.down
        columns = pl.ds(part * size, size)
        both = jnp.concatenate(
            [matrix(buffer[0, :, :, :, :, columns]), matrix(buffer[1, :, :, :, :, columns])], axis=1
        )
        value = dot(hidden[...], both)
        work[:, pl.ds(part * size, size)] = value[:, :size]
        work[:, pl.ds(width // 2 + part * size, size)] = value[:, size:]

    def finish():
        gain, shift = row(1), row(11)

        def low(rows, value):
            valid = jnp.concatenate([pair_column[rows, :]] * (width // 128), axis=1) >= 0
            kept.joined[rows, :] = jnp.where(valid, value, 0.0).astype(jnp.bfloat16)

        normalize(2, lambda rows: kept.normed[1, rows, :] * gain + shift + row(9), low)
        keep(kept.joined, kept_out.joined)

    present, counts = {}, {}
    waiting = []
    merged = set()

    def done(unit):
        present[unit.name] = present.get(unit.name, 0) + 1
        name = unit.name
        if present[name] == counts.get(name):
            keep(getattr(buffers, name), getattr(outs, name))

    schedule = Schedule(clock, done)

    def begin():
        if waiting:
            unit = waiting.pop(0)
            if unit.name and unit.name not in merged:
                merge(unit.name)
                merged.add(unit.name)
            schedule.launch(unit)

    def unit_of(buffer, name, columns):
        order = ("zyx", "zxy")[len(waiting) % 2]
        unit = GatherUnit(place, copies, clock, buffer, columns, order)
        unit.name, unit.begin = name, begin
        waiting.append(unit)

    unit_of(vectors_all, "", pl.ds(0, 128))
    for name in WEIGHTS:
        buffer = getattr(buffers, name)
        spans = column_spans(*buffer.shape[4:])
        counts[name] = len(spans)
        for columns in spans:
            unit_of(buffer, name, columns)

    def task(name, count, cost, function, *arguments):
        schedule.task(cost, function, *arguments, ready=lambda: present.get(name, 0) >= count)

    def spread():
        spread_vectors(vectors_all, rows_all, hidden_all, narrow, shards.down.shape[0], line)
        keep(rows_all, kept_out.rows)

    pair(text, pairs.text)
    pair(patches, pairs.patches)
    task("", 1, 1.0, spread)
    for part in range(3):
        task("qkv", part + 1, 1.5, project_qkv, part)
    task("", 1, 0.0, keep, qkv, kept_out.qkv)
    for number in range(H // 2):
        task("", 1, 1.8, attend, number)
        if number == 3:
            for part in range(2):
                task("ckv", part + 1, 0.5, project_patches, part)
            task("", 1, 0.1, share_keys)
    task("sout", 1, 2.0, self_out)
    task("cq", 1, 1.0, project_query)
    for owner in range(line):
        task("", 1, 1.5, cross, owner)
    task("cout", 1, 2.0, cross_out)
    for part in range(4):
        task("up", part + 1, 3.0, expand, part)
    for part in range(3):
        task("down", part + 1, 1.5, contract, part)
    task("", 1, 1.5, finish)
    for _ in range(3):
        begin()
    schedule.run()
    for copy in arrivals:
        copy.wait_recv()
    copies.finish()

SAVED = ("qkv", "attention", "query", "key_value", "cross_attention", "normed", "inverse", "slope", "rows")
ORDERS = ("yxz", "xyz")


class VectorUnit:
    def __init__(self, place, copies, clock, total, landings):
        self.place, self.copies, self.clock = place, copies, clock
        self.total, self.landings = total, landings
        self.stage = 0

    def send(self):
        place, stage = self.place, self.stage
        if stage < 3:
            devices = [place.across("cxy"[stage])]
        else:
            devices = [place.along(offset) for offset in range(1, place.line)]
        self.arrivals = []
        for number, device in enumerate(devices):
            there = self.landings, (stage + number,)
            self.arrivals.append(self.copies.start(self.total, there, device, there, False))
        self.due = self.clock.now + 3.0
        self.stage += 1

    def step(self):
        for copy in self.arrivals:
            copy.wait()
        value = self.total[...]
        for number in range(len(self.arrivals)):
            value += self.landings[self.stage - 1 + number]
        self.total[...] = value
        self.clock.now = max(self.clock.now, self.due) + 0.1
        if self.stage == 4:
            return True
        self.send()
        return False


def backward_kernel(line, *refs):
    refs = list(refs)
    take = lambda names: named(names, [refs.pop(0) for _ in names])
    pop = lambda count: [refs.pop(0) for _ in range(count)]
    weights, saved, pairs = take(WEIGHTS), take(SAVED), take(PAIRS)
    cotangent, pair_row = pop(2)
    outs = take(WEIGHTS)
    text_grad, patch_grad, gains_out, biases_out, hidden_out = pop(5)
    totals, first, second, third, finals, swapped, landed = (take(WEIGHTS) for _ in range(7))
    work, inverse, rows_all, small, small_landed, key_parts, key_landed, pair_column, hidden_sum = pop(9)
    grad_kv, sent, received, local = pop(4)
    place = Place(line)
    copies = Copies(sent, received, local)
    clock = Clock(60e3, 4.0, 24.0, 3.0, 1.15)
    core = place.core
    tokens, width = work.shape
    hidden_width = hidden_sum.shape[1]
    block = tokens // line
    keys = grad_kv.shape[0]
    scaling = 1.0 / math.sqrt(HD)
    remaining = {}
    swaps = {}

    def done(unit):
        if unit is vectors:
            return
        remaining[unit.name] -= 1
        if not remaining[unit.name]:
            final, there = getattr(finals, unit.name), getattr(swapped, unit.name)
            swaps[unit.name] = copies.start((final, (place.other["c"],)), there, place.across("c"), there)

    schedule = Schedule(clock, done)
    vectors = VectorUnit(place, copies, clock, small, small_landed)

    def prepare(name, rows, columns, count):
        remaining.setdefault(name, count)
        landings = [getattr(group, name) for group in (first, second, third)]
        order = ORDERS[prepare.number % len(ORDERS)]
        prepare.number += 1
        unit = SumUnit(
            place, copies, clock, getattr(totals, name), landings, getattr(finals, name), rows, columns, order
        )
        unit.name = name
        return unit

    def launch(*arguments):
        schedule.launch(prepare(*arguments))

    prepare.number = 0

    def task(cost, function, *arguments):
        schedule.task(cost, function, *arguments)

    def half(size, other=False, offset=0, part=None):
        which = 1 - core if other else core
        return pl.ds(pl.multiple_of(which * size + offset, 128), size if part is None else part)

    def hand_over(source, target, columns=None):
        size = target.shape[1]
        there = target if columns is None else (target, (slice(None), columns))
        away = half(size, True) if columns is None else half(size, True, columns.start, columns.size)
        return copies.start((source, (slice(None), away)), there, place.across("c"), there, False)

    def norm_back(number, bias_number, normed, upstream, low):
        gain = rows_all[pl.ds(number, 1), :]
        step = 64

        def one(index, carry):
            rows = pl.ds(pl.multiple_of(index * step, step), step)
            grad, normal = upstream(rows), normed[rows, :]
            scaled = grad * gain
            center = scaled - jnp.mean(scaled, axis=1, keepdims=True)
            center -= normal * jnp.mean(scaled * normal, axis=1, keepdims=True)
            value = inverse[number, rows, :][:, :1] * center
            work[rows, :] = value
            rounded = value.astype(jnp.bfloat16)
            low[rows, :] = rounded
            sums = (grad * normal, grad, rounded.astype(jnp.float32))
            return tuple(old + jnp.sum(new, axis=0, keepdims=True) for old, new in zip(carry, sums))

        zero = jnp.zeros((1, width), jnp.float32)
        gain_sum, shift_sum, bias_sum = lax.fori_loop(0, tokens // step, one, (zero, zero, zero))
        small[pl.ds(number, 1), :] = gain_sum
        small[pl.ds(10 + number, 1), :] = shift_sum
        small[pl.ds(bias_number, 1), :] = bias_sum

    def weight_grad(name, inputs, low, landing, columns, span=None):
        size = landing.shape[1]
        own = half(size, False, columns.start, columns.size)
        span = slice(None) if span is None else span
        value = dot(inputs[core, :, span], low[:, own], (0, 0))
        value += dot(inputs[1 - core, :, span], landing[:, columns], (0, 0))
        return value.astype(jnp.bfloat16)

    def spread_columns(name, inputs, low, columns, count):
        total = getattr(totals, name)
        value = weight_grad(name, inputs, low, getattr(landed, name), columns)
        total[:, :, :, :, columns] = value.reshape(total.shape[:4] + (columns.size,))
        launch(name, pl.ds(0, total.shape[3]), columns, count)

    def feed_forward(up, down, inputs_up, inputs_down, slope, normed, grad_low, cotangent_here):
        reads = [
            copies.read(source, target)
            for source, target in (
                (cotangent, cotangent_here),
                (saved.normed.at[2], normed),
                (saved.inverse, inverse),
                (saved.rows, rows_all),
                (weights.down, down),
                (saved.slope, slope),
                (pairs.hidden_low, inputs_down),
                (pairs.low_two, inputs_up),
                (weights.up, up),
            )
        ]
        sends = []

        def third_norm():
            for copy in reads[:4]:
                copy.wait()
            small[...] = jnp.zeros_like(small)

            def upstream(rows):
                valid = jnp.concatenate([pair_column[rows, :]] * (width // 128), axis=1) >= 0
                return jnp.where(valid, cotangent_here[rows, :].astype(jnp.float32), 0.0)

            norm_back(2, 9, normed, upstream, grad_low)
            place.meet()
            sends.append(hand_over(grad_low, landed.down))

        size = 384
        half_width = hidden_width // 2

        def expand(other):
            if other:
                for copy in reads[4:6]:
                    copy.wait()

            def one(part, carry):
                column = (1 - core if other else core) * half_width + part * size
                number = column // size
                both = jnp.concatenate(
                    [matrix(down[side, number // 2, lax.rem(number, 2)]) for side in range(2)], axis=1
                )
                columns = pl.ds(pl.multiple_of(column, 128), size)
                value = dot(grad_low[...], both, (1, 1)) * slope[:, columns].astype(jnp.float32)
                value = value.astype(jnp.bfloat16)
                slope[:, columns] = value
                hidden_sum[pl.ds(0, 1), columns] = jnp.sum(value.astype(jnp.float32), axis=0, keepdims=True)
                return carry

            lax.fori_loop(0, half_width // size, one, 0)
            if other:
                sends.append(hand_over(slope, landed.up))

        def grad_down():
            reads[6].wait()
            sends[0].wait_recv()
            total = totals.down
            tall = 48
            count = total.shape[3] // tall
            units = [
                prepare("down", pl.ds(row * tall, tall), pl.ds(0, width // 2), count) for row in range(count)
            ]
            slab = hidden_width // line
            for z in range(line):
                span = pl.ds(z * slab, slab)
                value = weight_grad("down", inputs_down, grad_low, landed.down, pl.ds(0, width // 2), span)
                total[z] = value.reshape(total.shape[1:])
                clock.now += 1.0
                for unit in units:
                    unit.send_slab(z)
            schedule.flying.extend(units)

        def grad_up(part):
            if part == 0:
                reads[7].wait()
                sends[1].wait_recv()
                for k in range(4):
                    small[pl.ds(13 + k, 1), :] = hidden_sum[pl.ds(0, 1), pl.ds(k * width, width)]
            spread_columns("up", inputs_up, slope, pl.ds(part * size, size), half_width // size)

        def grad_second():
            reads[8].wait()
            for side in range(2):
                work[...] += dot(slope[:, pl.ds(side * half_width, half_width)], matrix(up[side]), (1, 1))

        task(2.0, third_norm)
        task(2.0, expand, True)
        task(0.0, grad_down)
        task(2.0, expand, False)
        for part in range(half_width // size):
            task(1.2, grad_up, part)
        task(3.0, grad_second)
        schedule.run(False)
        for copy in sends:
            copy.wait_send()

    def attentions(qkv_w, ckv_w, sout_w, cq_w, cout_w, left_one, left_two, patch_pair, normed, query, key_value,
                   cross_attention, keys_all, values_all, qkv, attention, scores_low, grad_two_low, grad_query,
                   grad_one_low, grad_context):
        order = (
            (saved.normed.at[1], normed.at[1]),
            (weights.cout, cout_w),
            (pairs.context_cross, left_one),
            (saved.key_value, key_value),
            (saved.cross_attention, cross_attention),
            (saved.query, query),
            (weights.cq, cq_w),
            (saved.normed.at[0], normed.at[0]),
            (pairs.low_one, left_two),
            (weights.sout, sout_w),
            (weights.ckv, ckv_w),
            (pairs.patches, patch_pair),
            (saved.qkv, qkv),
            (saved.attention.at[pl.ds(0, 2)], attention.at[0]),
            (weights.qkv, qkv_w),
        )
        reads = [copies.read(source, target) for source, target in order]
        waited = set()
        later = {}
        sends = {}
        size = 384
        third_part = pl.ds(0, width // 2)

        def need(*numbers):
            for number in numbers:
                if number not in waited:
                    reads[number].wait()
                    waited.add(number)

        def second_norm():
            need(0)
            norm_back(1, 8, normed.at[1], lambda rows: work[rows, :], grad_two_low)
            sends["t"] = hand_over(grad_two_low, landed.cout)

        def context_grad():
            need(1)
            grad_context[...] = dot(grad_two_low[...], whole(cout_w), (1, 1)).astype(jnp.bfloat16)

        def cross(offset):
            need(3, 4, 5)
            owner = place.ahead(offset)
            lane = lax.broadcasted_iota(jnp.int32, (keys, width), 1) // HD
            key_rows = key_value[owner, :, pl.ds(0, width)].astype(jnp.float32)
            value_rows = key_value[owner, :, pl.ds(width, width)].astype(jnp.float32)
            for head in range(H):
                rows = pl.ds(head * keys, keys)
                keys_all[rows, :] = jnp.where(lane == head, key_rows, 0.0).astype(jnp.bfloat16)
                values_all[rows, :] = jnp.where(lane == head, value_rows, 0.0).astype(jnp.bfloat16)
            rows = pl.ds(pl.multiple_of(owner * block, block), block)
            probability = cross_attention[owner].astype(jnp.float32).reshape(H, keys, block)
            grad = dot(values_all[...], grad_context[rows, :], (1, 1)).reshape(H, keys, block)
            grad = probability * (grad - jnp.sum(probability * grad, axis=1, keepdims=True))
            grad = grad.reshape(H * keys, block).astype(jnp.bfloat16)
            grad_query[rows, :] = (dot(grad, keys_all[...], (0, 0)) * scaling).astype(jnp.bfloat16)
            lane = lax.broadcasted_iota(jnp.int32, (keys, 128), 1)
            for pair in range(H // 2):
                columns = pl.ds(pair * 128, 128)
                heads = slice(pair * 2 * keys, (pair + 1) * 2 * keys)
                value = dot(grad[heads], query[rows, columns]) * scaling
                key_parts[offset, :, columns] = jnp.where(lane < HD, value[:keys], value[keys:]).astype(
                    jnp.bfloat16
                )
                value = dot(cross_attention[owner, pl.ds(heads.start, 2 * keys), :], grad_context[rows, columns])
                key_parts[offset, :, pl.ds(width + pair * 128, 128)] = jnp.where(
                    lane < HD, value[:keys], value[keys:]
                ).astype(jnp.bfloat16)
            if offset:
                there = key_landed, (offset - 1,)
                sends[offset] = copies.start((key_parts, (offset,)), there, place.along(offset), there)
            if offset == 0:
                sends["q"] = hand_over(grad_query, landed.cq)

        def grad_cout():
            need(2)
            sends["t"].wait_recv()
            spread_columns("cout", left_one, grad_two_low, third_part, 1)
            later["context"] = copies.read(pairs.context, left_one)

        def grad_first():
            need(6)
            work[...] += dot(grad_query[...], whole(cq_w), (1, 1))
            small[pl.ds(6, 1), :] = jnp.sum(grad_query[...].astype(jnp.float32), axis=0, keepdims=True)

        def first_norm():
            need(7)
            norm_back(0, 5, normed.at[0], lambda rows: work[rows, :], grad_one_low)
            sends["s"] = hand_over(grad_one_low, landed.sout)

        def grad_cq():
            need(8)
            sends["q"].wait_recv()
            spread_columns("cq", left_two, grad_query, third_part, 1)
            later["text"] = copies.read(pairs.text, left_two)

        def self_context():
            need(9)
            grad_context[...] = dot(grad_one_low[...], whole(sout_w), (1, 1)).astype(jnp.bfloat16)

        def grad_sout():
            later["context"].wait()
            sends["s"].wait_recv()
            spread_columns("sout", left_one, grad_one_low, third_part, 1)

        def key_grad():
            value = key_parts[0].astype(jnp.float32)
            for offset in range(1, line):
                sends[offset].wait_recv()
                value += key_landed[offset - 1].astype(jnp.float32)
            value = value.astype(jnp.bfloat16)
            grad_kv[...] = value
            sends["k"] = hand_over(grad_kv, landed.ckv)
            small[pl.ds(7, 1), :] = jnp.sum(value[:, width:].astype(jnp.float32), axis=0, keepdims=True)
            need(10)
            patch_grad[...] = dot(grad_kv[...], whole(ckv_w), (1, 1))

        def grad_ckv(part):
            if part == 0:
                need(11)
                sends["k"].wait_recv()
            spread_columns("ckv", patch_pair, grad_kv, pl.ds(part * size, size), 2)

        strip = 128

        def attend(pair):
            slot = pair % 2
            if pair == 0:
                need(12, 13)
            else:
                later[pair].wait()
            if pair + 1 < H // 2:
                later[pair + 1] = copies.read(
                    saved.attention.at[pl.ds(2 * pair + 2, 2)], attention.at[1 - slot]
                )
            columns, key_columns = pl.ds(pair * 128, 128), pl.ds(width + pair * 128, 128)
            value_columns = pl.ds(2 * width + pair * 128, 128)

            def own(value, head):
                lane = lax.broadcasted_iota(jnp.int32, value.shape, 1)
                return jnp.where((lane < HD) == (head == 0), value.astype(jnp.float32), 0.0).astype(jnp.bfloat16)

            def one(number, carry):
                rows = pl.ds(pl.multiple_of(number * strip, strip), strip)
                for head in range(2):
                    grad = dot(own(grad_context[rows, columns], head), qkv[:, value_columns], (1, 1))
                    probability = attention[slot, head, rows, :].astype(jnp.float32)
                    grad = probability * (grad - jnp.sum(probability * grad, axis=1, keepdims=True))
                    scores_low[head, rows, :] = grad.astype(jnp.bfloat16)
                return carry

            lax.fori_loop(0, tokens // strip, one, 0)
            query_grad = key_grad = value_grad = 0.0
            for head in range(2):
                query_grad += dot(scores_low[head], own(qkv[:, key_columns], head))
                key_grad += dot(scores_low[head], own(qkv[:, columns], head), (0, 0))
                value_grad += dot(attention[slot, head], own(grad_context[:, columns], head), (0, 0))
            query_grad = (query_grad * scaling).astype(jnp.bfloat16)
            value_grad = value_grad.astype(jnp.bfloat16)
            qkv[:, columns] = query_grad
            qkv[:, key_columns] = (key_grad * scaling).astype(jnp.bfloat16)
            qkv[:, value_columns] = value_grad
            small[pl.ds(3, 1), columns] = jnp.sum(query_grad.astype(jnp.float32), axis=0, keepdims=True)
            small[pl.ds(4, 1), columns] = jnp.sum(value_grad.astype(jnp.float32), axis=0, keepdims=True)
            if pair + 1 == H // 2:
                sends["p"] = hand_over(qkv, landed.qkv)
                schedule.launch(vectors)

        def grad_qkv(part):
            if part == 0:
                later["text"].wait()
                sends["p"].wait_recv()
            spread_columns("qkv", left_two, qkv, pl.ds(part * size, size), 3)

        def text_back(side):
            need(14)
            size = 3 * width // 2
            work[...] += dot(qkv[:, pl.ds(side * size, size)], matrix(qkv_w[side]), (1, 1))
            if side == 1:
                copies.write(work, text_grad)

        task(2.0, second_norm)
        task(1.0, context_grad)
        task(1.0, grad_cout)
        for offset in list(range(1, line)) + [0]:
            task(2.0, cross, offset)
        task(1.0, grad_first)
        task(2.0, first_norm)
        task(1.0, grad_cq)
        task(1.0, self_context)
        task(1.0, key_grad)
        task(1.0, grad_sout)
        for part in range(2):
            task(0.5, grad_ckv, part)
        for number in range(H // 2):
            task(2.5, attend, number)
        for part in range(3):
            task(1.2, grad_qkv, part)
        for side in range(2):
            task(1.5, text_back, side)
        schedule.run()
        for name in ("t", "q", "s", "k", "p"):
            sends[name].wait_send()

    place.greet()
    pair_column[...] = jnp.broadcast_to(pair_row[...].astype(jnp.float32), (128, tokens)).T
    low = jnp.bfloat16
    wide = (tokens, hidden_width)
    rows = (tokens, width)
    shape = lambda ref: pltpu.VMEM(ref.shape, ref.dtype)
    pl.run_scoped(
        feed_forward,
        shape(weights.up),
        shape(weights.down),
        shape(pairs.low_two),
        shape(pairs.hidden_low),
        pltpu.VMEM(wide, low),
        pltpu.VMEM(rows, jnp.float32),
        pltpu.VMEM(rows, low),
        pltpu.VMEM(rows, low),
    )
    pl.run_scoped(
        attentions,
        shape(weights.qkv),
        shape(weights.ckv),
        shape(weights.sout),
        shape(weights.cq),
        shape(weights.cout),
        shape(pairs.context),
        shape(pairs.context),
        shape(pairs.patches),
        pltpu.VMEM((2,) + rows, jnp.float32),
        shape(saved.query),
        shape(saved.key_value),
        shape(saved.cross_attention),
        pltpu.VMEM((H * keys, width), low),
        pltpu.VMEM((H * keys, width), low),
        shape(saved.qkv),
        pltpu.VMEM((2, 2, tokens, tokens), low),
        pltpu.VMEM((2, tokens, tokens), low),
        pltpu.VMEM(rows, low),
        pltpu.VMEM(rows, low),
        pltpu.VMEM(rows, low),
        pltpu.VMEM(rows, low),
    )
    device = place.z * 8 + place.f
    value = small[...]
    narrow, slim = gains_out.shape[1], hidden_out.shape[1]
    turned = pltpu.roll(value, lax.rem(width - device * narrow, width), 1)
    gains_out[...] = turned[:3, :narrow]
    biases_out[...] = turned[3:13, :narrow]
    number = lax.broadcasted_iota(jnp.int32, value.shape, 0)
    picked = jnp.sum(jnp.where(number == 13 + place.z, value, 0.0), axis=0, keepdims=True)
    picked = pltpu.roll(jnp.broadcast_to(picked, (8, width)), lax.rem(width - place.f * slim, width), 1)
    hidden_out[...] = picked[:1, :slim]
    for name in WEIGHTS:
        swaps[name].wait_recv()
        out = getattr(outs, name)
        mine, other = getattr(finals, name)[core], getattr(swapped, name)[...]
        middle = mine.shape[1]
        out[:, :middle] = jnp.where(core == 0, mine, other)
        out[:, middle:] = jnp.where(core == 0, other, mine)
    copies.finish()


def gathered(line, shards):
    return [(2, line, 2, 2, 2 * shard.shape[0], shard.shape[1] // 2) for shard in shards]


def forward_all(line, shards, vectors, text, patches, pair_row, region_row):
    tokens, width = text.shape
    keys, depth = patches.shape
    wide = shards[5].shape[1]
    low, full = jnp.bfloat16, jnp.float32
    rows = (tokens, width)
    kept = [
        ((tokens, 3 * width), low),
        ((H, tokens, tokens), low),
        (rows, low),
        ((line, keys, 2 * width), low),
        ((line, H * keys, tokens // line), low),
        ((3,) + rows, full),
        ((3, tokens, 128), full),
        ((tokens, wide), low),
        (rows, low),
        ((16, width), full),
    ]
    locals_ = [((8, wide), full), (rows, low), (rows, low), (rows, low), (rows, low), ((tokens, wide), low)]
    paired = [rows, (keys, depth), rows, rows, rows, rows, (tokens, wide)]
    shapes = gathered(line, shards)
    out_shape = [jax.ShapeDtypeStruct(shape, low) for shape in shapes]
    out_shape += [jax.ShapeDtypeStruct(*shape) for shape in kept]
    out_shape += [jax.ShapeDtypeStruct((2,) + shape, low) for shape in paired]
    scratch = [pltpu.VMEM(shape, low) for shape in shapes]
    for _ in range(2):
        scratch += [pltpu.VMEM((padded(shard.shape[0]), shard.shape[1] // 2), low) for shard in shards]
    scratch += [pltpu.VMEM(*shape) for shape in kept + locals_]
    scratch += [
        pltpu.VMEM((2, line, 2, 2, 16, 128), low),
        pltpu.VMEM((tokens, 128), full),
        pltpu.VMEM(rows, full),
        pltpu.VMEM((H * keys, width), low),
        pltpu.VMEM((H * keys, width), low),
        pltpu.SemaphoreType.DMA((160,)),
        pltpu.SemaphoreType.DMA((160,)),
        pltpu.SemaphoreType.DMA((96,)),
    ]
    outs = pl.pallas_call(
        functools.partial(forward_kernel, line),
        out_shape=out_shape,
        in_specs=[pl.BlockSpec(memory_space=pltpu.VMEM)] * (len(shards) + 5),
        out_specs=[pl.BlockSpec(memory_space=pl.ANY)] * len(out_shape),
        scratch_shapes=scratch,
        compiler_params=pltpu.CompilerParams(
            collective_id=0, has_side_effects=True, vmem_limit_bytes=62 * 2**20
        ),
    )(*shards, vectors, text, patches, pair_row, region_row)
    count = len(shards)
    return outs[:count], outs[count : count + len(kept)], outs[count + len(kept) :]


def backward_all(line, weights, saved, pairs, cotangent, pair_row, narrow, slim):
    low, full = jnp.bfloat16, jnp.float32
    tokens, width = cotangent.shape
    keys, depth = pairs[1].shape[1:]
    wide = pairs[-1].shape[2]
    sizes = [weight.shape[4:] for weight in weights]
    scratch = []
    for lead in ((line, 2, 2), (line, 2), (line,), (line - 1,)):
        scratch += [pltpu.VMEM(lead + size, low) for size in sizes]
    scratch += [pltpu.VMEM((2, size[0] // 2, size[1]), full) for size in sizes]
    scratch += [pltpu.VMEM((size[0] // 2, size[1]), full) for size in sizes]
    for name, size in zip(WEIGHTS, sizes):
        scratch.append(pltpu.VMEM((keys if name == "ckv" else tokens, size[1]), low))
    scratch += [
        pltpu.VMEM((tokens, width), full),
        pltpu.VMEM((3, tokens, 128), full),
        pltpu.VMEM((16, width), full),
        pltpu.VMEM((24, width), full),
        pltpu.VMEM((2 + line, 24, width), full),
        pltpu.VMEM((line, keys, 2 * width), low),
        pltpu.VMEM((line - 1, keys, 2 * width), low),
        pltpu.VMEM((tokens, 128), full),
        pltpu.VMEM((8, wide), full),
        pltpu.VMEM((keys, 2 * width), low),
        pltpu.SemaphoreType.DMA((160,)),
        pltpu.SemaphoreType.DMA((160,)),
        pltpu.SemaphoreType.DMA((64,)),
    ]
    out_shape = [jax.ShapeDtypeStruct((size[0] // 2, 2 * size[1]), full) for size in sizes]
    out_shape += [
        jax.ShapeDtypeStruct((tokens, width), full),
        jax.ShapeDtypeStruct((keys, depth), full),
        jax.ShapeDtypeStruct((3, narrow), full),
        jax.ShapeDtypeStruct((10, narrow), full),
        jax.ShapeDtypeStruct((1, slim), full),
    ]
    vmem, anywhere = pl.BlockSpec(memory_space=pltpu.VMEM), pl.BlockSpec(memory_space=pl.ANY)
    count = len(weights)
    outs = pl.pallas_call(
        functools.partial(backward_kernel, line),
        out_shape=out_shape,
        in_specs=[anywhere] * (count + len(saved) + len(pairs) + 1) + [vmem],
        out_specs=[vmem] * count + [anywhere] + [vmem] * 4,
        scratch_shapes=scratch,
        compiler_params=pltpu.CompilerParams(
            collective_id=1, has_side_effects=True, vmem_limit_bytes=63 * 2**20
        ),
    )(*weights, *saved, *pairs, cotangent, pair_row)
    return outs[:count], outs[count:]


def hand_out_kernel(count, *refs):
    semaphores = refs[-1]
    moves = [
        pltpu.make_async_copy(source, target, semaphores.at[number])
        for number, (source, target) in enumerate(zip(refs[:count], refs[count : 2 * count]))
    ]
    for move in moves:
        move.start()
    for move in moves:
        move.wait()


def hand_out(values):
    count = len(values)
    anywhere = pl.BlockSpec(memory_space=pl.ANY)
    return pl.pallas_call(
        functools.partial(hand_out_kernel, count),
        out_shape=[jax.ShapeDtypeStruct(value.shape, value.dtype) for value in values],
        in_specs=[anywhere] * count,
        out_specs=[pl.BlockSpec(memory_space=pltpu.VMEM)] * count,
        scratch_shapes=[pltpu.SemaphoreType.DMA((count,))],
        compiler_params=pltpu.CompilerParams(vmem_limit_bytes=63 * 2**20),
    )(*values)


def fast_body(
    text_rows,
    patches,
    row_pair,
    row_region,
    self_qkv,
    self_out,
    cross_query,
    cross_key_value,
    cross_out,
    ffn_up,
    ffn_down,
    norm_gains,
    biases,
    ffn_bias,
    cotangent,
):
    line = lax.axis_size("dp")
    narrow, slim = norm_gains.shape[1], ffn_bias.shape[0]
    vectors = jnp.concatenate(
        [
            jnp.pad(norm_gains, ((0, 0), (0, 128 - narrow))),
            jnp.pad(biases, ((0, 0), (0, 128 - narrow))),
            jnp.pad(ffn_bias[None], ((0, 2), (0, 128 - slim))),
        ],
        axis=0,
    )
    shards = (self_qkv, cross_key_value, self_out, cross_query, cross_out, ffn_up, ffn_down)
    pair_row = row_pair.reshape(1, -1)
    weights, kept, pairs = forward_all(
        line,
        shards,
        vectors,
        text_rows,
        patches.reshape(-1, patches.shape[2]),
        pair_row,
        row_region.reshape(1, -1),
    )
    joined = kept[8]
    saved = kept[:8] + kept[9:]
    grads, (text_grad, patch_grad, gains, shifts, hidden) = backward_all(
        line, weights, saved, pairs, cotangent, pair_row, narrow, slim
    )
    results = hand_out((joined, text_grad, patch_grad, gains, shifts, hidden, *grads))
    joined, text_grad, patch_grad, gains, shifts, hidden, *grads = results
    grad_qkv, grad_ckv, grad_sout, grad_cq, grad_cout, grad_up, grad_down = grads
    return (
        joined,
        text_grad,
        patch_grad.reshape(patches.shape),
        grad_qkv,
        grad_sout,
        grad_cq,
        grad_ckv,
        grad_cout,
        grad_up,
        grad_down,
        gains,
        shifts,
        hidden.reshape(-1),
    )


def body(
    text_rows,
    patches,
    row_pair,
    row_region,
    self_qkv,
    self_out,
    cross_query,
    cross_key_value,
    cross_out,
    ffn_up,
    ffn_down,
    norm_gains,
    biases,
    ffn_bias,
    cotangent,
):
    weight_qkv, weight_sout, weight_cq, weight_ckv, weight_cout, gains_all, bias_all = (
        lax.all_gather(self_qkv, ("dp", "fsdp"), axis=0, tiled=True),
        lax.all_gather(self_out, ("dp", "fsdp"), axis=0, tiled=True),
        lax.all_gather(cross_query, ("dp", "fsdp"), axis=0, tiled=True),
        lax.all_gather(cross_key_value, ("dp", "fsdp"), axis=0, tiled=True),
        lax.all_gather(cross_out, ("dp", "fsdp"), axis=0, tiled=True),
        lax.all_gather(norm_gains, ("dp", "fsdp"), axis=1, tiled=True),
        lax.all_gather(biases, ("dp", "fsdp"), axis=1, tiled=True),
    )
    weight_up, weight_down, bias_up_all = (
        lax.all_gather(ffn_up, ("dp", "fsdp"), axis=0, tiled=True),
        lax.all_gather(ffn_down, ("dp", "fsdp"), axis=0, tiled=True),
        lax.all_gather(ffn_bias, ("dp", "fsdp"), axis=0, tiled=True),
    )
    gains = gains_all.astype(jnp.float32)
    bias_rows = bias_all.astype(jnp.float32)
    bias_hidden = bias_up_all.astype(jnp.float32)
    row_count, model_width = text_rows.shape
    owners = lax.axis_size("dp")
    block_rows = row_count // owners
    valid = (row_pair >= 0)[:, None]
    patch_rows = patches.reshape(-1, patches.shape[2])
    kv_projected = jnp.dot(patch_rows, weight_ckv, preferred_element_type=jnp.float32)
    key_local = kv_projected[:, :model_width].astype(jnp.bfloat16)
    value_local = (kv_projected[:, model_width:] + bias_rows[4]).astype(jnp.bfloat16)
    keys_count = key_local.shape[0]
    kept_self, context_self = self_forward(
        text_rows, row_pair, weight_qkv, bias_rows[0], bias_rows[1]
    )
    branch_self = (
        jnp.dot(context_self, weight_sout, preferred_element_type=jnp.float32) + bias_rows[2]
    )
    first, normed_one, inverse_one = norm_forward(
        text_rows.astype(jnp.float32) + branch_self, gains[0], bias_rows[7]
    )
    first_low = first.astype(jnp.bfloat16)
    queries = (
        jnp.dot(first_low, weight_cq, preferred_element_type=jnp.float32) + bias_rows[3]
    ).astype(jnp.bfloat16)
    region_blocks = row_region.reshape(owners, block_rows)
    arrived, arrived_region = (
        lax.all_to_all(
            queries.reshape(owners, block_rows, model_width),
            "dp",
            split_axis=0,
            concat_axis=0,
            tiled=True,
        ),
        lax.all_to_all(region_blocks, "dp", split_axis=0, concat_axis=0, tiled=True),
    )
    arrived = arrived.reshape(1, owners * block_rows, H, HD)
    arrived_region = arrived_region.reshape(1, owners * block_rows)
    key_view = key_local.reshape(1, keys_count, H, HD)
    value_view = value_local.reshape(1, keys_count, H, HD)
    logsum_cross, context_owner = cross_forward(arrived, key_view, value_view, arrived_region)
    context_cross = lax.all_to_all(
        context_owner.reshape(owners, block_rows, model_width),
        "dp",
        split_axis=0,
        concat_axis=0,
        tiled=True,
    ).reshape(row_count, model_width)
    branch_cross = (
        jnp.dot(context_cross, weight_cout, preferred_element_type=jnp.float32) + bias_rows[5]
    )
    second, normed_two, inverse_two = norm_forward(first + branch_cross, gains[1], bias_rows[8])
    second_low = second.astype(jnp.bfloat16)
    hidden_pre = jnp.dot(second_low, weight_up, preferred_element_type=jnp.float32) + bias_hidden
    hidden_low = gelu_exact(hidden_pre).astype(jnp.bfloat16)
    branch_ffn = jnp.dot(hidden_low, weight_down, preferred_element_type=jnp.float32) + bias_rows[6]
    result, normed_three, inverse_three = norm_forward(second + branch_ffn, gains[2], bias_rows[9])
    joined_text = jnp.where(valid, result, 0.0).astype(jnp.bfloat16)
    upstream = jnp.where(valid, cotangent.astype(jnp.float32), 0.0)
    grad_three, grad_gain_three, grad_shift_three = norm_backward(
        upstream, normed_three, inverse_three, gains[2]
    )
    grad_ffn = grad_three.astype(jnp.bfloat16)
    grad_hidden = times_transpose(grad_ffn, weight_down)
    grad_pre = jax.vjp(gelu_exact, hidden_pre)[1](grad_hidden)[0].astype(jnp.bfloat16)
    ffn_terms = (
        transpose_times(second_low, grad_pre),
        transpose_times(hidden_low, grad_ffn),
        jnp.sum(grad_pre, axis=0, dtype=jnp.float32),
    )
    grad_up, grad_down, grad_up_bias = (
        lax.psum_scatter(ffn_terms[0], ("dp", "fsdp"), scatter_dimension=0, tiled=True),
        lax.psum_scatter(ffn_terms[1], ("dp", "fsdp"), scatter_dimension=0, tiled=True),
        lax.psum_scatter(ffn_terms[2], ("dp", "fsdp"), scatter_dimension=0, tiled=True),
    )
    grad_second = grad_three + times_transpose(grad_pre, weight_up)
    grad_two, grad_gain_two, grad_shift_two = norm_backward(
        grad_second, normed_two, inverse_two, gains[1]
    )
    grad_cross = grad_two.astype(jnp.bfloat16)
    grad_context = times_transpose(grad_cross, weight_cout).astype(jnp.bfloat16)
    grad_arrived = lax.all_to_all(
        grad_context.reshape(owners, block_rows, model_width),
        "dp",
        split_axis=0,
        concat_axis=0,
        tiled=True,
    ).reshape(1, owners * block_rows, H, HD)
    grad_query_owner, grad_key, grad_value = cross_backward(
        arrived, key_view, value_view, arrived_region, logsum_cross, grad_arrived
    )
    grad_queries = lax.all_to_all(
        grad_query_owner.astype(jnp.bfloat16).reshape(owners, block_rows, model_width),
        "dp",
        split_axis=0,
        concat_axis=0,
        tiled=True,
    ).reshape(row_count, model_width)
    grad_key_total = grad_key.reshape(keys_count, model_width)
    grad_value_total = grad_value.reshape(keys_count, model_width)
    grad_kv = jnp.concatenate(
        [grad_key_total.astype(jnp.bfloat16), grad_value_total.astype(jnp.bfloat16)], axis=1
    )
    patch_grad = times_transpose(grad_kv, weight_ckv).reshape(patches.shape)
    grad_ckv = transpose_times(patch_rows, grad_kv)
    grad_cross_value_bias = jnp.sum(grad_kv[:, model_width:], axis=0, dtype=jnp.float32)
    grad_first = grad_two + times_transpose(grad_queries, weight_cq)
    grad_cq = transpose_times(first_low, grad_queries)
    grad_cout = transpose_times(context_cross, grad_cross)
    grad_one, grad_gain_one, grad_shift_one = norm_backward(
        grad_first, normed_one, inverse_one, gains[0]
    )
    grad_self = grad_one.astype(jnp.bfloat16)
    grad_sout = transpose_times(context_self, grad_self)
    grad_context_self = times_transpose(grad_self, weight_sout).astype(jnp.bfloat16)
    grad_projected = self_backward(kept_self, grad_context_self)
    grad_qkv = transpose_times(text_rows, grad_projected)
    text_grad = grad_one + times_transpose(grad_projected, weight_qkv)
    gain_terms = jnp.stack([grad_gain_one, grad_gain_two, grad_gain_three])
    bias_terms = jnp.stack(
        [
            jnp.sum(grad_projected[:, :model_width], axis=0, dtype=jnp.float32),
            jnp.sum(grad_projected[:, 2 * model_width :], axis=0, dtype=jnp.float32),
            jnp.sum(grad_self, axis=0, dtype=jnp.float32),
            jnp.sum(grad_queries, axis=0, dtype=jnp.float32),
            grad_cross_value_bias,
            jnp.sum(grad_cross, axis=0, dtype=jnp.float32),
            jnp.sum(grad_ffn, axis=0, dtype=jnp.float32),
            grad_shift_one,
            grad_shift_two,
            grad_shift_three,
        ]
    )
    attn_terms = (grad_qkv, grad_sout, grad_cq, grad_ckv, grad_cout, gain_terms, bias_terms)
    shard_qkv, shard_sout, shard_cq, shard_ckv, shard_cout, shard_gains, shard_biases = (
        lax.psum_scatter(attn_terms[0], ("dp", "fsdp"), scatter_dimension=0, tiled=True),
        lax.psum_scatter(attn_terms[1], ("dp", "fsdp"), scatter_dimension=0, tiled=True),
        lax.psum_scatter(attn_terms[2], ("dp", "fsdp"), scatter_dimension=0, tiled=True),
        lax.psum_scatter(attn_terms[3], ("dp", "fsdp"), scatter_dimension=0, tiled=True),
        lax.psum_scatter(attn_terms[4], ("dp", "fsdp"), scatter_dimension=0, tiled=True),
        lax.psum_scatter(attn_terms[5], ("dp", "fsdp"), scatter_dimension=1, tiled=True),
        lax.psum_scatter(attn_terms[6], ("dp", "fsdp"), scatter_dimension=1, tiled=True),
    )
    return (
        joined_text,
        text_grad,
        patch_grad,
        shard_qkv,
        shard_sout,
        shard_cq,
        shard_ckv,
        shard_cout,
        grad_up,
        grad_down,
        shard_gains,
        shard_biases,
        grad_up_bias,
    )


def solution(mesh):
    in_specs = (
        P(("dp", "fsdp"), None),
        P(("dp", "fsdp"), None, None),
        P(("dp", "fsdp")),
        P(("dp", "fsdp")),
        P(("dp", "fsdp"), None),
        P(("dp", "fsdp"), None),
        P(("dp", "fsdp"), None),
        P(("dp", "fsdp"), None),
        P(("dp", "fsdp"), None),
        P(("dp", "fsdp"), None),
        P(("dp", "fsdp"), None),
        P(None, ("dp", "fsdp")),
        P(None, ("dp", "fsdp")),
        P(("dp", "fsdp")),
        P(("dp", "fsdp"), None),
    )
    out_specs = (
        P(("dp", "fsdp"), None),
        P(("dp", "fsdp"), None),
        P(("dp", "fsdp"), None, None),
        P(("dp", "fsdp"), None),
        P(("dp", "fsdp"), None),
        P(("dp", "fsdp"), None),
        P(("dp", "fsdp"), None),
        P(("dp", "fsdp"), None),
        P(("dp", "fsdp"), None),
        P(("dp", "fsdp"), None),
        P(None, ("dp", "fsdp")),
        P(None, ("dp", "fsdp")),
        P(("dp", "fsdp")),
    )
    fast = mesh.shape["fsdp"] == 8
    chosen = fast_body if fast else body
    return jax.shard_map(chosen, mesh=mesh, in_specs=in_specs, out_specs=out_specs, check_vma=False)
```

```python
import functools
import math
import types

import jax
import jax.numpy as jnp
from jax import lax
from jax.experimental import pallas as pl
from jax.experimental.pallas import tpu as pltpu
from jax.sharding import PartitionSpec as P

H = 12
HD = 64
PR = 32
BLK = 512


EPSILON = 1e-06
NEGATIVE = -1e30


def times_transpose(left, right):
    return lax.dot_general(
        left, right, (((1,), (1,)), ((), ())), preferred_element_type=jnp.float32
    )


def transpose_times(left, right):
    return lax.dot_general(
        left, right, (((0,), (0,)), ((), ())), preferred_element_type=jnp.float32
    )


def gelu_exact(values):
    return jax.nn.gelu(values, approximate=False)


def norm_forward(summed, gain_row, shift_row):
    center = summed - jnp.mean(summed, axis=-1, keepdims=True)
    inverse = lax.rsqrt(jnp.mean(center * center, axis=-1, keepdims=True) + EPSILON)
    normed = center * inverse
    return (normed * gain_row + shift_row, normed, inverse)


def norm_backward(upstream, normed, inverse, gain_row):
    scaled = upstream * gain_row
    centered = (
        scaled
        - jnp.mean(scaled, axis=-1, keepdims=True)
        - normed * jnp.mean(scaled * normed, axis=-1, keepdims=True)
    )
    return (inverse * centered, jnp.sum(upstream * normed, axis=0), jnp.sum(upstream, axis=0))


def self_scores(query_rows, key_rows, segment):
    scores = jnp.einsum(
        "qhd,khd->hqk", query_rows, key_rows, preferred_element_type=jnp.float32
    ) * (1.0 / math.sqrt(HD))
    same_pair = segment[:, None] == segment[None, :]
    return jnp.where(same_pair[None], scores, NEGATIVE)


def self_window(window):
    query_rows, key_rows, value_rows, segment = window
    scores = self_scores(query_rows, key_rows, segment)
    highest = jnp.max(scores, axis=-1, keepdims=True)
    logsum = highest + jnp.log(jnp.sum(jnp.exp(scores - highest), axis=-1, keepdims=True))
    weights = jnp.exp(scores - logsum).astype(jnp.bfloat16)
    context = jnp.einsum("hqk,khd->qhd", weights, value_rows, preferred_element_type=jnp.float32)
    return (logsum, context.astype(jnp.bfloat16))


def self_window_back(window):
    query_rows, key_rows, value_rows, segment, logsum, grad_rows = window
    probability = jnp.exp(self_scores(query_rows, key_rows, segment) - logsum)
    grad_prob = jnp.einsum(
        "qhd,khd->hqk", grad_rows, value_rows, preferred_element_type=jnp.float32
    )
    grad_score = (
        probability * (grad_prob - jnp.sum(probability * grad_prob, axis=-1, keepdims=True))
    ).astype(jnp.bfloat16)
    scaling = 1.0 / math.sqrt(HD)
    grad_query = (
        jnp.einsum("hqk,khd->qhd", grad_score, key_rows, preferred_element_type=jnp.float32)
        * scaling
    )
    grad_key = (
        jnp.einsum("hqk,qhd->khd", grad_score, query_rows, preferred_element_type=jnp.float32)
        * scaling
    )
    grad_value = jnp.einsum(
        "hqk,qhd->khd",
        probability.astype(jnp.bfloat16),
        grad_rows,
        preferred_element_type=jnp.float32,
    )
    return jnp.concatenate(
        [grad_query.reshape(BLK, -1), grad_key.reshape(BLK, -1), grad_value.reshape(BLK, -1)],
        axis=1,
    ).astype(jnp.bfloat16)


def self_forward(text_rows, segment, weight_qkv, bias_query, bias_value):
    row_count, model_width = text_rows.shape
    blocks = row_count // BLK
    projected = jnp.dot(text_rows, weight_qkv, preferred_element_type=jnp.float32)
    query_rows = (
        (projected[:, :model_width] + bias_query).astype(jnp.bfloat16).reshape(blocks, BLK, H, HD)
    )
    key_rows = (
        projected[:, model_width : 2 * model_width].astype(jnp.bfloat16).reshape(blocks, BLK, H, HD)
    )
    value_rows = (
        (projected[:, 2 * model_width :] + bias_value)
        .astype(jnp.bfloat16)
        .reshape(blocks, BLK, H, HD)
    )
    segment = segment.reshape(blocks, BLK)
    logsum, context = lax.map(self_window, (query_rows, key_rows, value_rows, segment))
    return (
        (query_rows, key_rows, value_rows, segment, logsum),
        context.reshape(row_count, model_width),
    )


def self_backward(kept_self, grad_context):
    query_rows, key_rows, value_rows, segment, logsum = kept_self
    blocks = query_rows.shape[0]
    grad_rows = grad_context.reshape(blocks, BLK, H, HD)
    grad_projected = lax.map(
        self_window_back, (query_rows, key_rows, value_rows, segment, logsum, grad_rows)
    )
    return grad_projected.reshape(blocks * BLK, -1)


def cross_scores(query_rows, key_rows, region_rows):
    scores = jnp.einsum(
        "bkhd,brhd->bhkr", key_rows, query_rows, preferred_element_type=jnp.float32
    ) * (1.0 / math.sqrt(HD))
    key_region = lax.broadcasted_iota(jnp.int32, (key_rows.shape[1], 1), 0) // PR
    same_region = key_region[None] == region_rows[:, None, :]
    return jnp.where(same_region[:, None], scores, NEGATIVE)


def cross_forward(query_rows, key_rows, value_rows, region_rows):
    scores = cross_scores(query_rows, key_rows, region_rows)
    highest = jnp.max(scores, axis=2, keepdims=True)
    logsum = highest + jnp.log(jnp.sum(jnp.exp(scores - highest), axis=2, keepdims=True))
    weights = jnp.exp(scores - logsum).astype(jnp.bfloat16)
    context = jnp.einsum("bhkr,bkhd->brhd", weights, value_rows, preferred_element_type=jnp.float32)
    return (logsum, context.astype(jnp.bfloat16))


def cross_backward(query_rows, key_rows, value_rows, region_rows, logsum, grad_context):
    probability = jnp.exp(cross_scores(query_rows, key_rows, region_rows) - logsum)
    grad_prob = jnp.einsum(
        "bkhd,brhd->bhkr", value_rows, grad_context, preferred_element_type=jnp.float32
    )
    grad_score = (
        probability * (grad_prob - jnp.sum(probability * grad_prob, axis=2, keepdims=True))
    ).astype(jnp.bfloat16)
    scaling = 1.0 / math.sqrt(HD)
    grad_query = (
        jnp.einsum("bhkr,bkhd->brhd", grad_score, key_rows, preferred_element_type=jnp.float32)
        * scaling
    )
    grad_key = (
        jnp.einsum("bhkr,brhd->bkhd", grad_score, query_rows, preferred_element_type=jnp.float32)
        * scaling
    )
    grad_value = jnp.einsum(
        "bhkr,brhd->bkhd",
        probability.astype(jnp.bfloat16),
        grad_context,
        preferred_element_type=jnp.float32,
    )
    return (grad_query, grad_key, grad_value)


MESH = pl.DeviceIdType.MESH
WEIGHTS = ("qkv", "ckv", "sout", "cq", "cout", "up", "down")
CORE_LINK = 400e3


def named(names, refs):
    return types.SimpleNamespace(**dict(zip(names, refs)))


class Place:
    def __init__(self, line):
        self.line = line
        self.z = lax.axis_index("dp")
        self.f = lax.axis_index("fsdp")
        self.core = lax.rem(self.f, 2)
        self.x = lax.rem(self.f // 2, 2)
        self.y = self.f // 4
        self.other = {"c": 1 - self.core, "x": 1 - self.x, "y": 1 - self.y}
        steps = {"c": 1 - 2 * self.core, "x": 2 - 4 * self.x, "y": 4 - 8 * self.y}
        self.neighbours = {axis: self.f + step for axis, step in steps.items()}
        self.onward = [lax.rem(self.z + k, line) for k in range(line)]
        self.backward = [lax.rem(self.z + line - k, line) for k in range(line)]

    def across(self, axis):
        return (self.z, self.neighbours[axis])

    def along(self, offset):
        return (self.onward[offset], self.f)

    def ahead(self, offset):
        return self.onward[offset]

    def behind(self, offset):
        return self.backward[offset]

    def greet(self):
        barrier = pltpu.get_barrier_semaphore()
        partners = [self.across(axis) for axis in "cxy"] + [self.along(k) for k in range(1, self.line)]
        for device in partners:
            pl.semaphore_signal(barrier, inc=1, device_id=device, device_id_type=MESH)

    def meet(self):
        pl.semaphore_wait(pltpu.get_barrier_semaphore(), 2 + self.line)

    def block(self, whole):
        return tuple(slice(None) if axis in whole else getattr(self, axis) for axis in "zyx")


def spot(place):
    return place[0].at[place[1]] if isinstance(place, tuple) else place


class Copy:
    def __init__(self, make):
        self.make = make

    def wait_recv(self):
        self.make(True).wait_recv()

    def wait_send(self):
        self.make(False).wait_send()

    def wait(self):
        self.wait_send()
        self.wait_recv()


class LocalCopy(Copy):
    def wait(self):
        self.make(False).wait()


class Copies:
    def __init__(self, sent, received, local):
        self.sent, self.received, self.local = sent, received, local
        self.count = self.local_count = 0
        self.open = []
        self.writes = []

    def start(self, source, target, device, landing, remember=True):
        number = self.count
        self.count += 1
        copy = Copy(
            lambda arriving: pltpu.make_async_remote_copy(
                src_ref=spot(source),
                dst_ref=spot(landing if arriving else target),
                send_sem=self.sent.at[number],
                recv_sem=self.received.at[number],
                device_id=device,
                device_id_type=MESH,
            )
        )
        copy.make(False).start()
        if remember:
            self.open.append(copy)
        return copy

    def read(self, source, target):
        number = self.local_count
        self.local_count += 1
        copy = LocalCopy(
            lambda arriving: pltpu.make_async_copy(spot(source), spot(target), self.local.at[number])
        )
        copy.make(False).start()
        return copy

    def write(self, source, target):
        self.writes.append(self.read(source, target))

    def finish(self):
        for copy in self.writes:
            copy.wait()
        for copy in self.open:
            copy.wait_send()


class Clock:
    def __init__(self, link, hop, far, slack, scale):
        self.scale = scale
        self.link, self.hop, self.far, self.slack = link, hop, far, slack
        self.now = 0.0
        self.free = dict.fromkeys("czyx", 0.0)

    def send(self, axis, size):
        rate = CORE_LINK if axis == "c" else self.link
        start = max(self.now, self.free[axis])
        self.free[axis] = start + size / rate
        return self.free[axis] + (1.5 if axis == "c" else self.far if axis == "z" else self.hop)


def volume(shape):
    return 2 * math.prod(shape)


class GatherUnit:
    def __init__(self, place, copies, clock, buffer, rows, columns, order):
        self.place, self.copies, self.clock, self.buffer = place, copies, clock, buffer
        self.area, self.order = (rows, columns), order + "c"
        self.held, self.stage, self.arrivals = "", 0, []
        self.size = volume((rows.size, columns.size))

    def view(self, index, half=None):
        half = self.place.core if half is None else half
        return self.buffer, (half,) + index + self.area

    def send(self):
        place = self.place
        axis = self.order[self.stage]
        mine = place.block(self.held)
        blocks = math.prod({"z": place.line, "y": 2, "x": 2}[held] for held in self.held)
        if axis == "z":
            moves = [(place.along(k), (place.behind(k),) + mine[1:], None) for k in range(1, place.line)]
            blocks *= place.line
        elif axis == "c":
            moves = [(place.across(axis), mine, place.other["c"])]
        else:
            level = "zyx".index(axis)
            moves = [(place.across(axis), mine[:level] + (place.other[axis],) + mine[level + 1 :], None)]
        self.arrivals = [
            self.copies.start(self.view(mine), self.view(mine), device, self.view(theirs, half))
            for device, theirs, half in moves
        ]
        self.due = self.clock.send(axis, blocks * self.size)
        self.held += axis
        self.stage += 1

    def step(self):
        for copy in self.arrivals:
            copy.wait_recv()
        self.clock.now = max(self.clock.now, self.due) + 0.1
        if self.stage == len(self.order):
            return True
        if self.stage == 1:
            self.begin()
        self.send()
        return False


class SumUnit:
    def __init__(self, place, copies, clock, total, landings, result, rows, columns, order):
        self.place, self.copies, self.clock, self.total = place, copies, clock, total
        self.landings, self.result, self.order = landings, result, order
        self.area = (rows, columns)
        self.left, self.stage, self.arrivals = "zyx", 0, []
        self.size = volume((rows.size, columns.size))

    def send(self):
        place, area, stage = self.place, self.area, self.stage
        axis = self.order[stage]
        mine = place.block(self.left)
        level = "zyx".index(axis)
        landing = self.landings[stage]
        self.left = self.left.replace(axis, "")
        each = math.prod({"z": place.line, "y": 2, "x": 2}[left] for left in self.left)
        blocks = each
        if axis == "z":
            moves = []
            for offset in range(1, place.line):
                span = pl.ds((offset - 1) * each, each) if each > 1 else offset - 1
                moves.append((place.along(offset), place.ahead(offset), span))
            blocks *= place.line
        else:
            span = pl.ds(0, each) if each > 1 else 0
            if stage == 0:
                span = (pl.ds(0, place.line), pl.ds(0, 2))
            moves = [(place.across(axis), place.other[axis], span)]
        self.arrivals = []
        for device, goal, span in moves:
            there = landing, (span if isinstance(span, tuple) else (span,)) + area
            source = self.total, mine[:level] + (goal,) + mine[level + 1 :] + area
            self.arrivals.append(self.copies.start(source, there, device, there))
        self.due = self.clock.send(axis, blocks * self.size)
        self.axis = axis
        self.stage += 1

    def send_slab(self, z):
        place, axis = self.place, self.order[0]
        index = (z, place.other[axis], slice(None)) if axis == "y" else (z, slice(None), place.other[axis])
        there = self.landings[0], (z, slice(None)) + self.area
        self.arrivals.append(
            self.copies.start((self.total, index + self.area), there, place.across(axis), there)
        )
        self.due = self.clock.send(axis, 2 * self.size)
        if z == place.line - 1:
            self.left = self.left.replace(axis, "")
            self.axis, self.stage = axis, 1

    def step(self):
        for copy in self.arrivals:
            copy.wait_recv()
        self.clock.now = max(self.clock.now, self.due) + 0.2
        place, area, landing, line = self.place, self.area, self.landings[self.stage - 1], self.place.line

        def add(index, spots):
            value = self.total[index + area].astype(jnp.float32)
            for one in spots:
                value += landing[one + area].astype(jnp.float32)
            return value

        def store(index, spots):
            self.total[index + area] = add(index, spots).astype(jnp.bfloat16)

        if self.stage == 3:
            count = line - 1 if self.axis == "z" else 1
            value = add((place.z, place.y, place.x), [(k,) for k in range(count)])
            put_halves(self.result, area, value)
            return True
        if self.stage == 1:

            def one(z, carry):
                for other in range(2):
                    store((z, place.y, other) if self.axis == "y" else (z, other, place.x), [(z, other)])
                return carry

            lax.fori_loop(0, line, one, 0)
        elif self.axis == "z":
            for other in range(2):
                index = (place.z, place.y, other) if self.left == "x" else (place.z, other, place.x)
                store(index, [(k * 2 + other,) for k in range(line - 1)])
        else:

            def one(z, carry):
                store((z, place.y, place.x), [(z,)])
                return carry

            lax.fori_loop(0, line, one, 0)
        self.send()
        return False


def put_halves(final, area, value):
    rows, columns = area
    half = final.shape[1]
    done = 0
    while done < rows.size:
        core, at = (rows.start + done) // half, (rows.start + done) % half
        step = min(rows.size - done, half - at)
        final[core, pl.ds(at, step), columns] = value[done : done + step]
        done += step


class Schedule:
    def __init__(self, clock, done):
        self.clock, self.done = clock, done
        self.tasks, self.flying = [], []

    def task(self, cost, function, *arguments, ready=lambda: True):
        self.tasks.append((cost, functools.partial(function, *arguments), ready))

    def launch(self, unit):
        unit.send()
        self.flying.append(unit)

    def run(self, drain=True):
        while self.tasks or (drain and self.flying):
            soonest = min(self.flying, key=lambda unit: unit.due) if self.flying else None
            runnable = self.tasks and self.tasks[0][2]()
            if soonest is not None and (soonest.due + self.clock.slack <= self.clock.now or not runnable):
                if soonest.step():
                    self.flying.remove(soonest)
                    self.done(soonest)
            else:
                cost, function, _ = self.tasks.pop(0)
                function()
                self.clock.now += cost * self.clock.scale


def padded(rows):
    return -(-rows // 16) * 16


def matrix(value):
    return value.reshape(-1, value.shape[-1])


def dot(left, right, contract=(1, 0)):
    return lax.dot_general(
        left, right, (((contract[0],), (contract[1],)), ((), ())), preferred_element_type=jnp.float32
    )


def whole(buffer):
    return jnp.concatenate([matrix(buffer[0]), matrix(buffer[1])], axis=1)


def column_spans(rows, columns):
    wide = 384 if rows <= 64 else 128
    return [pl.ds(column, wide) for column in range(0, columns, wide)]


def row_spans(rows):
    tall = rows
    return [pl.ds(row, tall) for row in range(0, rows, tall)]


def merged_rows(place, mine, other):
    mine, other = mine.astype(jnp.float32), other.astype(jnp.float32)
    first = jnp.where(place.core == 0, mine, other)
    second = jnp.where(place.core == 0, other, mine)
    return jnp.concatenate([first, second], axis=0).astype(jnp.bfloat16)


def column_half(place, values, own):
    half = values.shape[1] // 2
    left, right = values[:, :half].astype(jnp.float32), values[:, half:].astype(jnp.float32)
    return jnp.where((place.core == 0) == own, left, right)

def gelu_pair(values):
    half_square = jnp.exp(values * values * -0.5)
    size = jnp.abs(values)
    t = 1.0 / (1.0 + (0.3275911 * math.sqrt(0.5)) * size)
    series = t * (
        0.5 * 0.254829592
        + t * (-0.5 * 0.284496736 + t * (0.5 * 1.421413741 + t * (-0.5 * 1.453152027 + t * (0.5 * 1.061405429))))
    )
    tail = series * half_square
    phi = jnp.where(values < 0, tail, 1.0 - tail)
    slope = phi + values * half_square * (1.0 / math.sqrt(2.0 * math.pi))
    return values * phi, slope


def spread_vectors(vectors_all, rows_out, hidden_out, narrow, wide, line):
    lanes = lax.broadcasted_iota(jnp.int32, (16, 128), 1)
    sums = {id(rows_out): {}, id(hidden_out): {}}

    def place(target, values, start, size):
        found = sums[id(target)]
        tile, shift = start // 128, start % 128
        rolled = pltpu.roll(values, shift, 1) if shift else values
        lane = lanes[: values.shape[0]]
        first = jnp.where((lane >= shift) & (lane < shift + size), rolled, 0.0)
        found[tile] = found[tile] + first if tile in found else first
        if shift + size > 128:
            second = jnp.where(lane < shift + size - 128, rolled, 0.0)
            tile += 1
            found[tile] = found[tile] + second if tile in found else second

    for z in range(line):
        for y in range(2):
            for x in range(2):
                for core in range(2):
                    device = ((z * 2 + y) * 2 + x) * 2 + core
                    values = vectors_all[core, z, y, x].astype(jnp.float32)
                    place(rows_out, values, device * narrow, narrow)
                    place(hidden_out, values[8:], device * wide, wide)
    for target in (rows_out, hidden_out):
        for tile, value in sums[id(target)].items():
            target[:, pl.ds(tile * 128, 128)] = value

KEPT = ("qkv", "attention", "query", "key_value", "cross_attention", "normed", "inverse", "slope", "joined", "rows")
PAIRS = ("text", "patches", "context", "low_one", "context_cross", "low_two", "hidden_low")
LOCAL = ("hidden", "context", "low_one", "context_cross", "low_two", "hidden_low")


def forward_kernel(line, *refs):
    refs = list(refs)
    take = lambda names: named(names, [refs.pop(0) for _ in names])
    shards = take(WEIGHTS)
    gains, shifts, slim_bias, text, patches, pair_row, region_row = [refs.pop(0) for _ in range(7)]
    outs, kept_out, pairs = take(WEIGHTS), take(KEPT), take(PAIRS)
    buffers, outgoing, incoming = take(WEIGHTS), take(WEIGHTS), take(WEIGHTS)
    kept = named(KEPT + LOCAL, [refs.pop(0) for _ in KEPT + LOCAL])
    vectors, vectors_all, pair_column, work, keys_all, values_all, sent, received, local = refs
    place = Place(line)
    copies = Copies(sent, received, local)
    clock = Clock(55e3, 1.5, 4.5, -0.5, 1.0)
    tokens, width = text.shape
    rows_all, hidden_all = kept.rows, kept.hidden
    block = tokens // line
    narrow = shards.qkv.shape[0]
    keys = patches.shape[0]
    place.greet()
    for name in WEIGHTS:
        shard, target = getattr(shards, name), getattr(outgoing, name)
        away = column_half(place, shard[...], False)
        padding = target.shape[0] - shard.shape[0]
        if padding:
            away = jnp.concatenate([away, jnp.zeros((padding, away.shape[1]), jnp.float32)], axis=0)
        target[...] = away.astype(jnp.bfloat16)
    vectors[...] = jnp.zeros_like(vectors)
    vectors[pl.ds(0, 3), pl.ds(0, narrow)] = gains[...].astype(jnp.float32)
    vectors[pl.ds(3, 10), pl.ds(0, narrow)] = shifts[...].astype(jnp.float32)
    vectors[pl.ds(13, 1), pl.ds(0, slim_bias.shape[1])] = slim_bias[...].astype(jnp.float32)
    vectors_all[place.core, place.z, place.y, place.x] = vectors[...].astype(jnp.bfloat16)
    place.meet()
    swaps = {}
    for name in WEIGHTS:
        there = getattr(incoming, name)
        swaps[name] = copies.start(getattr(outgoing, name), there, place.across("c"), there)
    pair_column[...] = jnp.broadcast_to(pair_row[...].astype(jnp.float32), (128, tokens)).T
    arrivals = []

    def merge(name):
        swaps[name].wait_recv()
        shard = getattr(shards, name)
        mine = column_half(place, shard[...], True)
        other = getattr(incoming, name)[...][: shard.shape[0]]
        getattr(buffers, name)[place.core, place.z, place.y, place.x] = merged_rows(place, mine, other)

    def keep(source, target):
        copies.write(source, target)

    def pair(source, target, *columns):
        there = target.at[(place.core,) + columns]
        copies.write(source, there)
        arrivals.append(
            copies.start(source, there, place.across("c"), target.at[(1 - place.core,) + columns])
        )

    def row(number):
        return rows_all[pl.ds(number, 1), :]

    qkv, context, low_one, query, context_cross = (
        kept.qkv, kept.context, kept.low_one, kept.query, kept.context_cross
    )
    hidden, slope, low_two = kept.hidden_low, kept.slope, kept.low_two
    attention, cross_attention = kept.attention, kept.cross_attention
    key_value = kept.key_value

    def project_qkv(part):
        def one(half, carry):
            size = 384
            column = pl.multiple_of(half * (3 * size) + part * size, 128)
            value = dot(text[...], matrix(buffers.qkv[half, :, :, :, :, pl.ds(part * size, size)]))
            group = (half * 3 + part) // 2
            shift = pl.multiple_of(lax.rem(half * 3 + part, 2) * size, 128)
            biased = jnp.where(
                group == 0,
                rows_all[pl.ds(3, 1), pl.ds(shift, size)],
                jnp.where(group == 1, 0.0, rows_all[pl.ds(4, 1), pl.ds(shift, size)]),
            )
            qkv[:, pl.ds(column, size)] = (value + biased).astype(jnp.bfloat16)
            return carry

        lax.fori_loop(0, 2, one, 0)

    strip = 128

    def attend(pair):
        lane = lax.broadcasted_iota(jnp.int32, (strip, 128), 1)
        columns = pl.ds(pair * 128, 128)

        def one(number, carry):
            rows = pl.ds(pl.multiple_of(number * strip, strip), strip)
            two = qkv[rows, columns].astype(jnp.float32) * (1.0 / math.sqrt(HD))
            key_rows = qkv[:, pl.ds(width + pair * 128, 128)]
            value_rows = qkv[:, pl.ds(2 * width + pair * 128, 128)]
            same = jnp.concatenate([pair_column[rows, :]] * (tokens // 128), axis=1) == pair_row[...].astype(
                jnp.float32
            )
            result = None
            for head in range(2):
                own = (lane < HD) if head == 0 else (lane >= HD)
                scores = dot(jnp.where(own, two, 0.0).astype(jnp.bfloat16), key_rows, (1, 1))
                scores = jnp.where(same, scores, NEGATIVE)
                scores = jnp.exp(scores - jnp.max(scores, axis=1, keepdims=True))
                scores = scores * (1.0 / jnp.sum(scores, axis=1, keepdims=True))
                low = scores.astype(jnp.bfloat16)
                attention[pair * 2 + head, rows, :] = low
                value = dot(low, value_rows)
                result = value if head == 0 else jnp.where(own, value, result)
            context[rows, columns] = result.astype(jnp.bfloat16)
            return carry

        lax.fori_loop(0, tokens // strip, one, 0)
        keep(attention.at[pl.ds(2 * pair, 2)], kept_out.attention.at[pl.ds(2 * pair, 2)])

    def normalize(number, summed, low):
        normed, inverse = kept.normed, kept.inverse
        gain, shift = row(number), row(10 + number)
        step = 64

        def one(index, carry):
            rows = pl.ds(pl.multiple_of(index * step, step), step)
            value = work[rows, :] + summed(rows)
            center = value - jnp.mean(value, axis=1, keepdims=True)
            scale = lax.rsqrt(jnp.mean(center * center, axis=1, keepdims=True) + EPSILON)
            value = center * scale
            normed[number, rows, :] = value
            inverse[number, rows, :] = jnp.broadcast_to(scale, (step, 128))
            low(rows, value * gain + shift)
            return carry

        lax.fori_loop(0, tokens // step, one, 0)
        keep(normed.at[number], kept_out.normed.at[number])
        keep(inverse.at[number], kept_out.inverse.at[number])

    def self_out():
        work[...] = dot(context[...], whole(buffers.sout))

        def low(rows, value):
            low_one[rows, :] = value.astype(jnp.bfloat16)

        normalize(0, lambda rows: text[rows, :].astype(jnp.float32) + row(5), low)
        pair(context, pairs.context)
        pair(low_one, pairs.low_one)

    def project_patches(part):
        size = 384
        value = dot(patches[...], matrix(buffers.ckv[0, :, :, :, :, pl.ds(part * size, size)]))
        key_value[place.z, :, pl.ds(part * size, size)] = value.astype(jnp.bfloat16)
        value = dot(patches[...], matrix(buffers.ckv[1, :, :, :, :, pl.ds(part * size, size)]))
        value += rows_all[pl.ds(7, 1), pl.ds(part * size, size)]
        key_value[place.z, :, pl.ds(width + part * size, size)] = value.astype(jnp.bfloat16)

    shared = []

    def share_keys():
        for offset in range(1, line):
            origin = place.behind(offset)
            shared.append(
                copies.start(
                    key_value.at[place.z], key_value.at[place.z], place.along(offset), key_value.at[origin]
                )
            )

    def project_query():
        work[...] = dot(low_one[...], whole(buffers.cq))
        query[...] = (work[...] + row(6)).astype(jnp.bfloat16)
        keep(query, kept_out.query)

    def cross(owner):
        if owner == 0:
            for copy in shared:
                copy.wait_recv()
            keep(key_value, kept_out.key_value)
        lane = lax.broadcasted_iota(jnp.int32, (keys, width), 1) // HD
        for head in range(H):
            rows = pl.ds(head * keys, keys)
            keys_all[rows, :] = jnp.where(
                lane == head, key_value[owner, :, pl.ds(0, width)].astype(jnp.float32), 0.0
            ).astype(jnp.bfloat16)
            values_all[rows, :] = jnp.where(
                lane == head, key_value[owner, :, pl.ds(width, width)].astype(jnp.float32), 0.0
            ).astype(jnp.bfloat16)
        rows = pl.ds(owner * block, block)
        scores = dot(keys_all[...], query[rows, :], (1, 1)) * (1.0 / math.sqrt(HD))
        region = lax.broadcasted_iota(jnp.int32, (keys, block), 0) // PR
        same = region == region_row[:, rows]
        scores = jnp.where(same[None], scores.reshape(H, keys, block), NEGATIVE)
        scores = jnp.exp(scores - jnp.max(scores, axis=1, keepdims=True))
        scores = scores * (1.0 / jnp.sum(scores, axis=1, keepdims=True))
        scores = scores.reshape(H * keys, block).astype(jnp.bfloat16)
        cross_attention[owner] = scores
        context_cross[rows, :] = dot(scores, values_all[...], (0, 0)).astype(jnp.bfloat16)
        if owner == line - 1:
            keep(cross_attention, kept_out.cross_attention)
            pair(context_cross, pairs.context_cross)

    def cross_out():
        work[...] = dot(context_cross[...], whole(buffers.cout))
        first_gain, first_shift = row(0), row(10)

        def low(rows, value):
            low_two[rows, :] = value.astype(jnp.bfloat16)

        normalize(1, lambda rows: kept.normed[0, rows, :] * first_gain + first_shift + row(8), low)
        pair(low_two, pairs.low_two)

    def expand(part, half):
        size = 384
        half_width = buffers.up.shape[5]
        columns = pl.ds(half * half_width + part * size, size)
        value = dot(low_two[...], matrix(buffers.up[half, :, :, :, :, pl.ds(part * size, size)]))
        value, grad = gelu_pair(value + hidden_all[pl.ds(5, 1), columns])
        hidden[:, columns] = value.astype(jnp.bfloat16)
        slope[:, columns] = grad.astype(jnp.bfloat16)
        pair(hidden.at[:, columns], pairs.hidden_low, slice(None), columns)
        keep(slope.at[:, columns], kept_out.slope.at[:, columns])

    def contract(part):
        size = 128
        buffer = buffers.down
        columns = pl.ds(part * size, size)
        both = jnp.concatenate(
            [matrix(buffer[0, :, :, :, :, columns]), matrix(buffer[1, :, :, :, :, columns])], axis=1
        )
        value = dot(hidden[...], both)
        work[:, pl.ds(part * size, size)] = value[:, :size]
        work[:, pl.ds(width // 2 + part * size, size)] = value[:, size:]

    def finish():
        gain, shift = row(1), row(11)

        def low(rows, value):
            valid = jnp.concatenate([pair_column[rows, :]] * (width // 128), axis=1) >= 0
            kept.joined[rows, :] = jnp.where(valid, value, 0.0).astype(jnp.bfloat16)

        normalize(2, lambda rows: kept.normed[1, rows, :] * gain + shift + row(9), low)
        keep(kept.joined, kept_out.joined)

    present, counts = {}, {}
    waiting = []
    merged = set()

    def done(unit):
        present[unit.name] = present.get(unit.name, 0) + 1
        name = unit.name
        if present[name] == counts.get(name):
            keep(getattr(buffers, name), getattr(outs, name))

    schedule = Schedule(clock, done)

    def begin():
        if waiting:
            unit = waiting.pop(0)
            if unit.name and unit.name not in merged:
                merge(unit.name)
                merged.add(unit.name)
            schedule.launch(unit)

    def unit_of(buffer, name, rows, columns):
        order = ("zyx", "zxy")[len(waiting) % 2]
        unit = GatherUnit(place, copies, clock, buffer, rows, columns, order)
        unit.name, unit.begin = name, begin
        waiting.append(unit)

    unit_of(vectors_all, "", pl.ds(0, 16), pl.ds(0, 128))
    for name in WEIGHTS:
        buffer = getattr(buffers, name)
        spans = column_spans(*buffer.shape[4:])
        rows = row_spans(buffer.shape[4])
        counts[name] = len(spans) * len(rows)
        for columns in spans:
            for span in rows:
                unit_of(buffer, name, span, columns)

    def task(name, count, cost, function, *arguments):
        schedule.task(cost, function, *arguments, ready=lambda: present.get(name, 0) >= count)

    def spread():
        spread_vectors(vectors_all, rows_all, hidden_all, narrow, shards.down.shape[0], line)
        keep(rows_all, kept_out.rows)

    pair(text, pairs.text)
    pair(patches, pairs.patches)
    task("", 1, 1.0, spread)
    for part in range(3):
        task("qkv", part + 1, 1.5, project_qkv, part)
    task("", 1, 0.0, keep, qkv, kept_out.qkv)
    for number in range(H // 2):
        task("", 1, 1.8, attend, number)
        if number == 3:
            for part in range(2):
                task("ckv", part + 1, 0.5, project_patches, part)
            task("", 1, 0.1, share_keys)
    task("sout", 1, 2.0, self_out)
    task("cq", 1, 1.0, project_query)
    for owner in range(line):
        task("", 1, 1.5, cross, owner)
    task("cout", 1, 2.0, cross_out)
    for part in range(4):
        for half in range(2):
            task("up", part + 1, 1.5, expand, part, half)
    for part in range(3):
        task("down", part + 1, 1.5, contract, part)
    task("", 1, 1.5, finish)
    for _ in range(3):
        begin()
    schedule.run()
    for copy in arrivals:
        copy.wait_recv()
    copies.finish()

SAVED = ("qkv", "attention", "query", "key_value", "cross_attention", "normed", "inverse", "slope", "rows")
ORDERS = ("xyz", "yxz")


class VectorUnit:
    def __init__(self, place, copies, clock, total, landings):
        self.place, self.copies, self.clock = place, copies, clock
        self.total, self.landings = total, landings
        self.stage = 0

    def send(self):
        place, stage = self.place, self.stage
        if stage < 3:
            devices = [place.across("cxy"[stage])]
        else:
            devices = [place.along(offset) for offset in range(1, place.line)]
        self.arrivals = []
        for number, device in enumerate(devices):
            there = self.landings, (stage + number,)
            self.arrivals.append(self.copies.start(self.total, there, device, there, False))
        self.due = self.clock.now + 3.0
        self.stage += 1

    def step(self):
        for copy in self.arrivals:
            copy.wait()
        value = self.total[...]
        for number in range(len(self.arrivals)):
            value += self.landings[self.stage - 1 + number]
        self.total[...] = value
        self.clock.now = max(self.clock.now, self.due) + 0.1
        if self.stage == 4:
            return True
        self.send()
        return False


def backward_kernel(line, *refs):
    refs = list(refs)
    take = lambda names: named(names, [refs.pop(0) for _ in names])
    pop = lambda count: [refs.pop(0) for _ in range(count)]
    weights, saved, pairs = take(WEIGHTS), take(SAVED), take(PAIRS)
    cotangent, pair_row = pop(2)
    outs = take(WEIGHTS)
    text_grad, patch_grad, gains_out, biases_out, hidden_out = pop(5)
    totals, first, second, third, finals, swapped, landed = (take(WEIGHTS) for _ in range(7))
    work, inverse, rows_all, small, small_landed, key_parts, key_landed, pair_column, hidden_sum = pop(9)
    grad_kv, sent, received, local = pop(4)
    place = Place(line)
    copies = Copies(sent, received, local)
    clock = Clock(60e3, 4.0, 24.0, 3.0, 1.15)
    core = place.core
    tokens, width = work.shape
    hidden_width = hidden_sum.shape[1]
    block = tokens // line
    keys = grad_kv.shape[0]
    scaling = 1.0 / math.sqrt(HD)
    remaining = {}
    swaps = {}

    def done(unit):
        if unit is vectors:
            return
        remaining[unit.name] -= 1
        if not remaining[unit.name]:
            final, there = getattr(finals, unit.name), getattr(swapped, unit.name)
            swaps[unit.name] = copies.start((final, (place.other["c"],)), there, place.across("c"), there)

    schedule = Schedule(clock, done)
    vectors = VectorUnit(place, copies, clock, small, small_landed)

    def prepare(name, rows, columns, count):
        remaining.setdefault(name, count)
        landings = [getattr(group, name) for group in (first, second, third)]
        order = ORDERS[prepare.number % len(ORDERS)]
        prepare.number += 1
        unit = SumUnit(
            place, copies, clock, getattr(totals, name), landings, getattr(finals, name), rows, columns, order
        )
        unit.name = name
        return unit

    def launch(*arguments):
        schedule.launch(prepare(*arguments))

    prepare.number = 0

    def task(cost, function, *arguments):
        schedule.task(cost, function, *arguments)

    def half(size, other=False, offset=0, part=None):
        which = 1 - core if other else core
        return pl.ds(pl.multiple_of(which * size + offset, 128), size if part is None else part)

    def hand_over(source, target, columns=None):
        size = target.shape[1]
        there = target if columns is None else (target, (slice(None), columns))
        away = half(size, True) if columns is None else half(size, True, columns.start, columns.size)
        return copies.start((source, (slice(None), away)), there, place.across("c"), there, False)

    def norm_back(number, bias_number, normed, upstream, low):
        gain = rows_all[pl.ds(number, 1), :]
        step = 64

        def one(index, carry):
            rows = pl.ds(pl.multiple_of(index * step, step), step)
            grad, normal = upstream(rows), normed[rows, :]
            scaled = grad * gain
            center = scaled - jnp.mean(scaled, axis=1, keepdims=True)
            center -= normal * jnp.mean(scaled * normal, axis=1, keepdims=True)
            value = inverse[number, rows, :][:, :1] * center
            work[rows, :] = value
            rounded = value.astype(jnp.bfloat16)
            low[rows, :] = rounded
            sums = (grad * normal, grad, rounded.astype(jnp.float32))
            return tuple(old + jnp.sum(new, axis=0, keepdims=True) for old, new in zip(carry, sums))

        zero = jnp.zeros((1, width), jnp.float32)
        gain_sum, shift_sum, bias_sum = lax.fori_loop(0, tokens // step, one, (zero, zero, zero))
        small[pl.ds(number, 1), :] = gain_sum
        small[pl.ds(10 + number, 1), :] = shift_sum
        small[pl.ds(bias_number, 1), :] = bias_sum

    def weight_grad(name, inputs, low, landing, columns, span=None):
        size = landing.shape[1]
        own = half(size, False, columns.start, columns.size)
        span = slice(None) if span is None else span
        value = dot(inputs[core, :, span], low[:, own], (0, 0))
        value += dot(inputs[1 - core, :, span], landing[:, columns], (0, 0))
        return value.astype(jnp.bfloat16)

    def spread_columns(name, inputs, low, columns, count, pieces=1):
        total = getattr(totals, name)
        value = weight_grad(name, inputs, low, getattr(landed, name), columns)
        total[:, :, :, :, columns] = value.reshape(total.shape[:4] + (columns.size,))
        for start in range(0, columns.size, columns.size // pieces):
            piece = pl.ds(columns.start + start, columns.size // pieces)
            launch(name, pl.ds(0, total.shape[3]), piece, count)

    def feed_forward(up, down, inputs_up, inputs_down, slope, normed, grad_low, cotangent_here):
        reads = [
            copies.read(source, target)
            for source, target in (
                (cotangent, cotangent_here),
                (saved.normed.at[2], normed),
                (saved.inverse, inverse),
                (saved.rows, rows_all),
                (weights.down, down),
                (saved.slope, slope),
                (pairs.hidden_low, inputs_down),
                (pairs.low_two, inputs_up),
                (weights.up, up),
            )
        ]
        sends = []

        def third_norm():
            for copy in reads[:4]:
                copy.wait()
            small[...] = jnp.zeros_like(small)

            def upstream(rows):
                valid = jnp.concatenate([pair_column[rows, :]] * (width // 128), axis=1) >= 0
                return jnp.where(valid, cotangent_here[rows, :].astype(jnp.float32), 0.0)

            norm_back(2, 9, normed, upstream, grad_low)
            place.meet()
            sends.append(hand_over(grad_low, landed.down))

        size = 384
        half_width = hidden_width // 2

        def expand(other):
            if other:
                for copy in reads[4:6]:
                    copy.wait()

            def one(part, carry):
                column = (1 - core if other else core) * half_width + part * size
                number = column // size
                both = jnp.concatenate(
                    [matrix(down[side, number // 2, lax.rem(number, 2)]) for side in range(2)], axis=1
                )
                columns = pl.ds(pl.multiple_of(column, 128), size)
                value = dot(grad_low[...], both, (1, 1)) * slope[:, columns].astype(jnp.float32)
                value = value.astype(jnp.bfloat16)
                slope[:, columns] = value
                hidden_sum[pl.ds(0, 1), columns] = jnp.sum(value.astype(jnp.float32), axis=0, keepdims=True)
                return carry

            lax.fori_loop(0, half_width // size, one, 0)
            if other:
                sends.append(hand_over(slope, landed.up))

        def grad_down():
            reads[6].wait()
            sends[0].wait_recv()
            total = totals.down
            tall = 48
            count = total.shape[3] // tall
            units = [
                prepare("down", pl.ds(row * tall, tall), pl.ds(0, width // 2), count) for row in range(count)
            ]
            slab = hidden_width // line
            for z in range(line):
                span = pl.ds(z * slab, slab)
                value = weight_grad("down", inputs_down, grad_low, landed.down, pl.ds(0, width // 2), span)
                total[z] = value.reshape(total.shape[1:])
                clock.now += 1.0
                for unit in units:
                    unit.send_slab(z)
            schedule.flying.extend(units)

        def grad_up(part):
            if part == 0:
                reads[7].wait()
                sends[1].wait_recv()
                for k in range(4):
                    small[pl.ds(13 + k, 1), :] = hidden_sum[pl.ds(0, 1), pl.ds(k * width, width)]
            spread_columns("up", inputs_up, slope, pl.ds(part * size, size), half_width // size)

        def grad_second():
            reads[8].wait()
            for side in range(2):
                work[...] += dot(slope[:, pl.ds(side * half_width, half_width)], matrix(up[side]), (1, 1))

        task(2.0, third_norm)
        task(2.0, expand, True)
        task(0.0, grad_down)
        task(2.0, expand, False)
        for part in range(half_width // size):
            task(1.2, grad_up, part)
        task(3.0, grad_second)
        schedule.run(False)
        for copy in sends:
            copy.wait_send()

    def attentions(qkv_w, ckv_w, sout_w, cq_w, cout_w, left_one, left_two, patch_pair, normed, query, key_value,
                   cross_attention, keys_all, values_all, qkv, attention, scores_low, grad_two_low, grad_query,
                   grad_one_low, grad_context):
        order = (
            (saved.normed.at[1], normed.at[1]),
            (weights.cout, cout_w),
            (pairs.context_cross, left_one),
            (saved.key_value, key_value),
            (saved.cross_attention, cross_attention),
            (saved.query, query),
            (weights.cq, cq_w),
            (saved.normed.at[0], normed.at[0]),
            (pairs.low_one, left_two),
            (weights.sout, sout_w),
            (weights.ckv, ckv_w),
            (pairs.patches, patch_pair),
            (saved.qkv, qkv),
            (saved.attention.at[pl.ds(0, 2)], attention.at[0]),
            (weights.qkv, qkv_w),
        )
        reads = [copies.read(source, target) for source, target in order]
        waited = set()
        later = {}
        sends = {}
        size = 384
        third_part = pl.ds(0, width // 2)

        def need(*numbers):
            for number in numbers:
                if number not in waited:
                    reads[number].wait()
                    waited.add(number)

        def second_norm():
            need(0)
            norm_back(1, 8, normed.at[1], lambda rows: work[rows, :], grad_two_low)
            sends["t"] = hand_over(grad_two_low, landed.cout)

        def context_grad():
            need(1)
            grad_context[...] = dot(grad_two_low[...], whole(cout_w), (1, 1)).astype(jnp.bfloat16)

        def cross(offset):
            need(3, 4, 5)
            owner = place.ahead(offset)
            lane = lax.broadcasted_iota(jnp.int32, (keys, width), 1) // HD
            key_rows = key_value[owner, :, pl.ds(0, width)].astype(jnp.float32)
            value_rows = key_value[owner, :, pl.ds(width, width)].astype(jnp.float32)
            for head in range(H):
                rows = pl.ds(head * keys, keys)
                keys_all[rows, :] = jnp.where(lane == head, key_rows, 0.0).astype(jnp.bfloat16)
                values_all[rows, :] = jnp.where(lane == head, value_rows, 0.0).astype(jnp.bfloat16)
            rows = pl.ds(pl.multiple_of(owner * block, block), block)
            probability = cross_attention[owner].astype(jnp.float32).reshape(H, keys, block)
            grad = dot(values_all[...], grad_context[rows, :], (1, 1)).reshape(H, keys, block)
            grad = probability * (grad - jnp.sum(probability * grad, axis=1, keepdims=True))
            grad = grad.reshape(H * keys, block).astype(jnp.bfloat16)
            grad_query[rows, :] = (dot(grad, keys_all[...], (0, 0)) * scaling).astype(jnp.bfloat16)
            lane = lax.broadcasted_iota(jnp.int32, (keys, 128), 1)
            for pair in range(H // 2):
                columns = pl.ds(pair * 128, 128)
                heads = slice(pair * 2 * keys, (pair + 1) * 2 * keys)
                value = dot(grad[heads], query[rows, columns]) * scaling
                key_parts[offset, :, columns] = jnp.where(lane < HD, value[:keys], value[keys:]).astype(
                    jnp.bfloat16
                )
                value = dot(cross_attention[owner, pl.ds(heads.start, 2 * keys), :], grad_context[rows, columns])
                key_parts[offset, :, pl.ds(width + pair * 128, 128)] = jnp.where(
                    lane < HD, value[:keys], value[keys:]
                ).astype(jnp.bfloat16)
            if offset:
                there = key_landed, (offset - 1,)
                sends[offset] = copies.start((key_parts, (offset,)), there, place.along(offset), there)
            if offset == 0:
                sends["q"] = hand_over(grad_query, landed.cq)

        def grad_cout():
            need(2)
            sends["t"].wait_recv()
            spread_columns("cout", left_one, grad_two_low, third_part, 1)
            later["context"] = copies.read(pairs.context, left_one)

        def grad_first():
            need(6)
            work[...] += dot(grad_query[...], whole(cq_w), (1, 1))
            small[pl.ds(6, 1), :] = jnp.sum(grad_query[...].astype(jnp.float32), axis=0, keepdims=True)

        def first_norm():
            need(7)
            norm_back(0, 5, normed.at[0], lambda rows: work[rows, :], grad_one_low)
            sends["s"] = hand_over(grad_one_low, landed.sout)

        def grad_cq():
            need(8)
            sends["q"].wait_recv()
            spread_columns("cq", left_two, grad_query, third_part, 1)
            later["text"] = copies.read(pairs.text, left_two)

        def self_context():
            need(9)
            grad_context[...] = dot(grad_one_low[...], whole(sout_w), (1, 1)).astype(jnp.bfloat16)

        def grad_sout():
            later["context"].wait()
            sends["s"].wait_recv()
            spread_columns("sout", left_one, grad_one_low, third_part, 1)

        def key_grad():
            value = key_parts[0].astype(jnp.float32)
            for offset in range(1, line):
                sends[offset].wait_recv()
                value += key_landed[offset - 1].astype(jnp.float32)
            value = value.astype(jnp.bfloat16)
            grad_kv[...] = value
            sends["k"] = hand_over(grad_kv, landed.ckv)
            small[pl.ds(7, 1), :] = jnp.sum(value[:, width:].astype(jnp.float32), axis=0, keepdims=True)
            need(10)
            patch_grad[...] = dot(grad_kv[...], whole(ckv_w), (1, 1))

        def grad_ckv(part):
            if part == 0:
                need(11)
                sends["k"].wait_recv()
            spread_columns("ckv", patch_pair, grad_kv, pl.ds(part * size, size), 2)

        strip = 128

        def attend(pair):
            slot = pair % 2
            if pair == 0:
                need(12, 13)
            else:
                later[pair].wait()
            if pair + 1 < H // 2:
                later[pair + 1] = copies.read(
                    saved.attention.at[pl.ds(2 * pair + 2, 2)], attention.at[1 - slot]
                )
            columns, key_columns = pl.ds(pair * 128, 128), pl.ds(width + pair * 128, 128)
            value_columns = pl.ds(2 * width + pair * 128, 128)

            def own(value, head):
                lane = lax.broadcasted_iota(jnp.int32, value.shape, 1)
                return jnp.where((lane < HD) == (head == 0), value.astype(jnp.float32), 0.0).astype(jnp.bfloat16)

            def one(number, carry):
                rows = pl.ds(pl.multiple_of(number * strip, strip), strip)
                for head in range(2):
                    grad = dot(own(grad_context[rows, columns], head), qkv[:, value_columns], (1, 1))
                    probability = attention[slot, head, rows, :].astype(jnp.float32)
                    grad = probability * (grad - jnp.sum(probability * grad, axis=1, keepdims=True))
                    scores_low[head, rows, :] = grad.astype(jnp.bfloat16)
                return carry

            lax.fori_loop(0, tokens // strip, one, 0)
            query_grad = key_grad = value_grad = 0.0
            for head in range(2):
                query_grad += dot(scores_low[head], own(qkv[:, key_columns], head))
                key_grad += dot(scores_low[head], own(qkv[:, columns], head), (0, 0))
                value_grad += dot(attention[slot, head], own(grad_context[:, columns], head), (0, 0))
            query_grad = (query_grad * scaling).astype(jnp.bfloat16)
            value_grad = value_grad.astype(jnp.bfloat16)
            qkv[:, columns] = query_grad
            qkv[:, key_columns] = (key_grad * scaling).astype(jnp.bfloat16)
            qkv[:, value_columns] = value_grad
            small[pl.ds(3, 1), columns] = jnp.sum(query_grad.astype(jnp.float32), axis=0, keepdims=True)
            small[pl.ds(4, 1), columns] = jnp.sum(value_grad.astype(jnp.float32), axis=0, keepdims=True)
            if pair + 1 == H // 2:
                sends["p"] = hand_over(qkv, landed.qkv)
                schedule.launch(vectors)

        def grad_qkv(part):
            if part == 0:
                later["text"].wait()
                sends["p"].wait_recv()
            spread_columns("qkv", left_two, qkv, pl.ds(part * size, size), 5, 3 if part == 2 else 1)

        def text_back(side):
            need(14)
            size = 3 * width // 2
            work[...] += dot(qkv[:, pl.ds(side * size, size)], matrix(qkv_w[side]), (1, 1))
            if side == 1:
                copies.write(work, text_grad)

        task(2.0, second_norm)
        task(1.0, context_grad)
        task(1.0, grad_cout)
        for offset in list(range(1, line)) + [0]:
            task(2.0, cross, offset)
        task(1.0, grad_first)
        task(2.0, first_norm)
        task(1.0, grad_cq)
        task(1.0, self_context)
        task(1.0, key_grad)
        task(1.0, grad_sout)
        for part in range(2):
            task(0.5, grad_ckv, part)
        for number in range(H // 2):
            task(2.5, attend, number)
        for part in range(3):
            task(1.2, grad_qkv, part)
        for side in range(2):
            task(1.5, text_back, side)
        schedule.run()
        for name in ("t", "q", "s", "k", "p"):
            sends[name].wait_send()

    place.greet()
    pair_column[...] = jnp.broadcast_to(pair_row[...].astype(jnp.float32), (128, tokens)).T
    low = jnp.bfloat16
    wide = (tokens, hidden_width)
    rows = (tokens, width)
    shape = lambda ref: pltpu.VMEM(ref.shape, ref.dtype)
    pl.run_scoped(
        feed_forward,
        shape(weights.up),
        shape(weights.down),
        shape(pairs.low_two),
        shape(pairs.hidden_low),
        pltpu.VMEM(wide, low),
        pltpu.VMEM(rows, jnp.float32),
        pltpu.VMEM(rows, low),
        pltpu.VMEM(rows, low),
    )
    pl.run_scoped(
        attentions,
        shape(weights.qkv),
        shape(weights.ckv),
        shape(weights.sout),
        shape(weights.cq),
        shape(weights.cout),
        shape(pairs.context),
        shape(pairs.context),
        shape(pairs.patches),
        pltpu.VMEM((2,) + rows, jnp.float32),
        shape(saved.query),
        shape(saved.key_value),
        shape(saved.cross_attention),
        pltpu.VMEM((H * keys, width), low),
        pltpu.VMEM((H * keys, width), low),
        shape(saved.qkv),
        pltpu.VMEM((2, 2, tokens, tokens), low),
        pltpu.VMEM((2, tokens, tokens), low),
        pltpu.VMEM(rows, low),
        pltpu.VMEM(rows, low),
        pltpu.VMEM(rows, low),
        pltpu.VMEM(rows, low),
    )
    device = place.z * 8 + place.f
    value = small[...]
    narrow, slim = gains_out.shape[1], hidden_out.shape[1]
    turned = pltpu.roll(value, lax.rem(width - device * narrow, width), 1)
    gains_out[...] = turned[:3, :narrow]
    biases_out[...] = turned[3:13, :narrow]
    number = lax.broadcasted_iota(jnp.int32, value.shape, 0)
    picked = jnp.sum(jnp.where(number == 13 + place.z, value, 0.0), axis=0, keepdims=True)
    picked = pltpu.roll(jnp.broadcast_to(picked, (8, width)), lax.rem(width - place.f * slim, width), 1)
    hidden_out[...] = picked[:1, :slim]
    for name in WEIGHTS:
        swaps[name].wait_recv()
        out = getattr(outs, name)
        mine, other = getattr(finals, name)[core], getattr(swapped, name)[...]
        middle = mine.shape[1]
        out[:, :middle] = jnp.where(core == 0, mine, other)
        out[:, middle:] = jnp.where(core == 0, other, mine)
    copies.finish()


def gathered(line, shards):
    return [(2, line, 2, 2, 2 * shard.shape[0], shard.shape[1] // 2) for shard in shards]


def forward_all(line, shards, gains, shifts, slim_bias, text, patches, pair_row, region_row):
    tokens, width = text.shape
    keys, depth = patches.shape
    wide = shards[5].shape[1]
    low, full = jnp.bfloat16, jnp.float32
    rows = (tokens, width)
    kept = [
        ((tokens, 3 * width), low),
        ((H, tokens, tokens), low),
        (rows, low),
        ((line, keys, 2 * width), low),
        ((line, H * keys, tokens // line), low),
        ((3,) + rows, full),
        ((3, tokens, 128), full),
        ((tokens, wide), low),
        (rows, low),
        ((16, width), full),
    ]
    locals_ = [((8, wide), full), (rows, low), (rows, low), (rows, low), (rows, low), ((tokens, wide), low)]
    paired = [rows, (keys, depth), rows, rows, rows, rows, (tokens, wide)]
    shapes = gathered(line, shards)
    out_shape = [jax.ShapeDtypeStruct(shape, low) for shape in shapes]
    out_shape += [jax.ShapeDtypeStruct(*shape) for shape in kept]
    out_shape += [jax.ShapeDtypeStruct((2,) + shape, low) for shape in paired]
    scratch = [pltpu.VMEM(shape, low) for shape in shapes]
    for _ in range(2):
        scratch += [pltpu.VMEM((padded(shard.shape[0]), shard.shape[1] // 2), low) for shard in shards]
    scratch += [pltpu.VMEM(*shape) for shape in kept + locals_]
    scratch += [
        pltpu.VMEM((16, 128), full),
        pltpu.VMEM((2, line, 2, 2, 16, 128), low),
        pltpu.VMEM((tokens, 128), full),
        pltpu.VMEM(rows, full),
        pltpu.VMEM((H * keys, width), low),
        pltpu.VMEM((H * keys, width), low),
        pltpu.SemaphoreType.DMA((160,)),
        pltpu.SemaphoreType.DMA((160,)),
        pltpu.SemaphoreType.DMA((96,)),
    ]
    outs = pl.pallas_call(
        functools.partial(forward_kernel, line),
        out_shape=out_shape,
        in_specs=[pl.BlockSpec(memory_space=pltpu.VMEM)] * (len(shards) + 7),
        out_specs=[pl.BlockSpec(memory_space=pl.ANY)] * len(out_shape),
        scratch_shapes=scratch,
        compiler_params=pltpu.CompilerParams(
            collective_id=0, has_side_effects=True, vmem_limit_bytes=62 * 2**20
        ),
    )(*shards, gains, shifts, slim_bias, text, patches, pair_row, region_row)
    count = len(shards)
    return outs[:count], outs[count : count + len(kept)], outs[count + len(kept) :]


def backward_all(line, weights, saved, pairs, cotangent, pair_row, narrow, slim):
    low, full = jnp.bfloat16, jnp.float32
    tokens, width = cotangent.shape
    keys, depth = pairs[1].shape[1:]
    wide = pairs[-1].shape[2]
    sizes = [weight.shape[4:] for weight in weights]
    scratch = []
    for lead in ((line, 2, 2), (line, 2), (line,), (line - 1,)):
        scratch += [pltpu.VMEM(lead + size, low) for size in sizes]
    scratch += [pltpu.VMEM((2, size[0] // 2, size[1]), full) for size in sizes]
    scratch += [pltpu.VMEM((size[0] // 2, size[1]), full) for size in sizes]
    for name, size in zip(WEIGHTS, sizes):
        scratch.append(pltpu.VMEM((keys if name == "ckv" else tokens, size[1]), low))
    scratch += [
        pltpu.VMEM((tokens, width), full),
        pltpu.VMEM((3, tokens, 128), full),
        pltpu.VMEM((16, width), full),
        pltpu.VMEM((24, width), full),
        pltpu.VMEM((2 + line, 24, width), full),
        pltpu.VMEM((line, keys, 2 * width), low),
        pltpu.VMEM((line - 1, keys, 2 * width), low),
        pltpu.VMEM((tokens, 128), full),
        pltpu.VMEM((8, wide), full),
        pltpu.VMEM((keys, 2 * width), low),
        pltpu.SemaphoreType.DMA((160,)),
        pltpu.SemaphoreType.DMA((160,)),
        pltpu.SemaphoreType.DMA((64,)),
    ]
    out_shape = [jax.ShapeDtypeStruct((size[0] // 2, 2 * size[1]), full) for size in sizes]
    out_shape += [
        jax.ShapeDtypeStruct((tokens, width), full),
        jax.ShapeDtypeStruct((keys, depth), full),
        jax.ShapeDtypeStruct((3, narrow), full),
        jax.ShapeDtypeStruct((10, narrow), full),
        jax.ShapeDtypeStruct((1, slim), full),
    ]
    vmem, anywhere = pl.BlockSpec(memory_space=pltpu.VMEM), pl.BlockSpec(memory_space=pl.ANY)
    count = len(weights)
    outs = pl.pallas_call(
        functools.partial(backward_kernel, line),
        out_shape=out_shape,
        in_specs=[anywhere] * (count + len(saved) + len(pairs) + 1) + [vmem],
        out_specs=[vmem] * count + [anywhere] + [vmem] * 4,
        scratch_shapes=scratch,
        compiler_params=pltpu.CompilerParams(
            collective_id=1, has_side_effects=True, vmem_limit_bytes=63 * 2**20
        ),
    )(*weights, *saved, *pairs, cotangent, pair_row)
    return outs[:count], outs[count:]


def hand_out_kernel(count, *refs):
    semaphores = refs[-1]
    moves = [
        pltpu.make_async_copy(source, target, semaphores.at[number])
        for number, (source, target) in enumerate(zip(refs[:count], refs[count : 2 * count]))
    ]
    for move in moves:
        move.start()
    for move in moves:
        move.wait()


def hand_out(values):
    count = len(values)
    anywhere = pl.BlockSpec(memory_space=pl.ANY)
    return pl.pallas_call(
        functools.partial(hand_out_kernel, count),
        out_shape=[jax.ShapeDtypeStruct(value.shape, value.dtype) for value in values],
        in_specs=[anywhere] * count,
        out_specs=[pl.BlockSpec(memory_space=pltpu.VMEM)] * count,
        scratch_shapes=[pltpu.SemaphoreType.DMA((count,))],
        compiler_params=pltpu.CompilerParams(vmem_limit_bytes=63 * 2**20),
    )(*values)


def fast_body(
    text_rows,
    patches,
    row_pair,
    row_region,
    self_qkv,
    self_out,
    cross_query,
    cross_key_value,
    cross_out,
    ffn_up,
    ffn_down,
    norm_gains,
    biases,
    ffn_bias,
    cotangent,
):
    line = lax.axis_size("dp")
    narrow, slim = norm_gains.shape[1], ffn_bias.shape[0]
    shards = (self_qkv, cross_key_value, self_out, cross_query, cross_out, ffn_up, ffn_down)
    pair_row = row_pair.reshape(1, -1)
    weights, kept, pairs = forward_all(
        line,
        shards,
        norm_gains,
        biases,
        ffn_bias[None],
        text_rows,
        patches.reshape(-1, patches.shape[2]),
        pair_row,
        row_region.reshape(1, -1),
    )
    joined = kept[8]
    saved = kept[:8] + kept[9:]
    grads, (text_grad, patch_grad, gains, shifts, hidden) = backward_all(
        line, weights, saved, pairs, cotangent, pair_row, narrow, slim
    )
    results = hand_out((joined, text_grad, patch_grad, gains, shifts, hidden, *grads))
    joined, text_grad, patch_grad, gains, shifts, hidden, *grads = results
    grad_qkv, grad_ckv, grad_sout, grad_cq, grad_cout, grad_up, grad_down = grads
    return (
        joined,
        text_grad,
        patch_grad.reshape(patches.shape),
        grad_qkv,
        grad_sout,
        grad_cq,
        grad_ckv,
        grad_cout,
        grad_up,
        grad_down,
        gains,
        shifts,
        hidden.reshape(-1),
    )


def body(
    text_rows,
    patches,
    row_pair,
    row_region,
    self_qkv,
    self_out,
    cross_query,
    cross_key_value,
    cross_out,
    ffn_up,
    ffn_down,
    norm_gains,
    biases,
    ffn_bias,
    cotangent,
):
    weight_qkv, weight_sout, weight_cq, weight_ckv, weight_cout, gains_all, bias_all = (
        lax.all_gather(self_qkv, ("dp", "fsdp"), axis=0, tiled=True),
        lax.all_gather(self_out, ("dp", "fsdp"), axis=0, tiled=True),
        lax.all_gather(cross_query, ("dp", "fsdp"), axis=0, tiled=True),
        lax.all_gather(cross_key_value, ("dp", "fsdp"), axis=0, tiled=True),
        lax.all_gather(cross_out, ("dp", "fsdp"), axis=0, tiled=True),
        lax.all_gather(norm_gains, ("dp", "fsdp"), axis=1, tiled=True),
        lax.all_gather(biases, ("dp", "fsdp"), axis=1, tiled=True),
    )
    weight_up, weight_down, bias_up_all = (
        lax.all_gather(ffn_up, ("dp", "fsdp"), axis=0, tiled=True),
        lax.all_gather(ffn_down, ("dp", "fsdp"), axis=0, tiled=True),
        lax.all_gather(ffn_bias, ("dp", "fsdp"), axis=0, tiled=True),
    )
    gains = gains_all.astype(jnp.float32)
    bias_rows = bias_all.astype(jnp.float32)
    bias_hidden = bias_up_all.astype(jnp.float32)
    row_count, model_width = text_rows.shape
    owners = lax.axis_size("dp")
    block_rows = row_count // owners
    valid = (row_pair >= 0)[:, None]
    patch_rows = patches.reshape(-1, patches.shape[2])
    kv_projected = jnp.dot(patch_rows, weight_ckv, preferred_element_type=jnp.float32)
    key_local = kv_projected[:, :model_width].astype(jnp.bfloat16)
    value_local = (kv_projected[:, model_width:] + bias_rows[4]).astype(jnp.bfloat16)
    keys_count = key_local.shape[0]
    kept_self, context_self = self_forward(
        text_rows, row_pair, weight_qkv, bias_rows[0], bias_rows[1]
    )
    branch_self = (
        jnp.dot(context_self, weight_sout, preferred_element_type=jnp.float32) + bias_rows[2]
    )
    first, normed_one, inverse_one = norm_forward(
        text_rows.astype(jnp.float32) + branch_self, gains[0], bias_rows[7]
    )
    first_low = first.astype(jnp.bfloat16)
    queries = (
        jnp.dot(first_low, weight_cq, preferred_element_type=jnp.float32) + bias_rows[3]
    ).astype(jnp.bfloat16)
    region_blocks = row_region.reshape(owners, block_rows)
    arrived, arrived_region = (
        lax.all_to_all(
            queries.reshape(owners, block_rows, model_width),
            "dp",
            split_axis=0,
            concat_axis=0,
            tiled=True,
        ),
        lax.all_to_all(region_blocks, "dp", split_axis=0, concat_axis=0, tiled=True),
    )
    arrived = arrived.reshape(1, owners * block_rows, H, HD)
    arrived_region = arrived_region.reshape(1, owners * block_rows)
    key_view = key_local.reshape(1, keys_count, H, HD)
    value_view = value_local.reshape(1, keys_count, H, HD)
    logsum_cross, context_owner = cross_forward(arrived, key_view, value_view, arrived_region)
    context_cross = lax.all_to_all(
        context_owner.reshape(owners, block_rows, model_width),
        "dp",
        split_axis=0,
        concat_axis=0,
        tiled=True,
    ).reshape(row_count, model_width)
    branch_cross = (
        jnp.dot(context_cross, weight_cout, preferred_element_type=jnp.float32) + bias_rows[5]
    )
    second, normed_two, inverse_two = norm_forward(first + branch_cross, gains[1], bias_rows[8])
    second_low = second.astype(jnp.bfloat16)
    hidden_pre = jnp.dot(second_low, weight_up, preferred_element_type=jnp.float32) + bias_hidden
    hidden_low = gelu_exact(hidden_pre).astype(jnp.bfloat16)
    branch_ffn = jnp.dot(hidden_low, weight_down, preferred_element_type=jnp.float32) + bias_rows[6]
    result, normed_three, inverse_three = norm_forward(second + branch_ffn, gains[2], bias_rows[9])
    joined_text = jnp.where(valid, result, 0.0).astype(jnp.bfloat16)
    upstream = jnp.where(valid, cotangent.astype(jnp.float32), 0.0)
    grad_three, grad_gain_three, grad_shift_three = norm_backward(
        upstream, normed_three, inverse_three, gains[2]
    )
    grad_ffn = grad_three.astype(jnp.bfloat16)
    grad_hidden = times_transpose(grad_ffn, weight_down)
    grad_pre = jax.vjp(gelu_exact, hidden_pre)[1](grad_hidden)[0].astype(jnp.bfloat16)
    ffn_terms = (
        transpose_times(second_low, grad_pre),
        transpose_times(hidden_low, grad_ffn),
        jnp.sum(grad_pre, axis=0, dtype=jnp.float32),
    )
    grad_up, grad_down, grad_up_bias = (
        lax.psum_scatter(ffn_terms[0], ("dp", "fsdp"), scatter_dimension=0, tiled=True),
        lax.psum_scatter(ffn_terms[1], ("dp", "fsdp"), scatter_dimension=0, tiled=True),
        lax.psum_scatter(ffn_terms[2], ("dp", "fsdp"), scatter_dimension=0, tiled=True),
    )
    grad_second = grad_three + times_transpose(grad_pre, weight_up)
    grad_two, grad_gain_two, grad_shift_two = norm_backward(
        grad_second, normed_two, inverse_two, gains[1]
    )
    grad_cross = grad_two.astype(jnp.bfloat16)
    grad_context = times_transpose(grad_cross, weight_cout).astype(jnp.bfloat16)
    grad_arrived = lax.all_to_all(
        grad_context.reshape(owners, block_rows, model_width),
        "dp",
        split_axis=0,
        concat_axis=0,
        tiled=True,
    ).reshape(1, owners * block_rows, H, HD)
    grad_query_owner, grad_key, grad_value = cross_backward(
        arrived, key_view, value_view, arrived_region, logsum_cross, grad_arrived
    )
    grad_queries = lax.all_to_all(
        grad_query_owner.astype(jnp.bfloat16).reshape(owners, block_rows, model_width),
        "dp",
        split_axis=0,
        concat_axis=0,
        tiled=True,
    ).reshape(row_count, model_width)
    grad_key_total = grad_key.reshape(keys_count, model_width)
    grad_value_total = grad_value.reshape(keys_count, model_width)
    grad_kv = jnp.concatenate(
        [grad_key_total.astype(jnp.bfloat16), grad_value_total.astype(jnp.bfloat16)], axis=1
    )
    patch_grad = times_transpose(grad_kv, weight_ckv).reshape(patches.shape)
    grad_ckv = transpose_times(patch_rows, grad_kv)
    grad_cross_value_bias = jnp.sum(grad_kv[:, model_width:], axis=0, dtype=jnp.float32)
    grad_first = grad_two + times_transpose(grad_queries, weight_cq)
    grad_cq = transpose_times(first_low, grad_queries)
    grad_cout = transpose_times(context_cross, grad_cross)
    grad_one, grad_gain_one, grad_shift_one = norm_backward(
        grad_first, normed_one, inverse_one, gains[0]
    )
    grad_self = grad_one.astype(jnp.bfloat16)
    grad_sout = transpose_times(context_self, grad_self)
    grad_context_self = times_transpose(grad_self, weight_sout).astype(jnp.bfloat16)
    grad_projected = self_backward(kept_self, grad_context_self)
    grad_qkv = transpose_times(text_rows, grad_projected)
    text_grad = grad_one + times_transpose(grad_projected, weight_qkv)
    gain_terms = jnp.stack([grad_gain_one, grad_gain_two, grad_gain_three])
    bias_terms = jnp.stack(
        [
            jnp.sum(grad_projected[:, :model_width], axis=0, dtype=jnp.float32),
            jnp.sum(grad_projected[:, 2 * model_width :], axis=0, dtype=jnp.float32),
            jnp.sum(grad_self, axis=0, dtype=jnp.float32),
            jnp.sum(grad_queries, axis=0, dtype=jnp.float32),
            grad_cross_value_bias,
            jnp.sum(grad_cross, axis=0, dtype=jnp.float32),
            jnp.sum(grad_ffn, axis=0, dtype=jnp.float32),
            grad_shift_one,
            grad_shift_two,
            grad_shift_three,
        ]
    )
    attn_terms = (grad_qkv, grad_sout, grad_cq, grad_ckv, grad_cout, gain_terms, bias_terms)
    shard_qkv, shard_sout, shard_cq, shard_ckv, shard_cout, shard_gains, shard_biases = (
        lax.psum_scatter(attn_terms[0], ("dp", "fsdp"), scatter_dimension=0, tiled=True),
        lax.psum_scatter(attn_terms[1], ("dp", "fsdp"), scatter_dimension=0, tiled=True),
        lax.psum_scatter(attn_terms[2], ("dp", "fsdp"), scatter_dimension=0, tiled=True),
        lax.psum_scatter(attn_terms[3], ("dp", "fsdp"), scatter_dimension=0, tiled=True),
        lax.psum_scatter(attn_terms[4], ("dp", "fsdp"), scatter_dimension=0, tiled=True),
        lax.psum_scatter(attn_terms[5], ("dp", "fsdp"), scatter_dimension=1, tiled=True),
        lax.psum_scatter(attn_terms[6], ("dp", "fsdp"), scatter_dimension=1, tiled=True),
    )
    return (
        joined_text,
        text_grad,
        patch_grad,
        shard_qkv,
        shard_sout,
        shard_cq,
        shard_ckv,
        shard_cout,
        grad_up,
        grad_down,
        shard_gains,
        shard_biases,
        grad_up_bias,
    )


def solution(mesh):
    in_specs = (
        P(("dp", "fsdp"), None),
        P(("dp", "fsdp"), None, None),
        P(("dp", "fsdp")),
        P(("dp", "fsdp")),
        P(("dp", "fsdp"), None),
        P(("dp", "fsdp"), None),
        P(("dp", "fsdp"), None),
        P(("dp", "fsdp"), None),
        P(("dp", "fsdp"), None),
        P(("dp", "fsdp"), None),
        P(("dp", "fsdp"), None),
        P(None, ("dp", "fsdp")),
        P(None, ("dp", "fsdp")),
        P(("dp", "fsdp")),
        P(("dp", "fsdp"), None),
    )
    out_specs = (
        P(("dp", "fsdp"), None),
        P(("dp", "fsdp"), None),
        P(("dp", "fsdp"), None, None),
        P(("dp", "fsdp"), None),
        P(("dp", "fsdp"), None),
        P(("dp", "fsdp"), None),
        P(("dp", "fsdp"), None),
        P(("dp", "fsdp"), None),
        P(("dp", "fsdp"), None),
        P(("dp", "fsdp"), None),
        P(None, ("dp", "fsdp")),
        P(None, ("dp", "fsdp")),
        P(("dp", "fsdp")),
    )
    fast = mesh.shape["fsdp"] == 8
    chosen = fast_body if fast else body
    return jax.shard_map(chosen, mesh=mesh, in_specs=in_specs, out_specs=out_specs, check_vma=False)
```

```python
import functools
import math
import types

import jax
import jax.numpy as jnp
from jax import lax
from jax.experimental import pallas as pl
from jax.experimental.pallas import tpu as pltpu
from jax.sharding import PartitionSpec as P

H = 12
HD = 64
PR = 32
BLK = 512


EPSILON = 1e-06
NEGATIVE = -1e30


def times_transpose(left, right):
    return lax.dot_general(
        left, right, (((1,), (1,)), ((), ())), preferred_element_type=jnp.float32
    )


def transpose_times(left, right):
    return lax.dot_general(
        left, right, (((0,), (0,)), ((), ())), preferred_element_type=jnp.float32
    )


def gelu_exact(values):
    return jax.nn.gelu(values, approximate=False)


def norm_forward(summed, gain_row, shift_row):
    center = summed - jnp.mean(summed, axis=-1, keepdims=True)
    inverse = lax.rsqrt(jnp.mean(center * center, axis=-1, keepdims=True) + EPSILON)
    normed = center * inverse
    return (normed * gain_row + shift_row, normed, inverse)


def norm_backward(upstream, normed, inverse, gain_row):
    scaled = upstream * gain_row
    centered = (
        scaled
        - jnp.mean(scaled, axis=-1, keepdims=True)
        - normed * jnp.mean(scaled * normed, axis=-1, keepdims=True)
    )
    return (inverse * centered, jnp.sum(upstream * normed, axis=0), jnp.sum(upstream, axis=0))


def self_scores(query_rows, key_rows, segment):
    scores = jnp.einsum(
        "qhd,khd->hqk", query_rows, key_rows, preferred_element_type=jnp.float32
    ) * (1.0 / math.sqrt(HD))
    same_pair = segment[:, None] == segment[None, :]
    return jnp.where(same_pair[None], scores, NEGATIVE)


def self_window(window):
    query_rows, key_rows, value_rows, segment = window
    scores = self_scores(query_rows, key_rows, segment)
    highest = jnp.max(scores, axis=-1, keepdims=True)
    logsum = highest + jnp.log(jnp.sum(jnp.exp(scores - highest), axis=-1, keepdims=True))
    weights = jnp.exp(scores - logsum).astype(jnp.bfloat16)
    context = jnp.einsum("hqk,khd->qhd", weights, value_rows, preferred_element_type=jnp.float32)
    return (logsum, context.astype(jnp.bfloat16))


def self_window_back(window):
    query_rows, key_rows, value_rows, segment, logsum, grad_rows = window
    probability = jnp.exp(self_scores(query_rows, key_rows, segment) - logsum)
    grad_prob = jnp.einsum(
        "qhd,khd->hqk", grad_rows, value_rows, preferred_element_type=jnp.float32
    )
    grad_score = (
        probability * (grad_prob - jnp.sum(probability * grad_prob, axis=-1, keepdims=True))
    ).astype(jnp.bfloat16)
    scaling = 1.0 / math.sqrt(HD)
    grad_query = (
        jnp.einsum("hqk,khd->qhd", grad_score, key_rows, preferred_element_type=jnp.float32)
        * scaling
    )
    grad_key = (
        jnp.einsum("hqk,qhd->khd", grad_score, query_rows, preferred_element_type=jnp.float32)
        * scaling
    )
    grad_value = jnp.einsum(
        "hqk,qhd->khd",
        probability.astype(jnp.bfloat16),
        grad_rows,
        preferred_element_type=jnp.float32,
    )
    return jnp.concatenate(
        [grad_query.reshape(BLK, -1), grad_key.reshape(BLK, -1), grad_value.reshape(BLK, -1)],
        axis=1,
    ).astype(jnp.bfloat16)


def self_forward(text_rows, segment, weight_qkv, bias_query, bias_value):
    row_count, model_width = text_rows.shape
    blocks = row_count // BLK
    projected = jnp.dot(text_rows, weight_qkv, preferred_element_type=jnp.float32)
    query_rows = (
        (projected[:, :model_width] + bias_query).astype(jnp.bfloat16).reshape(blocks, BLK, H, HD)
    )
    key_rows = (
        projected[:, model_width : 2 * model_width].astype(jnp.bfloat16).reshape(blocks, BLK, H, HD)
    )
    value_rows = (
        (projected[:, 2 * model_width :] + bias_value)
        .astype(jnp.bfloat16)
        .reshape(blocks, BLK, H, HD)
    )
    segment = segment.reshape(blocks, BLK)
    logsum, context = lax.map(self_window, (query_rows, key_rows, value_rows, segment))
    return (
        (query_rows, key_rows, value_rows, segment, logsum),
        context.reshape(row_count, model_width),
    )


def self_backward(kept_self, grad_context):
    query_rows, key_rows, value_rows, segment, logsum = kept_self
    blocks = query_rows.shape[0]
    grad_rows = grad_context.reshape(blocks, BLK, H, HD)
    grad_projected = lax.map(
        self_window_back, (query_rows, key_rows, value_rows, segment, logsum, grad_rows)
    )
    return grad_projected.reshape(blocks * BLK, -1)


def cross_scores(query_rows, key_rows, region_rows):
    scores = jnp.einsum(
        "bkhd,brhd->bhkr", key_rows, query_rows, preferred_element_type=jnp.float32
    ) * (1.0 / math.sqrt(HD))
    key_region = lax.broadcasted_iota(jnp.int32, (key_rows.shape[1], 1), 0) // PR
    same_region = key_region[None] == region_rows[:, None, :]
    return jnp.where(same_region[:, None], scores, NEGATIVE)


def cross_forward(query_rows, key_rows, value_rows, region_rows):
    scores = cross_scores(query_rows, key_rows, region_rows)
    highest = jnp.max(scores, axis=2, keepdims=True)
    logsum = highest + jnp.log(jnp.sum(jnp.exp(scores - highest), axis=2, keepdims=True))
    weights = jnp.exp(scores - logsum).astype(jnp.bfloat16)
    context = jnp.einsum("bhkr,bkhd->brhd", weights, value_rows, preferred_element_type=jnp.float32)
    return (logsum, context.astype(jnp.bfloat16))


def cross_backward(query_rows, key_rows, value_rows, region_rows, logsum, grad_context):
    probability = jnp.exp(cross_scores(query_rows, key_rows, region_rows) - logsum)
    grad_prob = jnp.einsum(
        "bkhd,brhd->bhkr", value_rows, grad_context, preferred_element_type=jnp.float32
    )
    grad_score = (
        probability * (grad_prob - jnp.sum(probability * grad_prob, axis=2, keepdims=True))
    ).astype(jnp.bfloat16)
    scaling = 1.0 / math.sqrt(HD)
    grad_query = (
        jnp.einsum("bhkr,bkhd->brhd", grad_score, key_rows, preferred_element_type=jnp.float32)
        * scaling
    )
    grad_key = (
        jnp.einsum("bhkr,brhd->bkhd", grad_score, query_rows, preferred_element_type=jnp.float32)
        * scaling
    )
    grad_value = jnp.einsum(
        "bhkr,brhd->bkhd",
        probability.astype(jnp.bfloat16),
        grad_context,
        preferred_element_type=jnp.float32,
    )
    return (grad_query, grad_key, grad_value)


MESH = pl.DeviceIdType.MESH
WEIGHTS = ("qkv", "ckv", "sout", "cq", "cout", "up", "down")
CORE_LINK = 400e3


def named(names, refs):
    return types.SimpleNamespace(**dict(zip(names, refs)))


class Place:
    def __init__(self, line):
        self.line = line
        self.z = lax.axis_index("dp")
        self.f = lax.axis_index("fsdp")
        self.core = lax.rem(self.f, 2)
        self.x = lax.rem(self.f // 2, 2)
        self.y = self.f // 4
        self.other = {"c": 1 - self.core, "x": 1 - self.x, "y": 1 - self.y}
        steps = {"c": 1 - 2 * self.core, "x": 2 - 4 * self.x, "y": 4 - 8 * self.y}
        self.neighbours = {axis: self.f + step for axis, step in steps.items()}
        self.onward = [lax.rem(self.z + k, line) for k in range(line)]
        self.backward = [lax.rem(self.z + line - k, line) for k in range(line)]

    def across(self, axis):
        return (self.z, self.neighbours[axis])

    def along(self, offset):
        return (self.onward[offset], self.f)

    def ahead(self, offset):
        return self.onward[offset]

    def behind(self, offset):
        return self.backward[offset]

    def greet(self):
        barrier = pltpu.get_barrier_semaphore()
        partners = [self.across(axis) for axis in "cxy"] + [self.along(k) for k in range(1, self.line)]
        for device in partners:
            pl.semaphore_signal(barrier, inc=1, device_id=device, device_id_type=MESH)

    def meet(self):
        pl.semaphore_wait(pltpu.get_barrier_semaphore(), 2 + self.line)

    def block(self, whole):
        return tuple(slice(None) if axis in whole else getattr(self, axis) for axis in "zyx")


def spot(place):
    return place[0].at[place[1]] if isinstance(place, tuple) else place


class Copy:
    def __init__(self, make):
        self.make = make

    def wait_recv(self):
        self.make(True).wait_recv()

    def wait_send(self):
        self.make(False).wait_send()

    def wait(self):
        self.wait_send()
        self.wait_recv()


class LocalCopy(Copy):
    def wait(self):
        self.make(False).wait()


class Copies:
    def __init__(self, sent, received, local):
        self.sent, self.received, self.local = sent, received, local
        self.count = self.local_count = 0
        self.open = []
        self.writes = []

    def start(self, source, target, device, landing, remember=True):
        number = self.count
        self.count += 1
        copy = Copy(
            lambda arriving: pltpu.make_async_remote_copy(
                src_ref=spot(source),
                dst_ref=spot(landing if arriving else target),
                send_sem=self.sent.at[number],
                recv_sem=self.received.at[number],
                device_id=device,
                device_id_type=MESH,
            )
        )
        copy.make(False).start()
        if remember:
            self.open.append(copy)
        return copy

    def read(self, source, target):
        number = self.local_count
        self.local_count += 1
        copy = LocalCopy(
            lambda arriving: pltpu.make_async_copy(spot(source), spot(target), self.local.at[number])
        )
        copy.make(False).start()
        return copy

    def write(self, source, target):
        self.writes.append(self.read(source, target))

    def finish(self):
        for copy in self.writes:
            copy.wait()
        for copy in self.open:
            copy.wait_send()


class Clock:
    def __init__(self, link, hop, far, slack, scale):
        self.scale = scale
        self.link, self.hop, self.far, self.slack = link, hop, far, slack
        self.now = 0.0
        self.free = dict.fromkeys("czyx", 0.0)

    def send(self, axis, size):
        rate = CORE_LINK if axis == "c" else self.link
        start = max(self.now, self.free[axis])
        self.free[axis] = start + size / rate
        return self.free[axis] + (1.5 if axis == "c" else self.far if axis == "z" else self.hop)


def volume(shape):
    return 2 * math.prod(shape)


class GatherUnit:
    def __init__(self, place, copies, clock, buffer, rows, columns, order):
        self.place, self.copies, self.clock, self.buffer = place, copies, clock, buffer
        self.area, self.order = (rows, columns), order + "c"
        self.held, self.stage, self.arrivals = "", 0, []
        self.size = volume((rows.size, columns.size))

    def view(self, index, half=None):
        half = self.place.core if half is None else half
        return self.buffer, (half,) + index + self.area

    def send(self):
        place = self.place
        axis = self.order[self.stage]
        mine = place.block(self.held)
        blocks = math.prod({"z": place.line, "y": 2, "x": 2}[held] for held in self.held)
        if axis == "z":
            moves = [(place.along(k), (place.behind(k),) + mine[1:], None) for k in range(1, place.line)]
            blocks *= place.line
        elif axis == "c":
            moves = [(place.across(axis), mine, place.other["c"])]
        else:
            level = "zyx".index(axis)
            moves = [(place.across(axis), mine[:level] + (place.other[axis],) + mine[level + 1 :], None)]
        self.arrivals = [
            self.copies.start(self.view(mine), self.view(mine), device, self.view(theirs, half))
            for device, theirs, half in moves
        ]
        self.due = self.clock.send(axis, blocks * self.size)
        self.held += axis
        self.stage += 1

    def step(self):
        for copy in self.arrivals:
            copy.wait_recv()
        self.clock.now = max(self.clock.now, self.due) + 0.1
        if self.stage == len(self.order):
            return True
        if self.stage == 1:
            self.begin()
        self.send()
        return False


class SumUnit:
    def __init__(self, place, copies, clock, total, landings, result, rows, columns, order):
        self.place, self.copies, self.clock, self.total = place, copies, clock, total
        self.landings, self.result, self.order = landings, result, order
        self.area = (rows, columns)
        self.left, self.stage, self.arrivals = "zyx", 0, []
        self.size = volume((rows.size, columns.size))

    def send(self):
        place, area, stage = self.place, self.area, self.stage
        axis = self.order[stage]
        mine = place.block(self.left)
        level = "zyx".index(axis)
        landing = self.landings[stage]
        self.left = self.left.replace(axis, "")
        each = math.prod({"z": place.line, "y": 2, "x": 2}[left] for left in self.left)
        blocks = each
        if axis == "z":
            moves = []
            for offset in range(1, place.line):
                span = pl.ds((offset - 1) * each, each) if each > 1 else offset - 1
                moves.append((place.along(offset), place.ahead(offset), span))
            blocks *= place.line
        else:
            span = pl.ds(0, each) if each > 1 else 0
            if stage == 0:
                span = (pl.ds(0, place.line), pl.ds(0, 2))
            moves = [(place.across(axis), place.other[axis], span)]
        self.arrivals = []
        for device, goal, span in moves:
            there = landing, (span if isinstance(span, tuple) else (span,)) + area
            source = self.total, mine[:level] + (goal,) + mine[level + 1 :] + area
            self.arrivals.append(self.copies.start(source, there, device, there))
        self.due = self.clock.send(axis, blocks * self.size)
        self.axis = axis
        self.stage += 1

    def send_slab(self, z):
        place, axis = self.place, self.order[0]
        index = (z, place.other[axis], slice(None)) if axis == "y" else (z, slice(None), place.other[axis])
        there = self.landings[0], (z, slice(None)) + self.area
        self.arrivals.append(
            self.copies.start((self.total, index + self.area), there, place.across(axis), there)
        )
        self.due = self.clock.send(axis, 2 * self.size)
        if z == place.line - 1:
            self.left = self.left.replace(axis, "")
            self.axis, self.stage = axis, 1

    def step(self):
        for copy in self.arrivals:
            copy.wait_recv()
        self.clock.now = max(self.clock.now, self.due) + 0.2
        place, area, landing, line = self.place, self.area, self.landings[self.stage - 1], self.place.line

        def add(index, spots):
            value = self.total[index + area].astype(jnp.float32)
            for one in spots:
                value += landing[one + area].astype(jnp.float32)
            return value

        def store(index, spots):
            self.total[index + area] = add(index, spots).astype(jnp.bfloat16)

        if self.stage == 3:
            count = line - 1 if self.axis == "z" else 1
            value = add((place.z, place.y, place.x), [(k,) for k in range(count)])
            put_halves(self.result, area, value)
            return True
        if self.stage == 1:

            def one(z, carry):
                for other in range(2):
                    store((z, place.y, other) if self.axis == "y" else (z, other, place.x), [(z, other)])
                return carry

            lax.fori_loop(0, line, one, 0)
        elif self.axis == "z":
            for other in range(2):
                index = (place.z, place.y, other) if self.left == "x" else (place.z, other, place.x)
                store(index, [(k * 2 + other,) for k in range(line - 1)])
        else:

            def one(z, carry):
                store((z, place.y, place.x), [(z,)])
                return carry

            lax.fori_loop(0, line, one, 0)
        self.send()
        return False


def put_halves(final, area, value):
    rows, columns = area
    half = final.shape[1]
    done = 0
    while done < rows.size:
        core, at = (rows.start + done) // half, (rows.start + done) % half
        step = min(rows.size - done, half - at)
        final[core, pl.ds(at, step), columns] = value[done : done + step]
        done += step


class Schedule:
    def __init__(self, clock, done):
        self.clock, self.done = clock, done
        self.tasks, self.flying = [], []

    def task(self, cost, function, *arguments, ready=lambda: True):
        self.tasks.append((cost, functools.partial(function, *arguments), ready))

    def launch(self, unit):
        unit.send()
        self.flying.append(unit)

    def run(self, drain=True):
        while self.tasks or (drain and self.flying):
            soonest = min(self.flying, key=lambda unit: unit.due) if self.flying else None
            runnable = self.tasks and self.tasks[0][2]()
            if soonest is not None and (soonest.due + self.clock.slack <= self.clock.now or not runnable):
                if soonest.step():
                    self.flying.remove(soonest)
                    self.done(soonest)
            else:
                cost, function, _ = self.tasks.pop(0)
                function()
                self.clock.now += cost * self.clock.scale


def padded(rows):
    return -(-rows // 16) * 16


def matrix(value):
    return value.reshape(-1, value.shape[-1])


def dot(left, right, contract=(1, 0)):
    return lax.dot_general(
        left, right, (((contract[0],), (contract[1],)), ((), ())), preferred_element_type=jnp.float32
    )


def whole(buffer):
    return jnp.concatenate([matrix(buffer[0]), matrix(buffer[1])], axis=1)


def column_spans(rows, columns):
    wide = 384 if rows <= 64 else 128
    return [pl.ds(column, wide) for column in range(0, columns, wide)]


def row_spans(rows):
    tall = rows
    return [pl.ds(row, tall) for row in range(0, rows, tall)]


def merged_rows(place, mine, other):
    mine, other = mine.astype(jnp.float32), other.astype(jnp.float32)
    first = jnp.where(place.core == 0, mine, other)
    second = jnp.where(place.core == 0, other, mine)
    return jnp.concatenate([first, second], axis=0).astype(jnp.bfloat16)


def column_half(place, values, own):
    half = values.shape[1] // 2
    left, right = values[:, :half].astype(jnp.float32), values[:, half:].astype(jnp.float32)
    return jnp.where((place.core == 0) == own, left, right)

def gelu_pair(values):
    half_square = jnp.exp(values * values * -0.5)
    size = jnp.abs(values)
    t = 1.0 / (1.0 + (0.3275911 * math.sqrt(0.5)) * size)
    series = t * (
        0.5 * 0.254829592
        + t * (-0.5 * 0.284496736 + t * (0.5 * 1.421413741 + t * (-0.5 * 1.453152027 + t * (0.5 * 1.061405429))))
    )
    tail = series * half_square
    phi = jnp.where(values < 0, tail, 1.0 - tail)
    slope = phi + values * half_square * (1.0 / math.sqrt(2.0 * math.pi))
    return values * phi, slope


def spread_vectors(vectors_all, rows_out, hidden_out, narrow, wide, line):
    lanes = lax.broadcasted_iota(jnp.int32, (16, 128), 1)
    sums = {id(rows_out): {}, id(hidden_out): {}}

    def place(target, values, start, size):
        found = sums[id(target)]
        tile, shift = start // 128, start % 128
        rolled = pltpu.roll(values, shift, 1) if shift else values
        lane = lanes[: values.shape[0]]
        first = jnp.where((lane >= shift) & (lane < shift + size), rolled, 0.0)
        found[tile] = found[tile] + first if tile in found else first
        if shift + size > 128:
            second = jnp.where(lane < shift + size - 128, rolled, 0.0)
            tile += 1
            found[tile] = found[tile] + second if tile in found else second

    for z in range(line):
        for y in range(2):
            for x in range(2):
                for core in range(2):
                    device = ((z * 2 + y) * 2 + x) * 2 + core
                    values = vectors_all[core, z, y, x].astype(jnp.float32)
                    place(rows_out, values, device * narrow, narrow)
                    place(hidden_out, values[8:], device * wide, wide)
    for target in (rows_out, hidden_out):
        for tile, value in sums[id(target)].items():
            target[:, pl.ds(tile * 128, 128)] = value

KEPT = ("qkv", "attention", "query", "key_value", "cross_attention", "normed", "inverse", "slope", "joined", "rows")
PAIRS = ("text", "patches", "context", "low_one", "context_cross", "low_two", "hidden_low")
LOCAL = ("hidden", "context", "low_one", "context_cross", "low_two", "hidden_low")


def forward_kernel(line, *refs):
    refs = list(refs)
    take = lambda names: named(names, [refs.pop(0) for _ in names])
    shards = take(WEIGHTS)
    gains, shifts, slim_bias, text, patches, pair_row, region_row = [refs.pop(0) for _ in range(7)]
    outs, kept_out, pairs = take(WEIGHTS), take(KEPT), take(PAIRS)
    buffers, outgoing, incoming = take(WEIGHTS), take(WEIGHTS), take(WEIGHTS)
    kept = named(KEPT + LOCAL, [refs.pop(0) for _ in KEPT + LOCAL])
    vectors, vectors_all, pair_column, work, keys_all, values_all, sent, received, local = refs
    place = Place(line)
    copies = Copies(sent, received, local)
    clock = Clock(55e3, 1.5, 4.5, -0.5, 1.0)
    tokens, width = text.shape
    rows_all, hidden_all = kept.rows, kept.hidden
    block = tokens // line
    narrow = shards.qkv.shape[0]
    keys = patches.shape[0]
    place.greet()
    for name in WEIGHTS:
        shard, target = getattr(shards, name), getattr(outgoing, name)
        away = column_half(place, shard[...], False)
        padding = target.shape[0] - shard.shape[0]
        if padding:
            away = jnp.concatenate([away, jnp.zeros((padding, away.shape[1]), jnp.float32)], axis=0)
        target[...] = away.astype(jnp.bfloat16)
    vectors[...] = jnp.zeros_like(vectors)
    vectors[pl.ds(0, 3), pl.ds(0, narrow)] = gains[...].astype(jnp.float32)
    vectors[pl.ds(3, 10), pl.ds(0, narrow)] = shifts[...].astype(jnp.float32)
    vectors[pl.ds(13, 1), pl.ds(0, slim_bias.shape[1])] = slim_bias[...].astype(jnp.float32)
    vectors_all[place.core, place.z, place.y, place.x] = vectors[...].astype(jnp.bfloat16)
    place.meet()
    swaps = {}
    for name in WEIGHTS:
        there = getattr(incoming, name)
        swaps[name] = copies.start(getattr(outgoing, name), there, place.across("c"), there)
    pair_column[...] = jnp.broadcast_to(pair_row[...].astype(jnp.float32), (128, tokens)).T
    arrivals = []

    def merge(name):
        swaps[name].wait_recv()
        shard = getattr(shards, name)
        mine = column_half(place, shard[...], True)
        other = getattr(incoming, name)[...][: shard.shape[0]]
        getattr(buffers, name)[place.core, place.z, place.y, place.x] = merged_rows(place, mine, other)

    def keep(source, target):
        copies.write(source, target)

    def pair(source, target, *columns):
        there = target.at[(place.core,) + columns]
        copies.write(source, there)
        arrivals.append(
            copies.start(source, there, place.across("c"), target.at[(1 - place.core,) + columns])
        )

    def row(number):
        return rows_all[pl.ds(number, 1), :]

    qkv, context, low_one, query, context_cross = (
        kept.qkv, kept.context, kept.low_one, kept.query, kept.context_cross
    )
    hidden, slope, low_two = kept.hidden_low, kept.slope, kept.low_two
    attention, cross_attention = kept.attention, kept.cross_attention
    key_value = kept.key_value

    def project_qkv(part):
        def one(half, carry):
            size = 384
            column = pl.multiple_of(half * (3 * size) + part * size, 128)
            value = dot(text[...], matrix(buffers.qkv[half, :, :, :, :, pl.ds(part * size, size)]))
            group = (half * 3 + part) // 2
            shift = pl.multiple_of(lax.rem(half * 3 + part, 2) * size, 128)
            biased = jnp.where(
                group == 0,
                rows_all[pl.ds(3, 1), pl.ds(shift, size)],
                jnp.where(group == 1, 0.0, rows_all[pl.ds(4, 1), pl.ds(shift, size)]),
            )
            qkv[:, pl.ds(column, size)] = (value + biased).astype(jnp.bfloat16)
            return carry

        lax.fori_loop(0, 2, one, 0)

    strip = 128

    def attend(pair):
        lane = lax.broadcasted_iota(jnp.int32, (strip, 128), 1)
        columns = pl.ds(pair * 128, 128)

        def one(number, carry):
            rows = pl.ds(pl.multiple_of(number * strip, strip), strip)
            two = qkv[rows, columns].astype(jnp.float32) * (1.0 / math.sqrt(HD))
            key_rows = qkv[:, pl.ds(width + pair * 128, 128)]
            value_rows = qkv[:, pl.ds(2 * width + pair * 128, 128)]
            same = jnp.concatenate([pair_column[rows, :]] * (tokens // 128), axis=1) == pair_row[...].astype(
                jnp.float32
            )
            result = None
            for head in range(2):
                own = (lane < HD) if head == 0 else (lane >= HD)
                scores = dot(jnp.where(own, two, 0.0).astype(jnp.bfloat16), key_rows, (1, 1))
                scores = jnp.where(same, scores, NEGATIVE)
                scores = jnp.exp(scores - jnp.max(scores, axis=1, keepdims=True))
                scores = scores * (1.0 / jnp.sum(scores, axis=1, keepdims=True))
                low = scores.astype(jnp.bfloat16)
                attention[pair * 2 + head, rows, :] = low
                value = dot(low, value_rows)
                result = value if head == 0 else jnp.where(own, value, result)
            context[rows, columns] = result.astype(jnp.bfloat16)
            return carry

        lax.fori_loop(0, tokens // strip, one, 0)
        keep(attention.at[pl.ds(2 * pair, 2)], kept_out.attention.at[pl.ds(2 * pair, 2)])

    def normalize(number, summed, low):
        normed, inverse = kept.normed, kept.inverse
        gain, shift = row(number), row(10 + number)
        step = 64

        def one(index, carry):
            rows = pl.ds(pl.multiple_of(index * step, step), step)
            value = work[rows, :] + summed(rows)
            center = value - jnp.mean(value, axis=1, keepdims=True)
            scale = lax.rsqrt(jnp.mean(center * center, axis=1, keepdims=True) + EPSILON)
            value = center * scale
            normed[number, rows, :] = value
            inverse[number, rows, :] = jnp.broadcast_to(scale, (step, 128))
            low(rows, value * gain + shift)
            return carry

        lax.fori_loop(0, tokens // step, one, 0)
        keep(normed.at[number], kept_out.normed.at[number])
        keep(inverse.at[number], kept_out.inverse.at[number])

    def self_out():
        work[...] = dot(context[...], whole(buffers.sout))

        def low(rows, value):
            low_one[rows, :] = value.astype(jnp.bfloat16)

        normalize(0, lambda rows: text[rows, :].astype(jnp.float32) + row(5), low)
        pair(context, pairs.context)
        pair(low_one, pairs.low_one)

    def project_patches(part):
        size = 384
        value = dot(patches[...], matrix(buffers.ckv[0, :, :, :, :, pl.ds(part * size, size)]))
        key_value[place.z, :, pl.ds(part * size, size)] = value.astype(jnp.bfloat16)
        value = dot(patches[...], matrix(buffers.ckv[1, :, :, :, :, pl.ds(part * size, size)]))
        value += rows_all[pl.ds(7, 1), pl.ds(part * size, size)]
        key_value[place.z, :, pl.ds(width + part * size, size)] = value.astype(jnp.bfloat16)

    shared = []

    def share_keys():
        for offset in range(1, line):
            origin = place.behind(offset)
            shared.append(
                copies.start(
                    key_value.at[place.z], key_value.at[place.z], place.along(offset), key_value.at[origin]
                )
            )

    def project_query():
        work[...] = dot(low_one[...], whole(buffers.cq))
        query[...] = (work[...] + row(6)).astype(jnp.bfloat16)
        keep(query, kept_out.query)

    def cross(owner):
        if owner == 0:
            for copy in shared:
                copy.wait_recv()
            keep(key_value, kept_out.key_value)
        lane = lax.broadcasted_iota(jnp.int32, (keys, width), 1) // HD
        for head in range(H):
            rows = pl.ds(head * keys, keys)
            keys_all[rows, :] = jnp.where(
                lane == head, key_value[owner, :, pl.ds(0, width)].astype(jnp.float32), 0.0
            ).astype(jnp.bfloat16)
            values_all[rows, :] = jnp.where(
                lane == head, key_value[owner, :, pl.ds(width, width)].astype(jnp.float32), 0.0
            ).astype(jnp.bfloat16)
        rows = pl.ds(owner * block, block)
        scores = dot(keys_all[...], query[rows, :], (1, 1)) * (1.0 / math.sqrt(HD))
        region = lax.broadcasted_iota(jnp.int32, (keys, block), 0) // PR
        same = region == region_row[:, rows]
        scores = jnp.where(same[None], scores.reshape(H, keys, block), NEGATIVE)
        scores = jnp.exp(scores - jnp.max(scores, axis=1, keepdims=True))
        scores = scores * (1.0 / jnp.sum(scores, axis=1, keepdims=True))
        scores = scores.reshape(H * keys, block).astype(jnp.bfloat16)
        cross_attention[owner] = scores
        context_cross[rows, :] = dot(scores, values_all[...], (0, 0)).astype(jnp.bfloat16)
        if owner == line - 1:
            keep(cross_attention, kept_out.cross_attention)
            pair(context_cross, pairs.context_cross)

    def cross_out():
        work[...] = dot(context_cross[...], whole(buffers.cout))
        first_gain, first_shift = row(0), row(10)

        def low(rows, value):
            low_two[rows, :] = value.astype(jnp.bfloat16)

        normalize(1, lambda rows: kept.normed[0, rows, :] * first_gain + first_shift + row(8), low)
        pair(low_two, pairs.low_two)

    def expand(part, half):
        size = 384
        half_width = buffers.up.shape[5]
        columns = pl.ds(half * half_width + part * size, size)
        value = dot(low_two[...], matrix(buffers.up[half, :, :, :, :, pl.ds(part * size, size)]))
        value, grad = gelu_pair(value + hidden_all[pl.ds(5, 1), columns])
        hidden[:, columns] = value.astype(jnp.bfloat16)
        slope[:, columns] = grad.astype(jnp.bfloat16)
        pair(hidden.at[:, columns], pairs.hidden_low, slice(None), columns)
        keep(slope.at[:, columns], kept_out.slope.at[:, columns])

    def contract(part):
        size = 128
        buffer = buffers.down
        columns = pl.ds(part * size, size)
        both = jnp.concatenate(
            [matrix(buffer[0, :, :, :, :, columns]), matrix(buffer[1, :, :, :, :, columns])], axis=1
        )
        value = dot(hidden[...], both)
        work[:, pl.ds(part * size, size)] = value[:, :size]
        work[:, pl.ds(width // 2 + part * size, size)] = value[:, size:]

    def finish():
        gain, shift = row(1), row(11)

        def low(rows, value):
            valid = jnp.concatenate([pair_column[rows, :]] * (width // 128), axis=1) >= 0
            kept.joined[rows, :] = jnp.where(valid, value, 0.0).astype(jnp.bfloat16)

        normalize(2, lambda rows: kept.normed[1, rows, :] * gain + shift + row(9), low)
        keep(kept.joined, kept_out.joined)

    present, counts = {}, {}
    waiting = []
    merged = set()

    def done(unit):
        present[unit.name] = present.get(unit.name, 0) + 1
        name = unit.name
        if present[name] == counts.get(name):
            keep(getattr(buffers, name), getattr(outs, name))

    schedule = Schedule(clock, done)

    def begin():
        if waiting:
            unit = waiting.pop(0)
            if unit.name and unit.name not in merged:
                merge(unit.name)
                merged.add(unit.name)
            schedule.launch(unit)

    def unit_of(buffer, name, rows, columns):
        order = ("zyx", "zxy")[len(waiting) % 2]
        unit = GatherUnit(place, copies, clock, buffer, rows, columns, order)
        unit.name, unit.begin = name, begin
        waiting.append(unit)

    unit_of(vectors_all, "", pl.ds(0, 16), pl.ds(0, 128))
    for name in WEIGHTS:
        buffer = getattr(buffers, name)
        spans = column_spans(*buffer.shape[4:])
        rows = row_spans(buffer.shape[4])
        counts[name] = len(spans) * len(rows)
        for columns in spans:
            for span in rows:
                unit_of(buffer, name, span, columns)

    def task(name, count, cost, function, *arguments):
        schedule.task(cost, function, *arguments, ready=lambda: present.get(name, 0) >= count)

    def spread():
        spread_vectors(vectors_all, rows_all, hidden_all, narrow, shards.down.shape[0], line)
        keep(rows_all, kept_out.rows)

    pair(text, pairs.text)
    pair(patches, pairs.patches)
    task("", 1, 1.0, spread)
    for part in range(3):
        task("qkv", part + 1, 1.5, project_qkv, part)
    task("", 1, 0.0, keep, qkv, kept_out.qkv)
    for number in range(H // 2):
        task("", 1, 1.8, attend, number)
        if number == 3:
            for part in range(2):
                task("ckv", part + 1, 0.5, project_patches, part)
            task("", 1, 0.1, share_keys)
    task("sout", 1, 2.0, self_out)
    task("cq", 1, 1.0, project_query)
    for owner in range(line):
        task("", 1, 1.5, cross, owner)
    task("cout", 1, 2.0, cross_out)
    for part in range(4):
        for half in range(2):
            task("up", part + 1, 1.5, expand, part, half)
    for part in range(3):
        task("down", part + 1, 1.5, contract, part)
    task("", 1, 1.5, finish)
    for _ in range(3):
        begin()
    schedule.run()
    for copy in arrivals:
        copy.wait_recv()
    copies.finish()

SAVED = ("qkv", "attention", "query", "key_value", "cross_attention", "normed", "inverse", "slope", "rows")
ORDERS = ("xyz", "yxz")


class VectorUnit:
    def __init__(self, place, copies, clock, total, landings):
        self.place, self.copies, self.clock = place, copies, clock
        self.total, self.landings = total, landings
        self.stage = 0

    def send(self):
        place, stage = self.place, self.stage
        if stage < 3:
            devices = [place.across("cxy"[stage])]
        else:
            devices = [place.along(offset) for offset in range(1, place.line)]
        self.arrivals = []
        for number, device in enumerate(devices):
            there = self.landings, (stage + number,)
            self.arrivals.append(self.copies.start(self.total, there, device, there, False))
        self.due = self.clock.now + 3.0
        self.stage += 1

    def step(self):
        for copy in self.arrivals:
            copy.wait()
        value = self.total[...]
        for number in range(len(self.arrivals)):
            value += self.landings[self.stage - 1 + number]
        self.total[...] = value
        self.clock.now = max(self.clock.now, self.due) + 0.1
        if self.stage == 4:
            return True
        self.send()
        return False


def backward_kernel(line, *refs):
    refs = list(refs)
    take = lambda names: named(names, [refs.pop(0) for _ in names])
    pop = lambda count: [refs.pop(0) for _ in range(count)]
    weights, saved, pairs = take(WEIGHTS), take(SAVED), take(PAIRS)
    cotangent, pair_row = pop(2)
    outs = take(WEIGHTS)
    text_grad, patch_grad, gains_out, biases_out, hidden_out = pop(5)
    totals, first, second, third, finals, swapped, landed = (take(WEIGHTS) for _ in range(7))
    work, inverse, rows_all, small, small_landed, key_parts, key_landed, pair_column, hidden_sum = pop(9)
    grad_kv, sent, received, local = pop(4)
    place = Place(line)
    copies = Copies(sent, received, local)
    clock = Clock(60e3, 4.0, 24.0, 3.0, 1.15)
    core = place.core
    tokens, width = work.shape
    hidden_width = hidden_sum.shape[1]
    block = tokens // line
    keys = grad_kv.shape[0]
    scaling = 1.0 / math.sqrt(HD)
    remaining = {}
    swaps = {}

    def done(unit):
        if unit is vectors:
            return
        remaining[unit.name] -= 1
        if not remaining[unit.name]:
            final, there = getattr(finals, unit.name), getattr(swapped, unit.name)
            swaps[unit.name] = copies.start((final, (place.other["c"],)), there, place.across("c"), there)

    schedule = Schedule(clock, done)
    vectors = VectorUnit(place, copies, clock, small, small_landed)

    def prepare(name, rows, columns, count):
        remaining.setdefault(name, count)
        landings = [getattr(group, name) for group in (first, second, third)]
        order = ORDERS[prepare.number % len(ORDERS)]
        prepare.number += 1
        unit = SumUnit(
            place, copies, clock, getattr(totals, name), landings, getattr(finals, name), rows, columns, order
        )
        unit.name = name
        return unit

    def launch(*arguments):
        schedule.launch(prepare(*arguments))

    prepare.number = 0

    def task(cost, function, *arguments):
        schedule.task(cost, function, *arguments)

    def half(size, other=False, offset=0, part=None):
        which = 1 - core if other else core
        return pl.ds(pl.multiple_of(which * size + offset, 128), size if part is None else part)

    def hand_over(source, target, columns=None):
        size = target.shape[1]
        there = target if columns is None else (target, (slice(None), columns))
        away = half(size, True) if columns is None else half(size, True, columns.start, columns.size)
        return copies.start((source, (slice(None), away)), there, place.across("c"), there, False)

    def norm_back(number, bias_number, normed, upstream, low):
        gain = rows_all[pl.ds(number, 1), :]
        step = 64

        def one(index, carry):
            rows = pl.ds(pl.multiple_of(index * step, step), step)
            grad, normal = upstream(rows), normed[rows, :]
            scaled = grad * gain
            center = scaled - jnp.mean(scaled, axis=1, keepdims=True)
            center -= normal * jnp.mean(scaled * normal, axis=1, keepdims=True)
            value = inverse[number, rows, :][:, :1] * center
            work[rows, :] = value
            rounded = value.astype(jnp.bfloat16)
            low[rows, :] = rounded
            sums = (grad * normal, grad, rounded.astype(jnp.float32))
            return tuple(old + jnp.sum(new, axis=0, keepdims=True) for old, new in zip(carry, sums))

        zero = jnp.zeros((1, width), jnp.float32)
        gain_sum, shift_sum, bias_sum = lax.fori_loop(0, tokens // step, one, (zero, zero, zero))
        small[pl.ds(number, 1), :] = gain_sum
        small[pl.ds(10 + number, 1), :] = shift_sum
        small[pl.ds(bias_number, 1), :] = bias_sum

    def weight_grad(name, inputs, low, landing, columns, span=None):
        size = landing.shape[1]
        own = half(size, False, columns.start, columns.size)
        span = slice(None) if span is None else span
        value = dot(inputs[core, :, span], low[:, own], (0, 0))
        value += dot(inputs[1 - core, :, span], landing[:, columns], (0, 0))
        return value.astype(jnp.bfloat16)

    def spread_columns(name, inputs, low, columns, count, pieces=1):
        total = getattr(totals, name)
        value = weight_grad(name, inputs, low, getattr(landed, name), columns)
        total[:, :, :, :, columns] = value.reshape(total.shape[:4] + (columns.size,))
        for start in range(0, columns.size, columns.size // pieces):
            piece = pl.ds(columns.start + start, columns.size // pieces)
            launch(name, pl.ds(0, total.shape[3]), piece, count)

    def feed_forward(up, down, inputs_up, inputs_down, slope, normed, grad_low, cotangent_here):
        reads = [
            copies.read(source, target)
            for source, target in (
                (cotangent, cotangent_here),
                (saved.normed.at[2], normed),
                (saved.inverse, inverse),
                (saved.rows, rows_all),
                (weights.down, down),
                (saved.slope, slope),
                (pairs.hidden_low, inputs_down),
                (pairs.low_two, inputs_up),
                (weights.up, up),
            )
        ]
        sends = []

        def third_norm():
            for copy in reads[:4]:
                copy.wait()
            small[...] = jnp.zeros_like(small)

            def upstream(rows):
                valid = jnp.concatenate([pair_column[rows, :]] * (width // 128), axis=1) >= 0
                return jnp.where(valid, cotangent_here[rows, :].astype(jnp.float32), 0.0)

            norm_back(2, 9, normed, upstream, grad_low)
            place.meet()
            sends.append(hand_over(grad_low, landed.down))

        size = 384
        half_width = hidden_width // 2

        def expand(other):
            if other:
                for copy in reads[4:6]:
                    copy.wait()

            def one(part, carry):
                column = (1 - core if other else core) * half_width + part * size
                number = column // size
                both = jnp.concatenate(
                    [matrix(down[side, number // 2, lax.rem(number, 2)]) for side in range(2)], axis=1
                )
                columns = pl.ds(pl.multiple_of(column, 128), size)
                value = dot(grad_low[...], both, (1, 1)) * slope[:, columns].astype(jnp.float32)
                value = value.astype(jnp.bfloat16)
                slope[:, columns] = value
                hidden_sum[pl.ds(0, 1), columns] = jnp.sum(value.astype(jnp.float32), axis=0, keepdims=True)
                return carry

            lax.fori_loop(0, half_width // size, one, 0)
            if other:
                sends.append(hand_over(slope, landed.up))

        def grad_down():
            reads[6].wait()
            sends[0].wait_recv()
            total = totals.down
            tall = 48
            count = total.shape[3] // tall
            units = [
                prepare("down", pl.ds(row * tall, tall), pl.ds(0, width // 2), count) for row in range(count)
            ]
            slab = hidden_width // line
            for z in range(line):
                span = pl.ds(z * slab, slab)
                value = weight_grad("down", inputs_down, grad_low, landed.down, pl.ds(0, width // 2), span)
                total[z] = value.reshape(total.shape[1:])
                clock.now += 1.0
                for unit in units:
                    unit.send_slab(z)
            schedule.flying.extend(units)

        def grad_up(part):
            if part == 0:
                reads[7].wait()
                sends[1].wait_recv()
                for k in range(4):
                    small[pl.ds(13 + k, 1), :] = hidden_sum[pl.ds(0, 1), pl.ds(k * width, width)]
            spread_columns("up", inputs_up, slope, pl.ds(part * size, size), half_width // size)

        def grad_second():
            reads[8].wait()
            for side in range(2):
                work[...] += dot(slope[:, pl.ds(side * half_width, half_width)], matrix(up[side]), (1, 1))

        task(2.0, third_norm)
        task(2.0, expand, True)
        task(0.0, grad_down)
        task(2.0, expand, False)
        for part in range(half_width // size):
            task(1.2, grad_up, part)
        task(3.0, grad_second)
        schedule.run(False)
        for copy in sends:
            copy.wait_send()

    def attentions(qkv_w, ckv_w, sout_w, cq_w, cout_w, left_one, left_two, patch_pair, normed, query, key_value,
                   cross_attention, keys_all, values_all, qkv, attention, scores_low, grad_two_low, grad_query,
                   grad_one_low, grad_context):
        order = (
            (saved.normed.at[1], normed.at[1]),
            (weights.cout, cout_w),
            (pairs.context_cross, left_one),
            (saved.key_value, key_value),
            (saved.cross_attention, cross_attention),
            (saved.query, query),
            (weights.cq, cq_w),
            (saved.normed.at[0], normed.at[0]),
            (pairs.low_one, left_two),
            (weights.sout, sout_w),
            (weights.ckv, ckv_w),
            (pairs.patches, patch_pair),
            (saved.qkv, qkv),
            (saved.attention.at[pl.ds(0, 2)], attention.at[0]),
            (weights.qkv, qkv_w),
        )
        reads = [copies.read(source, target) for source, target in order]
        waited = set()
        later = {}
        sends = {}
        size = 384
        third_part = pl.ds(0, width // 2)

        def need(*numbers):
            for number in numbers:
                if number not in waited:
                    reads[number].wait()
                    waited.add(number)

        def second_norm():
            need(0)
            norm_back(1, 8, normed.at[1], lambda rows: work[rows, :], grad_two_low)
            sends["t"] = hand_over(grad_two_low, landed.cout)

        def context_grad():
            need(1)
            grad_context[...] = dot(grad_two_low[...], whole(cout_w), (1, 1)).astype(jnp.bfloat16)

        def cross(offset):
            need(3, 4, 5)
            owner = place.ahead(offset)
            lane = lax.broadcasted_iota(jnp.int32, (keys, width), 1) // HD
            key_rows = key_value[owner, :, pl.ds(0, width)].astype(jnp.float32)
            value_rows = key_value[owner, :, pl.ds(width, width)].astype(jnp.float32)
            for head in range(H):
                rows = pl.ds(head * keys, keys)
                keys_all[rows, :] = jnp.where(lane == head, key_rows, 0.0).astype(jnp.bfloat16)
                values_all[rows, :] = jnp.where(lane == head, value_rows, 0.0).astype(jnp.bfloat16)
            rows = pl.ds(pl.multiple_of(owner * block, block), block)
            probability = cross_attention[owner].astype(jnp.float32).reshape(H, keys, block)
            grad = dot(values_all[...], grad_context[rows, :], (1, 1)).reshape(H, keys, block)
            grad = probability * (grad - jnp.sum(probability * grad, axis=1, keepdims=True))
            grad = grad.reshape(H * keys, block).astype(jnp.bfloat16)
            grad_query[rows, :] = (dot(grad, keys_all[...], (0, 0)) * scaling).astype(jnp.bfloat16)
            lane = lax.broadcasted_iota(jnp.int32, (keys, 128), 1)
            for pair in range(H // 2):
                columns = pl.ds(pair * 128, 128)
                heads = slice(pair * 2 * keys, (pair + 1) * 2 * keys)
                value = dot(grad[heads], query[rows, columns]) * scaling
                key_parts[offset, :, columns] = jnp.where(lane < HD, value[:keys], value[keys:]).astype(
                    jnp.bfloat16
                )
                value = dot(cross_attention[owner, pl.ds(heads.start, 2 * keys), :], grad_context[rows, columns])
                key_parts[offset, :, pl.ds(width + pair * 128, 128)] = jnp.where(
                    lane < HD, value[:keys], value[keys:]
                ).astype(jnp.bfloat16)
            if offset:
                there = key_landed, (offset - 1,)
                sends[offset] = copies.start((key_parts, (offset,)), there, place.along(offset), there)
            if offset == 0:
                sends["q"] = hand_over(grad_query, landed.cq)

        def grad_cout():
            need(2)
            sends["t"].wait_recv()
            spread_columns("cout", left_one, grad_two_low, third_part, 1)
            later["context"] = copies.read(pairs.context, left_one)

        def grad_first():
            need(6)
            work[...] += dot(grad_query[...], whole(cq_w), (1, 1))
            small[pl.ds(6, 1), :] = jnp.sum(grad_query[...].astype(jnp.float32), axis=0, keepdims=True)

        def first_norm():
            need(7)
            norm_back(0, 5, normed.at[0], lambda rows: work[rows, :], grad_one_low)
            sends["s"] = hand_over(grad_one_low, landed.sout)

        def grad_cq():
            need(8)
            sends["q"].wait_recv()
            spread_columns("cq", left_two, grad_query, third_part, 1)
            later["text"] = copies.read(pairs.text, left_two)

        def self_context():
            need(9)
            grad_context[...] = dot(grad_one_low[...], whole(sout_w), (1, 1)).astype(jnp.bfloat16)

        def grad_sout():
            later["context"].wait()
            sends["s"].wait_recv()
            spread_columns("sout", left_one, grad_one_low, third_part, 1)

        def key_grad():
            value = key_parts[0].astype(jnp.float32)
            for offset in range(1, line):
                sends[offset].wait_recv()
                value += key_landed[offset - 1].astype(jnp.float32)
            value = value.astype(jnp.bfloat16)
            grad_kv[...] = value
            sends["k"] = hand_over(grad_kv, landed.ckv)
            small[pl.ds(7, 1), :] = jnp.sum(value[:, width:].astype(jnp.float32), axis=0, keepdims=True)
            need(10)
            patch_grad[...] = dot(grad_kv[...], whole(ckv_w), (1, 1))

        def grad_ckv(part):
            if part == 0:
                need(11)
                sends["k"].wait_recv()
            spread_columns("ckv", patch_pair, grad_kv, pl.ds(part * size, size), 2)

        strip = 128

        def attend(pair):
            slot = pair % 2
            if pair == 0:
                need(12, 13)
            else:
                later[pair].wait()
            if pair + 1 < H // 2:
                later[pair + 1] = copies.read(
                    saved.attention.at[pl.ds(2 * pair + 2, 2)], attention.at[1 - slot]
                )
            columns, key_columns = pl.ds(pair * 128, 128), pl.ds(width + pair * 128, 128)
            value_columns = pl.ds(2 * width + pair * 128, 128)

            def own(value, head):
                lane = lax.broadcasted_iota(jnp.int32, value.shape, 1)
                return jnp.where((lane < HD) == (head == 0), value.astype(jnp.float32), 0.0).astype(jnp.bfloat16)

            def one(number, carry):
                rows = pl.ds(pl.multiple_of(number * strip, strip), strip)
                for head in range(2):
                    grad = dot(own(grad_context[rows, columns], head), qkv[:, value_columns], (1, 1))
                    probability = attention[slot, head, rows, :].astype(jnp.float32)
                    grad = probability * (grad - jnp.sum(probability * grad, axis=1, keepdims=True))
                    scores_low[head, rows, :] = grad.astype(jnp.bfloat16)
                return carry

            lax.fori_loop(0, tokens // strip, one, 0)
            query_grad = key_grad = value_grad = 0.0
            for head in range(2):
                query_grad += dot(scores_low[head], own(qkv[:, key_columns], head))
                key_grad += dot(scores_low[head], own(qkv[:, columns], head), (0, 0))
                value_grad += dot(attention[slot, head], own(grad_context[:, columns], head), (0, 0))
            query_grad = (query_grad * scaling).astype(jnp.bfloat16)
            value_grad = value_grad.astype(jnp.bfloat16)
            qkv[:, columns] = query_grad
            qkv[:, key_columns] = (key_grad * scaling).astype(jnp.bfloat16)
            qkv[:, value_columns] = value_grad
            small[pl.ds(3, 1), columns] = jnp.sum(query_grad.astype(jnp.float32), axis=0, keepdims=True)
            small[pl.ds(4, 1), columns] = jnp.sum(value_grad.astype(jnp.float32), axis=0, keepdims=True)
            if pair + 1 == H // 2:
                sends["p"] = hand_over(qkv, landed.qkv)
                schedule.launch(vectors)

        def grad_qkv(part):
            if part == 0:
                later["text"].wait()
                sends["p"].wait_recv()
            spread_columns("qkv", left_two, qkv, pl.ds(part * size, size), 5, 3 if part == 2 else 1)

        def text_back(side):
            need(14)
            size = 3 * width // 2
            work[...] += dot(qkv[:, pl.ds(side * size, size)], matrix(qkv_w[side]), (1, 1))
            if side == 1:
                copies.write(work, text_grad)

        task(2.0, second_norm)
        task(1.0, context_grad)
        task(1.0, grad_cout)
        for offset in list(range(1, line)) + [0]:
            task(2.0, cross, offset)
        task(1.0, grad_first)
        task(2.0, first_norm)
        task(1.0, grad_cq)
        task(1.0, self_context)
        task(1.0, key_grad)
        task(1.0, grad_sout)
        for part in range(2):
            task(0.5, grad_ckv, part)
        for number in range(H // 2):
            task(2.5, attend, number)
        for part in range(3):
            task(1.2, grad_qkv, part)
        for side in range(2):
            task(1.5, text_back, side)
        schedule.run()
        for name in ("t", "q", "s", "k", "p"):
            sends[name].wait_send()

    place.greet()
    pair_column[...] = jnp.broadcast_to(pair_row[...].astype(jnp.float32), (128, tokens)).T
    low = jnp.bfloat16
    wide = (tokens, hidden_width)
    rows = (tokens, width)
    shape = lambda ref: pltpu.VMEM(ref.shape, ref.dtype)
    pl.run_scoped(
        feed_forward,
        shape(weights.up),
        shape(weights.down),
        shape(pairs.low_two),
        shape(pairs.hidden_low),
        pltpu.VMEM(wide, low),
        pltpu.VMEM(rows, jnp.float32),
        pltpu.VMEM(rows, low),
        pltpu.VMEM(rows, low),
    )
    pl.run_scoped(
        attentions,
        shape(weights.qkv),
        shape(weights.ckv),
        shape(weights.sout),
        shape(weights.cq),
        shape(weights.cout),
        shape(pairs.context),
        shape(pairs.context),
        shape(pairs.patches),
        pltpu.VMEM((2,) + rows, jnp.float32),
        shape(saved.query),
        shape(saved.key_value),
        shape(saved.cross_attention),
        pltpu.VMEM((H * keys, width), low),
        pltpu.VMEM((H * keys, width), low),
        shape(saved.qkv),
        pltpu.VMEM((2, 2, tokens, tokens), low),
        pltpu.VMEM((2, tokens, tokens), low),
        pltpu.VMEM(rows, low),
        pltpu.VMEM(rows, low),
        pltpu.VMEM(rows, low),
        pltpu.VMEM(rows, low),
    )
    device = place.z * 8 + place.f
    value = small[...]
    narrow, slim = gains_out.shape[1], hidden_out.shape[1]
    turned = pltpu.roll(value, lax.rem(width - device * narrow, width), 1)
    gains_out[...] = turned[:3, :narrow]
    biases_out[...] = turned[3:13, :narrow]
    number = lax.broadcasted_iota(jnp.int32, value.shape, 0)
    picked = jnp.sum(jnp.where(number == 13 + place.z, value, 0.0), axis=0, keepdims=True)
    picked = pltpu.roll(jnp.broadcast_to(picked, (8, width)), lax.rem(width - place.f * slim, width), 1)
    hidden_out[...] = picked[:1, :slim]
    for name in WEIGHTS:
        swaps[name].wait_recv()
        out = getattr(outs, name)
        mine, other = getattr(finals, name)[core], getattr(swapped, name)[...]
        middle = mine.shape[1]
        out[:, :middle] = jnp.where(core == 0, mine, other)
        out[:, middle:] = jnp.where(core == 0, other, mine)
    copies.finish()


def gathered(line, shards):
    return [(2, line, 2, 2, 2 * shard.shape[0], shard.shape[1] // 2) for shard in shards]


def forward_all(line, shards, gains, shifts, slim_bias, text, patches, pair_row, region_row):
    tokens, width = text.shape
    keys, depth = patches.shape
    wide = shards[5].shape[1]
    low, full = jnp.bfloat16, jnp.float32
    rows = (tokens, width)
    kept = [
        ((tokens, 3 * width), low),
        ((H, tokens, tokens), low),
        (rows, low),
        ((line, keys, 2 * width), low),
        ((line, H * keys, tokens // line), low),
        ((3,) + rows, full),
        ((3, tokens, 128), full),
        ((tokens, wide), low),
        (rows, low),
        ((16, width), full),
    ]
    locals_ = [((8, wide), full), (rows, low), (rows, low), (rows, low), (rows, low), ((tokens, wide), low)]
    paired = [rows, (keys, depth), rows, rows, rows, rows, (tokens, wide)]
    shapes = gathered(line, shards)
    out_shape = [jax.ShapeDtypeStruct(shape, low) for shape in shapes]
    out_shape += [jax.ShapeDtypeStruct(*shape) for shape in kept]
    out_shape += [jax.ShapeDtypeStruct((2,) + shape, low) for shape in paired]
    scratch = [pltpu.VMEM(shape, low) for shape in shapes]
    for _ in range(2):
        scratch += [pltpu.VMEM((padded(shard.shape[0]), shard.shape[1] // 2), low) for shard in shards]
    scratch += [pltpu.VMEM(*shape) for shape in kept + locals_]
    scratch += [
        pltpu.VMEM((16, 128), full),
        pltpu.VMEM((2, line, 2, 2, 16, 128), low),
        pltpu.VMEM((tokens, 128), full),
        pltpu.VMEM(rows, full),
        pltpu.VMEM((H * keys, width), low),
        pltpu.VMEM((H * keys, width), low),
        pltpu.SemaphoreType.DMA((160,)),
        pltpu.SemaphoreType.DMA((160,)),
        pltpu.SemaphoreType.DMA((96,)),
    ]
    outs = pl.pallas_call(
        functools.partial(forward_kernel, line),
        out_shape=out_shape,
        in_specs=[pl.BlockSpec(memory_space=pltpu.VMEM)] * (len(shards) + 7),
        out_specs=[pl.BlockSpec(memory_space=pl.ANY)] * len(out_shape),
        scratch_shapes=scratch,
        compiler_params=pltpu.CompilerParams(
            collective_id=0, has_side_effects=True, vmem_limit_bytes=62 * 2**20
        ),
    )(*shards, gains, shifts, slim_bias, text, patches, pair_row, region_row)
    count = len(shards)
    return outs[:count], outs[count : count + len(kept)], outs[count + len(kept) :]


def backward_all(line, weights, saved, pairs, cotangent, pair_row, narrow, slim):
    low, full = jnp.bfloat16, jnp.float32
    tokens, width = cotangent.shape
    keys, depth = pairs[1].shape[1:]
    wide = pairs[-1].shape[2]
    sizes = [weight.shape[4:] for weight in weights]
    scratch = []
    for lead in ((line, 2, 2), (line, 2), (line,), (line - 1,)):
        scratch += [pltpu.VMEM(lead + size, low) for size in sizes]
    scratch += [pltpu.VMEM((2, size[0] // 2, size[1]), full) for size in sizes]
    scratch += [pltpu.VMEM((size[0] // 2, size[1]), full) for size in sizes]
    for name, size in zip(WEIGHTS, sizes):
        scratch.append(pltpu.VMEM((keys if name == "ckv" else tokens, size[1]), low))
    scratch += [
        pltpu.VMEM((tokens, width), full),
        pltpu.VMEM((3, tokens, 128), full),
        pltpu.VMEM((16, width), full),
        pltpu.VMEM((24, width), full),
        pltpu.VMEM((2 + line, 24, width), full),
        pltpu.VMEM((line, keys, 2 * width), low),
        pltpu.VMEM((line - 1, keys, 2 * width), low),
        pltpu.VMEM((tokens, 128), full),
        pltpu.VMEM((8, wide), full),
        pltpu.VMEM((keys, 2 * width), low),
        pltpu.SemaphoreType.DMA((160,)),
        pltpu.SemaphoreType.DMA((160,)),
        pltpu.SemaphoreType.DMA((64,)),
    ]
    out_shape = [jax.ShapeDtypeStruct((size[0] // 2, 2 * size[1]), full) for size in sizes]
    out_shape += [
        jax.ShapeDtypeStruct((tokens, width), full),
        jax.ShapeDtypeStruct((keys, depth), full),
        jax.ShapeDtypeStruct((3, narrow), full),
        jax.ShapeDtypeStruct((10, narrow), full),
        jax.ShapeDtypeStruct((1, slim), full),
    ]
    vmem, anywhere = pl.BlockSpec(memory_space=pltpu.VMEM), pl.BlockSpec(memory_space=pl.ANY)
    count = len(weights)
    outs = pl.pallas_call(
        functools.partial(backward_kernel, line),
        out_shape=out_shape,
        in_specs=[anywhere] * (count + len(saved) + len(pairs) + 1) + [vmem],
        out_specs=[vmem] * count + [anywhere] + [vmem] * 4,
        scratch_shapes=scratch,
        compiler_params=pltpu.CompilerParams(
            collective_id=1, has_side_effects=True, vmem_limit_bytes=63 * 2**20
        ),
    )(*weights, *saved, *pairs, cotangent, pair_row)
    return outs[:count], outs[count:]


def hand_out_kernel(count, *refs):
    sources, targets, stages = (refs[k * count : (k + 1) * count] for k in range(3))
    inward, outward = refs[3 * count :]
    reads = [
        pltpu.make_async_copy(source, stage, inward.at[number])
        for number, (source, stage) in enumerate(zip(sources, stages))
    ]
    writes = [
        pltpu.make_async_copy(stage, target, outward.at[number])
        for number, (stage, target) in enumerate(zip(stages, targets))
    ]
    for read in reads:
        read.start()
    for read, write in zip(reads, writes):
        read.wait()
        write.start()
    for write in writes:
        write.wait()


def hand_out(values):
    count = len(values)
    anywhere = pl.BlockSpec(memory_space=pl.ANY)
    return pl.pallas_call(
        functools.partial(hand_out_kernel, count),
        out_shape=[jax.ShapeDtypeStruct(value.shape, value.dtype) for value in values],
        in_specs=[anywhere] * count,
        out_specs=[anywhere] * count,
        scratch_shapes=[pltpu.VMEM(value.shape, value.dtype) for value in values]
        + [pltpu.SemaphoreType.DMA((count,)), pltpu.SemaphoreType.DMA((count,))],
        compiler_params=pltpu.CompilerParams(vmem_limit_bytes=63 * 2**20),
    )(*values)


def fast_body(
    text_rows,
    patches,
    row_pair,
    row_region,
    self_qkv,
    self_out,
    cross_query,
    cross_key_value,
    cross_out,
    ffn_up,
    ffn_down,
    norm_gains,
    biases,
    ffn_bias,
    cotangent,
):
    line = lax.axis_size("dp")
    narrow, slim = norm_gains.shape[1], ffn_bias.shape[0]
    shards = (self_qkv, cross_key_value, self_out, cross_query, cross_out, ffn_up, ffn_down)
    pair_row = row_pair.reshape(1, -1)
    weights, kept, pairs = forward_all(
        line,
        shards,
        norm_gains,
        biases,
        ffn_bias[None],
        text_rows,
        patches.reshape(-1, patches.shape[2]),
        pair_row,
        row_region.reshape(1, -1),
    )
    joined = kept[8]
    saved = kept[:8] + kept[9:]
    grads, (text_grad, patch_grad, gains, shifts, hidden) = backward_all(
        line, weights, saved, pairs, cotangent, pair_row, narrow, slim
    )
    results = hand_out((joined, text_grad, patch_grad, gains, shifts, hidden, *grads))
    joined, text_grad, patch_grad, gains, shifts, hidden, *grads = results
    grad_qkv, grad_ckv, grad_sout, grad_cq, grad_cout, grad_up, grad_down = grads
    return (
        joined,
        text_grad,
        patch_grad.reshape(patches.shape),
        grad_qkv,
        grad_sout,
        grad_cq,
        grad_ckv,
        grad_cout,
        grad_up,
        grad_down,
        gains,
        shifts,
        hidden.reshape(-1),
    )


def body(
    text_rows,
    patches,
    row_pair,
    row_region,
    self_qkv,
    self_out,
    cross_query,
    cross_key_value,
    cross_out,
    ffn_up,
    ffn_down,
    norm_gains,
    biases,
    ffn_bias,
    cotangent,
):
    weight_qkv, weight_sout, weight_cq, weight_ckv, weight_cout, gains_all, bias_all = (
        lax.all_gather(self_qkv, ("dp", "fsdp"), axis=0, tiled=True),
        lax.all_gather(self_out, ("dp", "fsdp"), axis=0, tiled=True),
        lax.all_gather(cross_query, ("dp", "fsdp"), axis=0, tiled=True),
        lax.all_gather(cross_key_value, ("dp", "fsdp"), axis=0, tiled=True),
        lax.all_gather(cross_out, ("dp", "fsdp"), axis=0, tiled=True),
        lax.all_gather(norm_gains, ("dp", "fsdp"), axis=1, tiled=True),
        lax.all_gather(biases, ("dp", "fsdp"), axis=1, tiled=True),
    )
    weight_up, weight_down, bias_up_all = (
        lax.all_gather(ffn_up, ("dp", "fsdp"), axis=0, tiled=True),
        lax.all_gather(ffn_down, ("dp", "fsdp"), axis=0, tiled=True),
        lax.all_gather(ffn_bias, ("dp", "fsdp"), axis=0, tiled=True),
    )
    gains = gains_all.astype(jnp.float32)
    bias_rows = bias_all.astype(jnp.float32)
    bias_hidden = bias_up_all.astype(jnp.float32)
    row_count, model_width = text_rows.shape
    owners = lax.axis_size("dp")
    block_rows = row_count // owners
    valid = (row_pair >= 0)[:, None]
    patch_rows = patches.reshape(-1, patches.shape[2])
    kv_projected = jnp.dot(patch_rows, weight_ckv, preferred_element_type=jnp.float32)
    key_local = kv_projected[:, :model_width].astype(jnp.bfloat16)
    value_local = (kv_projected[:, model_width:] + bias_rows[4]).astype(jnp.bfloat16)
    keys_count = key_local.shape[0]
    kept_self, context_self = self_forward(
        text_rows, row_pair, weight_qkv, bias_rows[0], bias_rows[1]
    )
    branch_self = (
        jnp.dot(context_self, weight_sout, preferred_element_type=jnp.float32) + bias_rows[2]
    )
    first, normed_one, inverse_one = norm_forward(
        text_rows.astype(jnp.float32) + branch_self, gains[0], bias_rows[7]
    )
    first_low = first.astype(jnp.bfloat16)
    queries = (
        jnp.dot(first_low, weight_cq, preferred_element_type=jnp.float32) + bias_rows[3]
    ).astype(jnp.bfloat16)
    region_blocks = row_region.reshape(owners, block_rows)
    arrived, arrived_region = (
        lax.all_to_all(
            queries.reshape(owners, block_rows, model_width),
            "dp",
            split_axis=0,
            concat_axis=0,
            tiled=True,
        ),
        lax.all_to_all(region_blocks, "dp", split_axis=0, concat_axis=0, tiled=True),
    )
    arrived = arrived.reshape(1, owners * block_rows, H, HD)
    arrived_region = arrived_region.reshape(1, owners * block_rows)
    key_view = key_local.reshape(1, keys_count, H, HD)
    value_view = value_local.reshape(1, keys_count, H, HD)
    logsum_cross, context_owner = cross_forward(arrived, key_view, value_view, arrived_region)
    context_cross = lax.all_to_all(
        context_owner.reshape(owners, block_rows, model_width),
        "dp",
        split_axis=0,
        concat_axis=0,
        tiled=True,
    ).reshape(row_count, model_width)
    branch_cross = (
        jnp.dot(context_cross, weight_cout, preferred_element_type=jnp.float32) + bias_rows[5]
    )
    second, normed_two, inverse_two = norm_forward(first + branch_cross, gains[1], bias_rows[8])
    second_low = second.astype(jnp.bfloat16)
    hidden_pre = jnp.dot(second_low, weight_up, preferred_element_type=jnp.float32) + bias_hidden
    hidden_low = gelu_exact(hidden_pre).astype(jnp.bfloat16)
    branch_ffn = jnp.dot(hidden_low, weight_down, preferred_element_type=jnp.float32) + bias_rows[6]
    result, normed_three, inverse_three = norm_forward(second + branch_ffn, gains[2], bias_rows[9])
    joined_text = jnp.where(valid, result, 0.0).astype(jnp.bfloat16)
    upstream = jnp.where(valid, cotangent.astype(jnp.float32), 0.0)
    grad_three, grad_gain_three, grad_shift_three = norm_backward(
        upstream, normed_three, inverse_three, gains[2]
    )
    grad_ffn = grad_three.astype(jnp.bfloat16)
    grad_hidden = times_transpose(grad_ffn, weight_down)
    grad_pre = jax.vjp(gelu_exact, hidden_pre)[1](grad_hidden)[0].astype(jnp.bfloat16)
    ffn_terms = (
        transpose_times(second_low, grad_pre),
        transpose_times(hidden_low, grad_ffn),
        jnp.sum(grad_pre, axis=0, dtype=jnp.float32),
    )
    grad_up, grad_down, grad_up_bias = (
        lax.psum_scatter(ffn_terms[0], ("dp", "fsdp"), scatter_dimension=0, tiled=True),
        lax.psum_scatter(ffn_terms[1], ("dp", "fsdp"), scatter_dimension=0, tiled=True),
        lax.psum_scatter(ffn_terms[2], ("dp", "fsdp"), scatter_dimension=0, tiled=True),
    )
    grad_second = grad_three + times_transpose(grad_pre, weight_up)
    grad_two, grad_gain_two, grad_shift_two = norm_backward(
        grad_second, normed_two, inverse_two, gains[1]
    )
    grad_cross = grad_two.astype(jnp.bfloat16)
    grad_context = times_transpose(grad_cross, weight_cout).astype(jnp.bfloat16)
    grad_arrived = lax.all_to_all(
        grad_context.reshape(owners, block_rows, model_width),
        "dp",
        split_axis=0,
        concat_axis=0,
        tiled=True,
    ).reshape(1, owners * block_rows, H, HD)
    grad_query_owner, grad_key, grad_value = cross_backward(
        arrived, key_view, value_view, arrived_region, logsum_cross, grad_arrived
    )
    grad_queries = lax.all_to_all(
        grad_query_owner.astype(jnp.bfloat16).reshape(owners, block_rows, model_width),
        "dp",
        split_axis=0,
        concat_axis=0,
        tiled=True,
    ).reshape(row_count, model_width)
    grad_key_total = grad_key.reshape(keys_count, model_width)
    grad_value_total = grad_value.reshape(keys_count, model_width)
    grad_kv = jnp.concatenate(
        [grad_key_total.astype(jnp.bfloat16), grad_value_total.astype(jnp.bfloat16)], axis=1
    )
    patch_grad = times_transpose(grad_kv, weight_ckv).reshape(patches.shape)
    grad_ckv = transpose_times(patch_rows, grad_kv)
    grad_cross_value_bias = jnp.sum(grad_kv[:, model_width:], axis=0, dtype=jnp.float32)
    grad_first = grad_two + times_transpose(grad_queries, weight_cq)
    grad_cq = transpose_times(first_low, grad_queries)
    grad_cout = transpose_times(context_cross, grad_cross)
    grad_one, grad_gain_one, grad_shift_one = norm_backward(
        grad_first, normed_one, inverse_one, gains[0]
    )
    grad_self = grad_one.astype(jnp.bfloat16)
    grad_sout = transpose_times(context_self, grad_self)
    grad_context_self = times_transpose(grad_self, weight_sout).astype(jnp.bfloat16)
    grad_projected = self_backward(kept_self, grad_context_self)
    grad_qkv = transpose_times(text_rows, grad_projected)
    text_grad = grad_one + times_transpose(grad_projected, weight_qkv)
    gain_terms = jnp.stack([grad_gain_one, grad_gain_two, grad_gain_three])
    bias_terms = jnp.stack(
        [
            jnp.sum(grad_projected[:, :model_width], axis=0, dtype=jnp.float32),
            jnp.sum(grad_projected[:, 2 * model_width :], axis=0, dtype=jnp.float32),
            jnp.sum(grad_self, axis=0, dtype=jnp.float32),
            jnp.sum(grad_queries, axis=0, dtype=jnp.float32),
            grad_cross_value_bias,
            jnp.sum(grad_cross, axis=0, dtype=jnp.float32),
            jnp.sum(grad_ffn, axis=0, dtype=jnp.float32),
            grad_shift_one,
            grad_shift_two,
            grad_shift_three,
        ]
    )
    attn_terms = (grad_qkv, grad_sout, grad_cq, grad_ckv, grad_cout, gain_terms, bias_terms)
    shard_qkv, shard_sout, shard_cq, shard_ckv, shard_cout, shard_gains, shard_biases = (
        lax.psum_scatter(attn_terms[0], ("dp", "fsdp"), scatter_dimension=0, tiled=True),
        lax.psum_scatter(attn_terms[1], ("dp", "fsdp"), scatter_dimension=0, tiled=True),
        lax.psum_scatter(attn_terms[2], ("dp", "fsdp"), scatter_dimension=0, tiled=True),
        lax.psum_scatter(attn_terms[3], ("dp", "fsdp"), scatter_dimension=0, tiled=True),
        lax.psum_scatter(attn_terms[4], ("dp", "fsdp"), scatter_dimension=0, tiled=True),
        lax.psum_scatter(attn_terms[5], ("dp", "fsdp"), scatter_dimension=1, tiled=True),
        lax.psum_scatter(attn_terms[6], ("dp", "fsdp"), scatter_dimension=1, tiled=True),
    )
    return (
        joined_text,
        text_grad,
        patch_grad,
        shard_qkv,
        shard_sout,
        shard_cq,
        shard_ckv,
        shard_cout,
        grad_up,
        grad_down,
        shard_gains,
        shard_biases,
        grad_up_bias,
    )


def solution(mesh):
    in_specs = (
        P(("dp", "fsdp"), None),
        P(("dp", "fsdp"), None, None),
        P(("dp", "fsdp")),
        P(("dp", "fsdp")),
        P(("dp", "fsdp"), None),
        P(("dp", "fsdp"), None),
        P(("dp", "fsdp"), None),
        P(("dp", "fsdp"), None),
        P(("dp", "fsdp"), None),
        P(("dp", "fsdp"), None),
        P(("dp", "fsdp"), None),
        P(None, ("dp", "fsdp")),
        P(None, ("dp", "fsdp")),
        P(("dp", "fsdp")),
        P(("dp", "fsdp"), None),
    )
    out_specs = (
        P(("dp", "fsdp"), None),
        P(("dp", "fsdp"), None),
        P(("dp", "fsdp"), None, None),
        P(("dp", "fsdp"), None),
        P(("dp", "fsdp"), None),
        P(("dp", "fsdp"), None),
        P(("dp", "fsdp"), None),
        P(("dp", "fsdp"), None),
        P(("dp", "fsdp"), None),
        P(("dp", "fsdp"), None),
        P(None, ("dp", "fsdp")),
        P(None, ("dp", "fsdp")),
        P(("dp", "fsdp")),
    )
    fast = mesh.shape["fsdp"] == 8
    chosen = fast_body if fast else body
    return jax.shard_map(chosen, mesh=mesh, in_specs=in_specs, out_specs=out_specs, check_vma=False)
```
